256 devices in a mesh: seq: 32 (over z, x), batch: 8 (over y, core).
Axes of the slice: x: 4, y: 4, z: 8, core: 2. Of those that a mesh axis runs over, the one named last changes fastest.
Arguments:
- inputs: bfloat16 [16, 2048, 256], P('batch', 'seq'), may hold values from -6 to 6
- w_in: bfloat16 [256, 192], replicated, may hold values from -0.375 to 0.375
- u_rec: float32 [64, 192], replicated, may hold values from -0.375 to 0.375
- timescale: float32 [64], replicated, may hold values from 4 to 16384
- other_bias: float32 [3, 64], replicated, may hold values from -3 to 3
- h_init: float32 [64, 16], P(None, 'batch'), may hold values from -6 to 6
- cotangent: float32 [64, 16, 2048], P(None, 'batch', 'seq'), may hold values from -0.0625 to 0.0625
Outputs:
- states: float32 [64, 16, 2048], P(None, 'batch', 'seq')
- grad_in: float32 [256, 192], replicated
- grad_rec: float32 [64, 192], replicated
- grad_timescale: float32 [64], replicated
- grad_other: float32 [3, 64], replicated
The draws below stay inside these ranges and needn't reach their ends.
All inputs are finite; a program needn't handle non-finite values.
Results may differ from the reference program's by a relative error of at most 0.00045.
Values sent between devices are 32-bit elements; how exact they have to be, the bound alone decides.
No kernel may reach another device: no remote copies, remote signals or barrier semaphores. Data moves between devices by JAX's collectives and lax.ppermute only.
A program may use at most 128 MiB of HBM per device.

```python
import math
import jax
import jax.numpy as jnp
from jax import lax

H = 64
X = 256
NEWTON = 3
SEQLEN = 2048
BATCH = 16


def draw_timescale(key, part):
    key = jax.random.fold_in(key, 11)
    first, second, third, fourth = jax.random.split(key, 4)
    share = 0.5
    slow = jax.random.bernoulli(first, share, (H,))
    level = jax.random.uniform(second, (H,), jnp.float32)
    logs = jnp.where(slow, math.log(SEQLEN) + level * math.log(8.0), math.log(4.0) + level * math.log(12.0))
    taus = jnp.clip(jnp.exp(logs), 4.0, 8.0 * SEQLEN)
    lowest = jax.random.randint(third, (), 0, H)
    highest = (lowest + 1 + jax.random.randint(fourth, (), 0, H - 1)) % H
    places = jnp.arange(H)
    taus = jnp.where(places == lowest, 4.0, taus)
    taus = jnp.where(places == highest, 8.0 * SEQLEN, taus)
    return taus.astype(jnp.float32)


def block_scale(rng, dims, shards, smallest, high):
    def one(position, shards_of):
        heights = jax.random.uniform(jax.random.fold_in(jax.random.fold_in(rng, 6), position), (shards_of,), jnp.float32, smallest / len(shards), high / len(shards))
        return jnp.repeat(jnp.exp(heights), dims[position] // shards_of).reshape((-1,) + (1,) * (len(dims) - position - 1))

    factor_of = one(*shards[0])
    for cut in shards[1:]:
        factor_of = factor_of * one(*cut)
    return factor_of


def centred(own_key, extent, scale, most, cuts=(), kind=jnp.bfloat16):
    array = jax.random.normal(own_key, extent, jnp.float32) * scale
    if len(cuts) > 0:
        array = block_scale(own_key, extent, cuts, -0.22, 0.18) * array
    return jnp.clip(array, min=-most, max=most).astype(kind)


def setup_inputs(seed: int = 0) -> dict:
    streams_of = jax.random.split(jax.random.key(seed), 8)
    return {
        "inputs": centred(streams_of[0], (BATCH, SEQLEN, X), 1.0, 6.0, ((0, 8), (1, 32))),
        "w_in": centred(streams_of[1], (X, 3 * H), X ** -0.5, 0.375),
        "u_rec": centred(streams_of[2], (H, 3 * H), (0.5 / H ** 0.5), 0.375, (), jnp.float32),
        "timescale": draw_timescale(jax.random.fold_in(streams_of[7], 71), 0),
        "other_bias": centred(streams_of[4], (3, H), 0.5, 3.0, (), jnp.float32),
        "h_init": centred(streams_of[5], (H, BATCH), 1.0, 6.0, ((1, 8),), jnp.float32),
        "cotangent": centred(streams_of[6], (H, BATCH, SEQLEN), (2.0 / (BATCH * SEQLEN) ** 0.5), 0.0625, ((1, 8), (2, 32)), jnp.float32),
    }


HIGH = lax.Precision.HIGHEST

def cell(prev, xproj, u_rec, timescale, other_bias):
    width = prev.shape[1]
    mixed = jnp.dot(prev, u_rec, precision=HIGH)
    update = jax.nn.sigmoid(xproj[:, :width] + mixed[:, :width] + jnp.log(timescale))
    reset = jax.nn.sigmoid(xproj[:, width:2 * width] + mixed[:, width:2 * width] + other_bias[0])
    recur = mixed[:, 2 * width:] + other_bias[2]
    cand = jnp.tanh(xproj[:, 2 * width:] + other_bias[1] + reset * recur)
    return (1.0 - update) * cand + update * prev

def reference(inputs, w_in, u_rec, timescale, other_bias, h_init, cotangent):
    batch, length, feats = inputs.shape
    flat = jnp.dot(inputs.reshape(batch * length, feats), w_in, preferred_element_type=jnp.float32)
    xproj = flat.reshape(batch, length, -1).transpose(1, 0, 2)
    start = h_init.T
    traj = jnp.zeros((length, batch, h_init.shape[0]), jnp.float32)

    def forward(prior):
        prev = jnp.concatenate([start[None], prior[:-1]], axis=0)

        def advance(state, items):
            past, proj = items
            value, linear = jax.jvp(lambda v: cell(v, proj, u_rec, timescale, other_bias), (past,), (state - past,))
            fresh = value + linear
            return (fresh, fresh)
        return lax.scan(advance, start, (prev, xproj))[1]
    for _ in range(NEWTON):
        traj = forward(traj)
    prev = jnp.concatenate([start[None], traj[:-1]], axis=0)
    sources = cotangent.transpose(2, 1, 0)

    def retreat(passed, items):
        past, proj, source = items
        lam = source + passed
        _, pull = jax.vjp(lambda v: cell(v, proj, u_rec, timescale, other_bias), past)
        return (pull(lam)[0], lam)
    lams = lax.scan(retreat, jnp.zeros_like(start), (prev, xproj, sources), reverse=True)[1]
    rows = length * batch
    prev_flat = prev.reshape(rows, -1)
    _, pull = jax.vjp(lambda xq, uq, tq, oq: cell(prev_flat, xq, uq, tq, oq), xproj.reshape(rows, -1), u_rec, timescale, other_bias)
    d_x, d_u, d_t, d_o = pull(lams.reshape(rows, -1))
    x_flat = inputs.transpose(1, 0, 2).reshape(rows, feats).astype(jnp.float32)
    grad_in = jnp.dot(x_flat.T, d_x, precision=HIGH)
    return (traj.transpose(2, 1, 0), grad_in, d_u, d_t, d_o)
```

```python
import functools

import jax
import jax.numpy as jnp
from jax import lax
from jax.experimental import pallas as pl
from jax.experimental.pallas import tpu as pltpu
from jax.sharding import PartitionSpec as P

NEWTON = 3
H = 64
LANES = 128
CHUNKS = 8
STEPS = 8
COLS = H + 1
ROWS = COLS * CHUNKS
BLOCK = 13
MAP = 40
PART = 200
F32 = jnp.float32
BF16 = jnp.bfloat16
VMEM = pltpu.VMEM
SMEM = pltpu.SMEM


def split(value):
    high = value.astype(BF16)
    return high, (value - high.astype(F32)).astype(BF16)


def mm(left, right):
    return jnp.dot(left, right, preferred_element_type=F32)


def mm_nt(left, right):
    return lax.dot_general(left, right, (((1,), (1,)), ((), ())), preferred_element_type=F32)


def mm_tn(left, right):
    return lax.dot_general(left, right, (((0,), (0,)), ((), ())), preferred_element_type=F32)


def left3(value):
    high, low = split(value)
    return jnp.concatenate([high, low, high], axis=1)


def right3(value):
    high, low = split(value)
    return jnp.concatenate([high, high, low], axis=0)


def lane_low(shape):
    return lax.broadcasted_iota(jnp.int32, shape, 1) < H


def swap_halves(value):
    return jnp.concatenate([value[:, H:], value[:, :H]], axis=1)


def doubled(value, half):
    low = lane_low(value.shape)
    other = swap_halves(value)
    return jnp.where(low, value, other) if half == 0 else jnp.where(low, other, value)


def right_doubled(matrix):
    high, low = split(matrix)
    return jnp.concatenate([high, low, high, low], axis=0)


def left_doubled(value):
    high, low = split(value)
    return jnp.concatenate([high, low], axis=1)


def block_diagonal(matrix):
    low = lane_low(matrix.shape)
    return jnp.concatenate([jnp.where(low, matrix, 0.0), jnp.where(low, 0.0, matrix)], axis=0)


def weights_kernel(u_ref, scale_ref, other_ref, w3_ref, uth_ref, utl_ref, ud_ref, bias_ref):
    zero = jnp.zeros((H, H), F32)
    for g in range(3):
        block = u_ref[:, g * H : (g + 1) * H]
        ud_ref[g] = jnp.concatenate([block, block], axis=1)
        diag = jnp.concatenate(
            [jnp.concatenate([block, zero], axis=1), jnp.concatenate([zero, block], axis=1)], axis=0
        )
        at = slice(g * LANES, (g + 1) * LANES)
        high, low = split(diag)
        w3_ref[0:LANES, at] = high
        w3_ref[LANES : 2 * LANES, at] = high
        w3_ref[2 * LANES : 3 * LANES, at] = low
        high, low = split(diag.T)
        uth_ref[at, :] = high
        utl_ref[at, :] = low
    rows = [jnp.log(scale_ref[...]), other_ref[0:1, :], other_ref[1:2, :], other_ref[2:3, :]]
    rows = [jnp.concatenate([row, row], axis=1) for row in rows]
    bias_ref[...] = jnp.concatenate(rows + [jnp.zeros((4, LANES), F32)], axis=0)


def pack_kernel(where_ref, x_ref, cot_ref, h_ref, out_ref):
    odd = where_ref[0]
    zero = jnp.zeros((H, H), F32)
    for m in range(2):
        first = odd == m
        x = jnp.where(first, x_ref[0].astype(F32), x_ref[1].astype(F32))
        out_ref[m, 0:64, :] = x[:, :LANES]
        out_ref[m, 64:128, :] = x[:, LANES:]
        cot = jnp.where(first, cot_ref[0], cot_ref[1])
        low = jnp.concatenate([cot, zero], axis=1)
        high = jnp.concatenate([zero, cot], axis=1)
        out_ref[m, 128:192, :] = jnp.where(odd == 0, low, high)
        start = jnp.where(first, h_ref[0:1, :], h_ref[1:2, :])
        start = jnp.concatenate([start, start], axis=1)
        out_ref[m, 192:200, :] = jnp.broadcast_to(start, (8, LANES))


def coefficients(prev, x3, bias, w3):
    mixed = mm(left3(prev), w3)
    mz, mr, mn = mixed[:, :LANES], mixed[:, LANES : 2 * LANES], mixed[:, 2 * LANES :]
    update = jax.nn.sigmoid(x3[0] + mz)
    reset = jax.nn.sigmoid(x3[1] + mr)
    recur = mn + bias[3:4, :]
    cand = jnp.tanh(x3[2] + reset * recur)
    fresh = (1.0 - update) * cand + update * prev
    slope = (1.0 - update) * (1.0 - cand * cand)
    cz = (prev - cand) * update * (1.0 - update)
    cr = slope * recur * reset * (1.0 - reset)
    cn = slope * reset
    offset = fresh - (update * prev + cz * mz + cr * mr + cn * mn)
    return update, cz, cr, cn, slope, offset


def scan_maps(coef, w3_ref, ud_ref, maps_ref):
    update, cz, cr, cn, _, offset = coef
    shape = (BLOCK, CHUNKS, LANES)
    for j in range(STEPS):
        at = slice(j * CHUNKS, (j + 1) * CHUNKS)
        up_j, cz_j, cr_j, cn_j = (a[at][None] for a in (update, cz, cr, cn))
        for b in range(COLS // BLOCK):
            rows = slice(b * BLOCK * CHUNKS, (b + 1) * BLOCK * CHUNKS)
            last = b == COLS // BLOCK - 1
            if j == 0:
                real = BLOCK - 1 if last else BLOCK
                cols = slice(b * BLOCK, b * BLOCK + real)
                k = lax.broadcasted_iota(jnp.int32, (real, CHUNKS, LANES), 0) + b * BLOCK
                lane = lax.broadcasted_iota(jnp.int32, (real, CHUNKS, LANES), 2) % H
                new = jnp.where(k == lane, up_j, 0.0)
                for c, g in ((cz_j, 0), (cr_j, 1), (cn_j, 2)):
                    new = new + c * ud_ref[g, cols, :][:, None, :]
                if last:
                    new = jnp.concatenate([new, offset[at][None]], axis=0)
            else:
                old = maps_ref[j - 1, rows, :]
                prod = mm(left3(old), w3_ref[...]).reshape(BLOCK, CHUNKS, 3 * LANES)
                new = (
                    up_j * old.reshape(shape)
                    + cz_j * prod[..., :LANES]
                    + cr_j * prod[..., LANES : 2 * LANES]
                    + cn_j * prod[..., 2 * LANES :]
                )
                if last:
                    new = jnp.concatenate([new[: BLOCK - 1], new[BLOCK - 1 :] + offset[at][None]], axis=0)
            maps_ref[j, rows, :] = new.reshape(BLOCK * CHUNKS, LANES)


def chunk_matrix(maps_ref, c):
    return maps_ref[STEPS - 1, pl.ds(c, H, stride=CHUNKS), :]


def chain_chunks(maps_ref, prefix_ref):
    row = lax.broadcasted_iota(jnp.int32, (72, LANES), 0)
    total = None
    for c in range(CHUNKS):
        matrix = chunk_matrix(maps_ref, c)
        vector = maps_ref[STEPS - 1, H * CHUNKS + c : H * CHUNKS + c + 1, :]
        if c == 0:
            total = jnp.concatenate([matrix, vector, jnp.zeros((7, LANES), F32)], axis=0)
        else:
            total = mm(left3(total), right3(block_diagonal(matrix)))
            total = total + jnp.where(row == H, vector, 0.0)
        prefix_ref[c] = total
    return total


def join_halves(total):
    row = lax.broadcasted_iota(jnp.int32, (72, LANES), 0)
    second = doubled(total, 1)
    both = mm(left_doubled(doubled(total, 0)), right_doubled(second[:H]))
    return both + jnp.where(row == H, second, 0.0)


def send_map(total, out_ref):
    low = lane_low((H // 2, LANES))
    packed = jnp.where(low, total[: H // 2], total[H // 2 : H])
    for z in range(out_ref.shape[0]):
        out_ref[z, : H // 2, :] = packed
        out_ref[z, H // 2 :, :] = total[H:]


def unpack_map(packed):
    body = packed[: H // 2]
    other = swap_halves(body)
    low = lane_low(body.shape)
    matrix = jnp.concatenate([jnp.where(low, body, other), jnp.where(low, other, body)], axis=0)
    return matrix, packed[H // 2 : H // 2 + 1]


def apply_row(state, matrix, vector):
    return mm(left_doubled(state), right_doubled(matrix)) + vector


def enter_device(where_ref, own_ref, other_ref, start, reverse):
    core, mine = where_ref[1], where_ref[2]
    planes = own_ref.shape[0]
    state = start
    order = list(range(2 * planes))
    for n in reversed(order) if reverse else order:
        z, kappa = n // 2, n % 2
        packed = jnp.where(core == kappa, own_ref[z], other_ref[z])
        fresh = apply_row(state, *unpack_map(packed))
        reached = (mine < n) if reverse else (mine > n)
        state = jnp.where(reached, fresh, state)
    return state


def spread(rows, count):
    k = lax.broadcasted_iota(jnp.int32, (count,) + rows.shape, 0)
    lane = lax.broadcasted_iota(jnp.int32, (count,) + rows.shape, 2) % H
    picked = jnp.where(k == lane, rows[None], 0.0).reshape(count * rows.shape[0], LANES)
    one = (
        lax.broadcasted_iota(jnp.int32, (LANES, LANES), 0) // H
        == lax.broadcasted_iota(jnp.int32, (LANES, LANES), 1) // H
    )
    one = jnp.where(one, 1.0, 0.0).astype(BF16)
    high, low = split(picked)
    rest = (picked - high.astype(F32) - low.astype(F32)).astype(BF16)
    return mm(jnp.concatenate([high, low, rest], axis=1), jnp.concatenate([one, one, one], axis=0))


def enter_chunks(state, prefix_ref):
    low = lane_low((CHUNKS, LANES))
    ends = prefix_ref[CHUNKS - 1]
    first = doubled(ends, 0)
    middle = apply_row(state, first[:H], first[H : H + 1])
    halves = jnp.where(low, state, middle)
    column = spread(halves[0:1], H)
    row = lax.broadcasted_iota(jnp.int32, (CHUNKS, LANES), 0)
    entering = halves
    for c in range(1, CHUNKS):
        before = prefix_ref[c - 1]
        value = jnp.sum(before[:H] * column, axis=0, keepdims=True) + before[H : H + 1]
        entering = jnp.where(row == c, value, entering)
    return entering


def trajectory(entering, maps_ref, spread_ref):
    spread_ref[...] = spread(entering, H)
    states = [maps_ref[j, H * CHUNKS :, :] for j in range(STEPS)]
    for b in range(0, H * CHUNKS, 64):
        factor = spread_ref[b : b + 64, :].reshape(8, CHUNKS, LANES)
        for j in range(STEPS):
            block = maps_ref[j, b : b + 64, :].reshape(8, CHUNKS, LANES)
            states[j] = states[j] + jnp.sum(block * factor, axis=0)
    return states


def phase(prev, x3_ref, bias_ref, w3_ref, ud_ref, maps_ref, prefix_ref, out_ref):
    coef = coefficients(prev, x3_ref, bias_ref[...], w3_ref[...])
    scan_maps(coef, w3_ref, ud_ref, maps_ref)
    total = chain_chunks(maps_ref, prefix_ref)
    send_map(join_halves(total), out_ref)


def first_kernel(
    where_ref, a_ref, b_ref, w_ref, w3_ref, ud_ref, bias_ref,
    x3_ref, xin_ref, cot_ref, start_ref, maps_ref, prefix_ref, out_ref,
):
    odd, mine = where_ref[0], where_ref[2]
    pieces = []
    for v in range(2):
        for j in range(STEPS):
            rows = [
                jnp.where(odd == v, a_ref[pl.ds(o + j, 8, stride=8), :], b_ref[pl.ds(o + j, 8, stride=8), :])
                for o in (0, 64)
            ]
            pieces.append(jnp.concatenate(rows, axis=1))
    xin = jnp.concatenate(pieces, axis=0).astype(BF16)
    xin_ref[...] = xin
    cot_ref[...] = jnp.concatenate(
        [a_ref[pl.ds(128 + j, 8, stride=8), :] + b_ref[pl.ds(128 + j, 8, stride=8), :] for j in range(STEPS)],
        axis=0,
    )
    start = a_ref[192:200, :]
    start_ref[...] = start
    flat = mm(xin, w_ref[...])
    bias = bias_ref[...]
    for g in range(3):
        cols = slice(g * H, (g + 1) * H)
        x3_ref[g] = jnp.concatenate([flat[:64, cols], flat[64:, cols]], axis=1) + bias[g : g + 1, :]
    row = lax.broadcasted_iota(jnp.int32, (64, LANES), 0)
    lane = lax.broadcasted_iota(jnp.int32, (64, LANES), 1)
    here = (row == 0) & (lane < H) & (mine == 0)
    prev = jnp.where(here, start[0:1, :], 0.0)
    phase(prev, x3_ref, bias_ref, w3_ref, ud_ref, maps_ref, prefix_ref, out_ref)


def next_kernel(
    where_ref, own_ref, other_ref, start_ref, x3_ref, bias_ref, w3_ref, ud_ref, old_ref, before_ref,
    maps_ref, prefix_ref, out_ref, spread_ref,
):
    state = enter_device(where_ref, own_ref, other_ref, start_ref[...], False)
    entering = enter_chunks(state, before_ref)
    states = trajectory(entering, old_ref, spread_ref)
    prev = jnp.concatenate([entering] + states[:-1], axis=0)
    phase(prev, x3_ref, bias_ref, w3_ref, ud_ref, maps_ref, prefix_ref, out_ref)


def half_sums(value):
    row = lax.broadcasted_iota(jnp.int32, (8, LANES), 0)
    low = lane_low((8, LANES))
    pick = jnp.where((row == 0) & low, 1.0, 0.0) + jnp.where((row == 1) & ~low, 1.0, 0.0)
    pick = pick.astype(BF16)
    return mm_nt(jnp.concatenate([pick, pick], axis=1), left_doubled(value))


def turn_kernel(
    where_ref, own_ref, other_ref, start_ref, x3_ref, bias_ref, w3_ref, ud_ref, old_ref, before_ref, cot_ref,
    states_ref, coef_ref, chunk_ref, vector_ref, half_ref, out_ref, spread_ref, maps_ref, prefix_ref, acc_ref,
):
    state = enter_device(where_ref, own_ref, other_ref, start_ref[...], False)
    entering = enter_chunks(state, before_ref)
    states = trajectory(entering, old_ref, spread_ref)
    for j in range(STEPS):
        states_ref[pl.ds(j, CHUNKS, stride=STEPS), :] = states[j]
    prev = jnp.concatenate([entering] + states[:-1], axis=0)
    coef = coefficients(prev, x3_ref, bias_ref[...], w3_ref[...])
    coef_ref[0] = prev
    for n in range(5):
        coef_ref[n + 1] = coef[n]
    scan_maps(coef, w3_ref, ud_ref, maps_ref)
    total = chain_chunks(maps_ref, prefix_ref)
    for b in range(0, H * CHUNKS, 64):
        acc = jnp.zeros((8, CHUNKS, LANES), F32)
        for j in range(STEPS):
            block = maps_ref[j, b : b + 64, :].reshape(8, CHUNKS, LANES)
            acc = acc + block * cot_ref[j * CHUNKS : (j + 1) * CHUNKS, :][None]
        acc_ref[b : b + 64, :] = acc.reshape(64, LANES)
    vectors = []
    for c in range(CHUNKS):
        chunk_ref[c] = chunk_matrix(maps_ref, c)
        sums = half_sums(acc_ref[pl.ds(c, H, stride=CHUNKS), :])
        vectors.append(jnp.concatenate([sums[0:1], sums[1:2]], axis=1))
    vector_ref[...] = jnp.concatenate(vectors, axis=0)
    whole = jnp.zeros((H, LANES), F32)
    for c in range(1, CHUNKS):
        whole = whole + prefix_ref[c - 1][:H] * vectors[c]
    sums = half_sums(whole)
    ends = jnp.concatenate([sums[0:1], sums[1:2]], axis=1) + vectors[0]
    tail = doubled(ends, 1)
    low = lane_low((H, LANES))
    sums = half_sums(jnp.where(low, total[:H], 0.0) * tail)
    left = ends[:, :H] + sums[0:1]
    both = join_halves(total)
    square = jnp.transpose(both[:H])[:H]
    flipped = jnp.concatenate([square, square], axis=1)
    pad = jnp.zeros((7, LANES), F32)
    send_map(jnp.concatenate([flipped, jnp.concatenate([left, left], axis=1), pad], axis=0), out_ref)
    later = jnp.transpose(total[:H])[H:]
    half_ref[...] = jnp.concatenate([jnp.concatenate([later, later], axis=1), tail, pad], axis=0)


def gradient_kernel(
    where_ref, own_ref, other_ref, coef_ref, chunk_ref, vector_ref, half_ref, cot_ref, uth_ref, utl_ref,
    xin_ref, bias_ref, scale_ref, out_ref,
):
    low = lane_low((CHUNKS, LANES))
    row = lax.broadcasted_iota(jnp.int32, (CHUNKS, LANES), 0)
    right = enter_device(where_ref, own_ref, other_ref, jnp.zeros((CHUNKS, LANES), F32), True)
    half = half_ref[...]
    middle = apply_row(right, half[:H], half[H : H + 1])
    value = jnp.where(low, middle, right)
    passed = value
    for c in reversed(range(1, CHUNKS)):
        high, low_part = split(block_diagonal(chunk_ref[c]))
        value = mm_nt(left3(value), jnp.concatenate([high, high, low_part], axis=1)) + vector_ref[c : c + 1, :]
        passed = jnp.where(row < c, value, passed)
    dz, dr, dn, ds = [None] * STEPS, [None] * STEPS, [None] * STEPS, [None] * STEPS
    for j in reversed(range(STEPS)):
        at = slice(j * CHUNKS, (j + 1) * CHUNKS)
        lam = cot_ref[at, :] + passed
        dz[j], dr[j], dn[j] = coef_ref[2, at, :] * lam, coef_ref[3, at, :] * lam, coef_ref[4, at, :] * lam
        ds[j] = coef_ref[5, at, :] * lam
        if j > 0:
            high, low_part = split(jnp.concatenate([dz[j], dr[j], dn[j]], axis=1))
            both = mm(jnp.concatenate([high, low_part], axis=0), uth_ref[...])
            pulled = both[:CHUNKS] + both[CHUNKS:] + mm(high, utl_ref[...])
            passed = coef_ref[1, at, :] * lam + pulled
    dz, dr, dn, ds = (jnp.concatenate(part, axis=0) for part in (dz, dr, dn, ds))

    def stacked(value):
        return jnp.concatenate([value[:, :H], value[:, H:]], axis=0)

    sz, sr, sn, ss = (stacked(part) for part in (dz, dr, dn, ds))
    zero = jnp.zeros((2 * 64, H), F32)
    high, low_part = split(jnp.concatenate([sz, sr, ss, zero], axis=1))
    xin = xin_ref[...]
    grad_in = mm_tn(jnp.concatenate([xin, xin], axis=0), jnp.concatenate([high, low_part], axis=0))
    high, low_part = split(jnp.concatenate([sz, sr, sn, zero], axis=1))
    prev_high, prev_low = split(stacked(coef_ref[0]))
    grad_rec = mm_tn(
        jnp.concatenate([prev_high, prev_low, prev_high], axis=0),
        jnp.concatenate([high, high, low_part], axis=0),
    )
    out_ref[0:256, :] = grad_in[:, :LANES]
    rest = grad_in[:, LANES:]
    out_ref[256:384, :] = jnp.concatenate([rest[:128, :H], rest[128:, :H]], axis=1)
    out_ref[384:448, :] = grad_rec[:, :LANES]
    rest = grad_rec[:, LANES:]
    out_ref[448:480, :] = jnp.concatenate([rest[:32, :H], rest[32:, :H]], axis=1)
    sums = [jnp.sum(part, axis=0, keepdims=True) for part in (sz, sr, ss, sn)]
    scale = sums[0] / scale_ref[...]
    tail = jnp.concatenate(
        [jnp.concatenate([scale, sums[1]], axis=1), jnp.concatenate([sums[2], sums[3]], axis=1)], axis=0
    )
    out_ref[480:512, :] = jnp.concatenate([tail, jnp.zeros((30, LANES), F32)], axis=0)


def unpack_kernel(where_ref, own_ref, other_ref, in_ref, rec_ref, scale_ref, bias_ref):
    first = where_ref[1] == 0
    own = own_ref[...].reshape(256, LANES)
    other = other_ref[...].reshape(256, LANES)
    top, bottom = jnp.where(first, own, other), jnp.where(first, other, own)
    in_ref[:, :LANES] = top
    in_ref[0:128, LANES:] = bottom[:128, :H]
    in_ref[128:, LANES:] = bottom[:128, H:]
    rec_ref[:, :LANES] = bottom[128:192]
    rec_ref[0:32, LANES:] = bottom[192:224, :H]
    rec_ref[32:, LANES:] = bottom[192:224, H:]
    scale_ref[...] = bottom[224:225, :H]
    bias_ref[...] = jnp.concatenate([bottom[224:225, H:], bottom[225:226, :H], bottom[225:226, H:]], axis=0)


def call(kernel, outs, kinds, *operands, scratch=()):
    specs = [pl.BlockSpec(memory_space=SMEM if kind == "s" else VMEM) for kind in kinds]
    return pl.pallas_call(
        kernel,
        out_shape=[jax.ShapeDtypeStruct(*out) for out in outs],
        in_specs=specs,
        out_specs=[pl.BlockSpec(memory_space=VMEM)] * len(outs),
        scratch_shapes=list(scratch),
        compiler_params=pltpu.CompilerParams(vmem_limit_bytes=48 * 1024 * 1024),
    )(*operands)


def local(planes, width, ys, inputs, w_in, u_rec, timescale, other_bias, h_init, cotangent):
    place, part = lax.axis_index("seq"), lax.axis_index("batch")
    z, x, core = place // width, place % width, part % 2
    where = jnp.stack([x % 2, core, z * 2 + core]).astype(jnp.int32)

    def at(z, x, y, core):
        return (z * width + x) * (2 * ys) + y * 2 + core

    there, back = [], []
    for m in range(2):
        pairs = [
            (at(z, x, y, c), at(z, 2 * c + ((x % 2) ^ m), y, x // 2))
            for z in range(planes) for x in range(width) for y in range(ys) for c in range(2)
        ]
        there.append(pairs)
        back.append([(b, a) for a, b in pairs])
    along_x = [[z * width + x for x in range(width)] for z in range(planes)]
    along_z = [[z * width + x for z in range(planes)] for x in range(width)]
    along_y = [[y * 2 + c for y in range(ys)] for c in range(2)]
    cores = [(b, b ^ 1) for b in range(2 * ys)]
    axes = ("seq", "batch")

    def exchange(value):
        own = lax.all_to_all(value, "seq", 0, 0, axis_index_groups=along_z, tiled=True)
        return own, lax.ppermute(own, "batch", cores)

    w3, uth, utl, ud, bias = call(
        weights_kernel,
        [((384, 384), BF16), ((384, LANES), BF16), ((384, LANES), BF16), ((3, H, LANES), F32), ((8, LANES), F32)],
        "vvv", u_rec, timescale[None, :], other_bias,
    )
    (packed,) = call(
        pack_kernel, [((2, PART, LANES), F32)], "svvv",
        where, inputs, jnp.transpose(cotangent, (1, 2, 0)), h_init.T,
    )
    one = lax.ppermute(packed[0], axes, there[0])
    two = lax.ppermute(packed[1], axes, there[1])
    maps_t, prefix_t, send_t = ((STEPS, ROWS, LANES), F32), ((CHUNKS, 72, LANES), F32), ((planes, MAP, LANES), F32)
    x3, xin, cot, start, maps, prefix, send = call(
        first_kernel,
        [((3, 64, LANES), F32), ((128, 256), BF16), ((64, LANES), F32), ((8, LANES), F32), maps_t, prefix_t, send_t],
        "svvvvvv", where, one, two, w_in, w3, ud, bias,
    )
    spread_s = pltpu.VMEM((H * CHUNKS, LANES), F32)
    for _ in range(NEWTON - 1):
        own, other = exchange(send)
        maps, prefix, send = call(
            next_kernel, [maps_t, prefix_t, send_t], "svvvvvvvvv",
            where, own, other, start, x3, bias, w3, ud, maps, prefix, scratch=[spread_s],
        )
    own, other = exchange(send)
    states, coef, chunk, vector, half, send = call(
        turn_kernel,
        [((64, LANES), F32), ((6, 64, LANES), F32), ((CHUNKS, H, LANES), F32), ((8, LANES), F32), ((72, LANES), F32), send_t],
        "svvvvvvvvvv", where, own, other, start, x3, bias, w3, ud, maps, prefix, cot,
        scratch=[spread_s, pltpu.VMEM(*maps_t), pltpu.VMEM(*prefix_t), pltpu.VMEM((H * CHUNKS, LANES), F32)],
    )
    own, other = exchange(send)
    (grads,) = call(
        gradient_kernel, [((512, LANES), F32)], "svvvvvvvvvvvv",
        where, own, other, coef, chunk, vector, half, cot, uth, utl, xin, bias, timescale[None, :],
    )
    odd = x % 2
    low, high = states[:, :H], states[:, H:]
    even = odd == 0
    home = [
        lax.ppermute(jnp.where(even == (m == 0), low, high), axes, back[m]) for m in range(2)
    ]
    first, second = jnp.where(even, home[0], home[1]), jnp.where(even, home[1], home[0])
    traj = jnp.transpose(jnp.stack([first, second]), (2, 0, 1))

    halves = grads.reshape(2, 256, LANES)
    mine = jnp.where(core == 0, halves[0], halves[1])
    send = jnp.where(core == 0, halves[1], halves[0])
    part = mine + lax.ppermute(send, "batch", cores)
    part = lax.all_to_all(part.reshape(width, -1, LANES), "seq", 0, 0, axis_index_groups=along_x, tiled=True).sum(0)

    def everyone(value, axis, groups):
        wide = jnp.broadcast_to(value[None], (len(groups[0]),) + value.shape)
        return lax.all_to_all(wide, axis, 0, 0, axis_index_groups=groups, tiled=True)

    part = everyone(part, "batch", along_y).sum(0)
    part = everyone(part, "seq", along_z).sum(0)
    part = everyone(part, "seq", along_x)
    other = lax.ppermute(part, "batch", cores)
    grad_in, grad_rec, grad_scale, grad_other = call(
        unpack_kernel, [((256, 192), F32), ((H, 192), F32), ((1, H), F32), ((3, H), F32)], "svv", where, part, other,
    )
    return traj, grad_in, grad_rec, grad_scale[0], grad_other


def solution(mesh):
    width = 4
    planes = mesh.shape["seq"] // width
    ys = mesh.shape["batch"] // 2
    return jax.shard_map(
        functools.partial(local, planes, width, ys),
        mesh=mesh,
        in_specs=(P("batch", "seq", None), P(), P(), P(), P(), P(None, "batch"), P(None, "batch", "seq")),
        out_specs=(P(None, "batch", "seq"), P(), P(), P(), P()),
        check_vma=False,
    )
```

```python
import functools

import jax
import jax.numpy as jnp
from jax import lax
from jax.experimental import pallas as pl
from jax.experimental.pallas import tpu as pltpu
from jax.sharding import PartitionSpec as P

NEWTON = 3
H = 64
LANES = 128
CHUNKS = 8
STEPS = 8
COLS = H + 1
ROWS = COLS * CHUNKS
BLOCK = 13
MAP = 40
PART = 200
F32 = jnp.float32
BF16 = jnp.bfloat16
VMEM = pltpu.VMEM
SMEM = pltpu.SMEM


def split(value):
    high = value.astype(BF16)
    return high, (value - high.astype(F32)).astype(BF16)


def mm(left, right):
    return jnp.dot(left, right, preferred_element_type=F32)


def mm_nt(left, right):
    return lax.dot_general(left, right, (((1,), (1,)), ((), ())), preferred_element_type=F32)


def mm_tn(left, right):
    return lax.dot_general(left, right, (((0,), (0,)), ((), ())), preferred_element_type=F32)


def left3(value):
    high, low = split(value)
    return jnp.concatenate([high, low, high], axis=1)


def right3(value):
    high, low = split(value)
    return jnp.concatenate([high, high, low], axis=0)


def lane_low(shape):
    return lax.broadcasted_iota(jnp.int32, shape, 1) < H


def swap_halves(value):
    return pltpu.roll(value, H, axis=1)


def doubled(value, half):
    low = lane_low(value.shape)
    other = swap_halves(value)
    return jnp.where(low, value, other) if half == 0 else jnp.where(low, other, value)


def right_doubled(matrix):
    high, low = split(matrix)
    return jnp.concatenate([high, low, high, low], axis=0)


def left_doubled(value):
    high, low = split(value)
    return jnp.concatenate([high, low], axis=1)


def block_diagonal(matrix):
    low = lane_low(matrix.shape)
    return jnp.concatenate([jnp.where(low, matrix, 0.0), jnp.where(low, 0.0, matrix)], axis=0)


def fetch(sources, targets, sems):
    copies = [pltpu.make_async_copy(a, b, sems.at[n]) for n, (a, b) in enumerate(zip(sources, targets))]
    for copy in copies:
        copy.start()
    for copy in copies:
        copy.wait()


def weights_kernel(
    u_hbm, scale_hbm, other_hbm, w_hbm, w3_ref, ws_ref, uth_ref, utl_ref, ud_ref, bias_ref, w_ref,
    u_ref, scale_ref, other_ref, sems,
):
    fetch((u_hbm, scale_hbm, other_hbm, w_hbm), (u_ref, scale_ref, other_ref, w_ref), sems)
    zero = jnp.zeros((H, H), F32)
    for g in range(3):
        block = u_ref[:, g * H : (g + 1) * H]
        ud_ref[g] = jnp.concatenate([block, block], axis=1)
        diag = jnp.concatenate(
            [jnp.concatenate([block, zero], axis=1), jnp.concatenate([zero, block], axis=1)], axis=0
        )
        at = slice(g * LANES, (g + 1) * LANES)
        high, low = split(diag)
        w3_ref[0:LANES, at] = high
        w3_ref[LANES : 2 * LANES, at] = high
        w3_ref[2 * LANES : 3 * LANES, at] = low
        ws_ref[0:LANES, at] = high
        ws_ref[LANES : 2 * LANES, at] = high
        ws_ref[2 * LANES : 3 * LANES, at] = low
        if g == 2:
            ws_ref[0:LANES, 3 * LANES :] = low
            ws_ref[LANES : 2 * LANES, 3 * LANES :] = low
            ws_ref[2 * LANES : 3 * LANES, 3 * LANES :] = low
        high, low = split(diag.T)
        uth_ref[at, :] = high
        utl_ref[at, :] = low
    scale = scale_ref[...]
    rows = [jnp.log(scale), other_ref[0:1, :], other_ref[1:2, :], other_ref[2:3, :], scale]
    rows = [jnp.concatenate([row, row], axis=1) for row in rows]
    bias_ref[...] = jnp.concatenate(rows + [jnp.zeros((3, LANES), F32)], axis=0)


def pack_kernel(where_ref, x_hbm, cot_hbm, h_hbm, one_ref, two_ref, x_ref, cot_ref, h_ref, sems):
    fetch((x_hbm, cot_hbm, h_hbm), (x_ref, cot_ref, h_ref), sems)
    odd = where_ref[0]
    zero = jnp.zeros((H, H), F32)
    cots = []
    for e in range(2):
        cots.append(jnp.transpose(jnp.concatenate([cot_ref[:, e, :], zero], axis=1))[:H])
    for m, out_ref in enumerate((one_ref, two_ref)):
        first = odd == m
        x = jnp.where(first, x_ref[0].astype(F32), x_ref[1].astype(F32))
        out_ref[0:64, :] = x[:, :LANES]
        out_ref[64:128, :] = x[:, LANES:]
        cot = jnp.where(first, cots[0], cots[1])
        low = jnp.concatenate([cot, zero], axis=1)
        high = jnp.concatenate([zero, cot], axis=1)
        out_ref[128:192, :] = jnp.where(odd == 0, low, high)
        start = jnp.where(first, h_ref[0:1, :], h_ref[1:2, :])
        start = jnp.concatenate([start, start], axis=1)
        out_ref[192:200, :] = jnp.broadcast_to(start, (8, LANES))


def coefficients(prev, x3, bias, w3):
    mixed = mm(left3(prev), w3)
    mz, mr, mn = mixed[:, :LANES], mixed[:, LANES : 2 * LANES], mixed[:, 2 * LANES :]
    update = jax.nn.sigmoid(x3[0] + mz)
    reset = jax.nn.sigmoid(x3[1] + mr)
    recur = mn + bias[3:4, :]
    cand = jnp.tanh(x3[2] + reset * recur)
    fresh = (1.0 - update) * cand + update * prev
    slope = (1.0 - update) * (1.0 - cand * cand)
    cz = (prev - cand) * update * (1.0 - update)
    cr = slope * recur * reset * (1.0 - reset)
    cn = slope * reset
    offset = fresh - (update * prev + cz * mz + cr * mr + cn * mn)
    return update, cz, cr, cn, slope, offset


def gate_products(rows, ws_ref):
    high, low = split(rows)
    pair = jnp.concatenate([high, low], axis=1)
    both = mm(jnp.concatenate([pair, high], axis=1), ws_ref[:, : 2 * LANES])
    last = mm(pair, ws_ref[: 2 * LANES, 2 * LANES :])
    return both[:, :LANES], both[:, LANES:], last[:, :LANES] + last[:, LANES:]


def scan_maps(coef, ws_ref, ud_ref, maps_ref):
    update, cz, cr, cn, _, offset = coef
    shape = (BLOCK, CHUNKS, LANES)
    for j in range(STEPS):
        at = slice(j * CHUNKS, (j + 1) * CHUNKS)
        up_j, cz_j, cr_j, cn_j = (a[at][None] for a in (update, cz, cr, cn))
        for b in range(COLS // BLOCK):
            rows = slice(b * BLOCK * CHUNKS, (b + 1) * BLOCK * CHUNKS)
            last = b == COLS // BLOCK - 1
            if j == 0:
                real = BLOCK - 1 if last else BLOCK
                cols = slice(b * BLOCK, b * BLOCK + real)
                k = lax.broadcasted_iota(jnp.int32, (real, CHUNKS, LANES), 0) + b * BLOCK
                lane = lax.broadcasted_iota(jnp.int32, (real, CHUNKS, LANES), 2) % H
                new = jnp.where(k == lane, up_j, 0.0)
                for c, g in ((cz_j, 0), (cr_j, 1), (cn_j, 2)):
                    new = new + c * ud_ref[g, cols, :][:, None, :]
                if last:
                    new = jnp.concatenate([new, offset[at][None]], axis=0)
            else:
                old = maps_ref[j - 1, rows, :]
                mz, mr, mn = (part.reshape(shape) for part in gate_products(old, ws_ref))
                new = up_j * old.reshape(shape) + cz_j * mz + cr_j * mr + cn_j * mn
                if last:
                    new = jnp.concatenate([new[: BLOCK - 1], new[BLOCK - 1 :] + offset[at][None]], axis=0)
            maps_ref[j, rows, :] = new.reshape(BLOCK * CHUNKS, LANES)


def chunk_matrix(maps_ref, c):
    return maps_ref[STEPS - 1, pl.ds(c, H, stride=CHUNKS), :]


def chain_chunks(maps_ref, prefix_ref):
    row = lax.broadcasted_iota(jnp.int32, (72, LANES), 0)
    total = None
    for c in range(CHUNKS):
        matrix = chunk_matrix(maps_ref, c)
        vector = maps_ref[STEPS - 1, H * CHUNKS + c : H * CHUNKS + c + 1, :]
        if c == 0:
            total = jnp.concatenate([matrix, vector, jnp.zeros((7, LANES), F32)], axis=0)
        else:
            total = mm(left3(total), right3(block_diagonal(matrix)))
            total = total + jnp.where(row == H, vector, 0.0)
        prefix_ref[c] = total
    return total


def join_halves(total):
    row = lax.broadcasted_iota(jnp.int32, (72, LANES), 0)
    second = doubled(total, 1)
    both = mm(left_doubled(doubled(total, 0)), right_doubled(second[:H]))
    return both + jnp.where(row == H, second, 0.0)


def send_map(total, flipped, where_ref, out_ref):
    low = lane_low((H // 2, LANES))
    matrix = jnp.where(where_ref[1] == 0, flipped, total[:H])
    packed = jnp.where(low, matrix[: H // 2], matrix[H // 2 :])
    for z in range(out_ref.shape[0]):
        out_ref[z, : H // 2, :] = packed
        out_ref[z, H // 2 :, :] = total[H:]


def flip(matrix):
    square = jnp.transpose(matrix)[:H]
    return jnp.concatenate([square, square], axis=1)


def unpack_map(packed, whole):
    body = packed[: H // 2]
    other = swap_halves(body)
    low = lane_low(body.shape)
    if whole:
        parts = [jnp.where(low, body, other), jnp.where(low, other, body)]
    else:
        parts = [jnp.where(low, body, 0.0), jnp.where(low, other, 0.0)]
    return jnp.concatenate(parts, axis=0), packed[H // 2 : H // 2 + 1]


def apply_row(state, matrix, vector):
    return mm(left_doubled(state), right_doubled(matrix)) + vector


def enter_device(where_ref, own_ref, other_ref, start, reverse):
    core, mine = where_ref[1], where_ref[2]
    planes = own_ref.shape[0]
    row = lax.broadcasted_iota(jnp.int32, (H, LANES), 0)
    lane = lax.broadcasted_iota(jnp.int32, (H, LANES), 1)
    eye = jnp.where(row == lane, 1.0, 0.0)
    eyes = jnp.where(row == lane % H, 1.0, 0.0)
    state = start[0:1]
    order = list(range(2 * planes))
    for n in reversed(order) if reverse else order:
        z, kappa = n // 2, n % 2
        reached = (mine < n) if reverse else (mine > n)
        packed = jnp.where(core == kappa, own_ref[z], other_ref[z])
        to_column = kappa == (1 if reverse else 0)
        matrix, vector = unpack_map(packed, not to_column)
        vector = jnp.where(reached, vector, 0.0)
        if to_column:
            matrix = jnp.where(reached, matrix, eye)
            summed = jnp.sum(matrix * state + eye * vector, axis=1, keepdims=True)
            state = jnp.broadcast_to(summed, (H, LANES))
        else:
            matrix = jnp.where(reached, matrix, eyes)
            state = jnp.sum(matrix * state, axis=0, keepdims=True) + vector
    return jnp.broadcast_to(state, (CHUNKS, LANES))


def spread(rows, count):
    k = lax.broadcasted_iota(jnp.int32, (count,) + rows.shape, 0)
    lane = lax.broadcasted_iota(jnp.int32, (count,) + rows.shape, 2) % H
    picked = jnp.where(k == lane, rows[None], 0.0).reshape(count * rows.shape[0], LANES)
    one = (
        lax.broadcasted_iota(jnp.int32, (LANES, LANES), 0) // H
        == lax.broadcasted_iota(jnp.int32, (LANES, LANES), 1) // H
    )
    one = jnp.where(one, 1.0, 0.0).astype(BF16)
    high, low = split(picked)
    rest = (picked - high.astype(F32) - low.astype(F32)).astype(BF16)
    return mm(jnp.concatenate([high, low, rest], axis=1), jnp.concatenate([one, one, one], axis=0))


def enter_chunks(state, prefix_ref):
    low = lane_low((CHUNKS, LANES))
    ends = prefix_ref[CHUNKS - 1]
    first = doubled(ends, 0)
    middle = apply_row(state, first[:H], first[H : H + 1])
    halves = jnp.where(low, state, middle)
    column = spread(halves[0:1], H)
    row = lax.broadcasted_iota(jnp.int32, (CHUNKS, LANES), 0)
    entering = halves
    for c in range(1, CHUNKS):
        before = prefix_ref[c - 1]
        value = jnp.sum(before[:H] * column, axis=0, keepdims=True) + before[H : H + 1]
        entering = jnp.where(row == c, value, entering)
    return entering


def trajectory(entering, maps_ref, spread_ref):
    spread_ref[...] = spread(entering, H)
    states = [maps_ref[j, H * CHUNKS :, :] for j in range(STEPS)]
    for b in range(0, H * CHUNKS, 64):
        factor = spread_ref[b : b + 64, :].reshape(8, CHUNKS, LANES)
        for j in range(STEPS):
            block = maps_ref[j, b : b + 64, :].reshape(8, CHUNKS, LANES)
            states[j] = states[j] + jnp.sum(block * factor, axis=0)
    return states


def phase(where_ref, prev, x3_ref, bias_ref, w3_ref, ws_ref, ud_ref, maps_ref, prefix_ref, out_ref):
    coef = coefficients(prev, x3_ref, bias_ref[...], w3_ref[...])
    scan_maps(coef, ws_ref, ud_ref, maps_ref)
    total = chain_chunks(maps_ref, prefix_ref)
    total = join_halves(total)
    send_map(total, flip(total[:H]), where_ref, out_ref)


def first_kernel(
    where_ref, a_ref, b_ref, w_ref, w3_ref, ws_ref, ud_ref, bias_ref,
    x3_ref, xin_ref, cot_ref, start_ref, maps_ref, prefix_ref, out_ref,
):
    odd, mine = where_ref[0], where_ref[2]
    pieces = []
    for v in range(2):
        for j in range(STEPS):
            rows = [
                jnp.where(odd == v, a_ref[pl.ds(o + j, 8, stride=8), :], b_ref[pl.ds(o + j, 8, stride=8), :])
                for o in (0, 64)
            ]
            pieces.append(jnp.concatenate(rows, axis=1))
    xin = jnp.concatenate(pieces, axis=0).astype(BF16)
    xin_ref[...] = xin
    cot_ref[...] = jnp.concatenate(
        [a_ref[pl.ds(128 + j, 8, stride=8), :] + b_ref[pl.ds(128 + j, 8, stride=8), :] for j in range(STEPS)],
        axis=0,
    )
    start = a_ref[192:200, :]
    start_ref[...] = start
    flat = mm_nt(xin, w_ref[...])
    bias = bias_ref[...]
    for g in range(3):
        cols = slice(g * H, (g + 1) * H)
        x3_ref[g] = jnp.concatenate([flat[:64, cols], flat[64:, cols]], axis=1) + bias[g : g + 1, :]
    row = lax.broadcasted_iota(jnp.int32, (64, LANES), 0)
    lane = lax.broadcasted_iota(jnp.int32, (64, LANES), 1)
    here = (row == 0) & (lane < H) & (mine == 0)
    prev = jnp.where(here, start[0:1, :], 0.0)
    phase(where_ref, prev, x3_ref, bias_ref, w3_ref, ws_ref, ud_ref, maps_ref, prefix_ref, out_ref)


def next_kernel(
    where_ref, own_ref, other_ref, start_ref, x3_ref, bias_ref, w3_ref, ws_ref, ud_ref, old_ref, before_ref,
    maps_ref, prefix_ref, out_ref, spread_ref,
):
    state = enter_device(where_ref, own_ref, other_ref, start_ref[...], False)
    entering = enter_chunks(state, before_ref)
    states = trajectory(entering, old_ref, spread_ref)
    prev = jnp.concatenate([entering] + states[:-1], axis=0)
    phase(where_ref, prev, x3_ref, bias_ref, w3_ref, ws_ref, ud_ref, maps_ref, prefix_ref, out_ref)


def half_sums(value):
    row = lax.broadcasted_iota(jnp.int32, (8, LANES), 0)
    low = lane_low((8, LANES))
    pick = jnp.where((row == 0) & low, 1.0, 0.0) + jnp.where((row == 1) & ~low, 1.0, 0.0)
    pick = pick.astype(BF16)
    return mm_nt(jnp.concatenate([pick, pick], axis=1), left_doubled(value))


def turn_kernel(
    where_ref, own_ref, other_ref, start_ref, x3_ref, bias_ref, w3_ref, ws_ref, ud_ref, old_ref, before_ref, cot_ref,
    states_ref, coef_ref, chunk_ref, vector_ref, half_ref, out_ref,
    spread_ref, maps_ref, prefix_ref, acc_ref,
):
    state = enter_device(where_ref, own_ref, other_ref, start_ref[...], False)
    entering = enter_chunks(state, before_ref)
    states = trajectory(entering, old_ref, spread_ref)
    for j in range(STEPS):
        states_ref[pl.ds(j, CHUNKS, stride=STEPS), :] = states[j]
    prev = jnp.concatenate([entering] + states[:-1], axis=0)
    coef = coefficients(prev, x3_ref, bias_ref[...], w3_ref[...])
    coef_ref[0] = prev
    for n in range(5):
        coef_ref[n + 1] = coef[n]
    scan_maps(coef, ws_ref, ud_ref, maps_ref)
    total = chain_chunks(maps_ref, prefix_ref)
    for b in range(0, H * CHUNKS, 64):
        acc = jnp.zeros((8, CHUNKS, LANES), F32)
        for j in range(STEPS):
            block = maps_ref[j, b : b + 64, :].reshape(8, CHUNKS, LANES)
            acc = acc + block * cot_ref[j * CHUNKS : (j + 1) * CHUNKS, :][None]
        acc_ref[b : b + 64, :] = acc.reshape(64, LANES)
    vectors = []
    for c in range(CHUNKS):
        chunk_ref[c] = chunk_matrix(maps_ref, c)
        sums = half_sums(acc_ref[pl.ds(c, H, stride=CHUNKS), :])
        vectors.append(jnp.concatenate([sums[0:1], sums[1:2]], axis=1))
    vector_ref[...] = jnp.concatenate(vectors, axis=0)
    whole = jnp.zeros((H, LANES), F32)
    for c in range(1, CHUNKS):
        whole = whole + prefix_ref[c - 1][:H] * vectors[c]
    sums = half_sums(whole)
    ends = jnp.concatenate([sums[0:1], sums[1:2]], axis=1) + vectors[0]
    tail = doubled(ends, 1)
    low = lane_low((H, LANES))
    sums = half_sums(jnp.where(low, total[:H], 0.0) * tail)
    left = ends[:, :H] + sums[0:1]
    both = join_halves(total)
    pad = jnp.zeros((7, LANES), F32)
    left = jnp.concatenate([left, left], axis=1)
    send_map(jnp.concatenate([both[:H], left, pad], axis=0), flip(both[:H]), where_ref, out_ref)
    half_ref[...] = jnp.concatenate([flip(doubled(total[:H], 1)), tail, pad], axis=0)


def gradient_kernel(
    where_ref, own_ref, other_ref, coef_ref, chunk_ref, vector_ref, half_ref, cot_ref, uth_ref, utl_ref,
    xin_ref, bias_ref, states_ref, across_ref, keep_ref, give_ref, home_ref, full_ref,
):
    low = lane_low((CHUNKS, LANES))
    row = lax.broadcasted_iota(jnp.int32, (CHUNKS, LANES), 0)
    right = enter_device(where_ref, own_ref, other_ref, jnp.zeros((CHUNKS, LANES), F32), True)
    half = half_ref[...]
    middle = apply_row(right, half[:H], half[H : H + 1])
    value = jnp.where(low, middle, right)
    passed = value
    for c in reversed(range(1, CHUNKS)):
        high, low_part = split(block_diagonal(chunk_ref[c]))
        value = mm_nt(left3(value), jnp.concatenate([high, high, low_part], axis=1)) + vector_ref[c : c + 1, :]
        passed = jnp.where(row < c, value, passed)
    dz, dr, dn, ds = [None] * STEPS, [None] * STEPS, [None] * STEPS, [None] * STEPS
    for j in reversed(range(STEPS)):
        at = slice(j * CHUNKS, (j + 1) * CHUNKS)
        lam = cot_ref[at, :] + passed
        dz[j], dr[j], dn[j] = coef_ref[2, at, :] * lam, coef_ref[3, at, :] * lam, coef_ref[4, at, :] * lam
        ds[j] = coef_ref[5, at, :] * lam
        if j > 0:
            high, low_part = split(jnp.concatenate([dz[j], dr[j], dn[j]], axis=1))
            both = mm(jnp.concatenate([high, low_part], axis=0), uth_ref[...])
            pulled = both[:CHUNKS] + both[CHUNKS:] + mm(high, utl_ref[...])
            passed = coef_ref[1, at, :] * lam + pulled
    dz, dr, dn, ds = (jnp.concatenate(part, axis=0) for part in (dz, dr, dn, ds))

    def stacked(value):
        return jnp.concatenate([value[:, :H], value[:, H:]], axis=0)

    sz, sr, sn, ss = (stacked(part) for part in (dz, dr, dn, ds))
    zero = jnp.zeros((2 * 64, H), F32)
    high, low_part = split(jnp.concatenate([sz, sr, ss, zero], axis=1))
    xin = xin_ref[...]
    grad_in = mm_tn(jnp.concatenate([high, low_part], axis=0), jnp.concatenate([xin, xin], axis=0))
    high, low_part = split(jnp.concatenate([sz, sr, sn, zero], axis=1))
    prev_high, prev_low = split(stacked(coef_ref[0]))
    grad_rec = mm_tn(
        jnp.concatenate([prev_high, prev_low, prev_high], axis=0),
        jnp.concatenate([high, high, low_part], axis=0),
    )
    full_ref[0:192, :] = grad_in[:192, :LANES]
    full_ref[192:384, :] = grad_in[:192, LANES:]
    full_ref[384:448, :] = grad_rec[:, :LANES]
    rest = grad_rec[:, LANES:]
    full_ref[448:480, :] = jnp.concatenate([rest[:32, :H], rest[32:, :H]], axis=1)
    sums = [jnp.sum(part, axis=0, keepdims=True) for part in (sz, sr, ss, sn)]
    scale = sums[0] / bias_ref[4:5, :H]
    tail = jnp.concatenate(
        [jnp.concatenate([scale, sums[1]], axis=1), jnp.concatenate([sums[2], sums[3]], axis=1)], axis=0
    )
    full_ref[480:512, :] = jnp.concatenate([tail, jnp.zeros((30, LANES), F32)], axis=0)
    core, x = where_ref[1], where_ref[3]
    for d in range(4):
        part = lax.rem(x + d, 4)
        rows = slice(d * 64, (d + 1) * 64)
        keep_ref[rows, :] = full_ref[pl.ds(pl.multiple_of((core * 4 + part) * 64, 64), 64), :]
        give_ref[rows, :] = full_ref[pl.ds(pl.multiple_of(((1 - core) * 4 + part) * 64, 64), 64), :]
    for d in range(4):
        part = lax.rem(x + d, 4)
        whole = jnp.where(part // 2 == core, states_ref[...], across_ref[...])
        block = jnp.where(lax.rem(part, 2) == 0, whole, swap_halves(whole))
        home_ref[d] = jnp.where(lane_low((32, LANES)), block[:32], swap_halves(block[32:]))


def unpack_kernel(
    where_ref, one_ref, two_ref, three_ref, both_ref, home_ref, early0_ref, early1_ref, early2_ref,
    in_ref, rec_ref, scale_ref, bias_ref, traj_ref, full_ref,
):
    core, x = where_ref[1], where_ref[3]
    pieces = (both_ref, one_ref, two_ref, three_ref)
    early = (early0_ref, early1_ref, early2_ref)
    blocks = [home_ref[0]] + [ref[64:96, :] for ref in early]
    for e in range(2):
        where = lax.rem(x + 4 - 2 * core - e, 4)
        block = blocks[0]
        for d in range(1, 4):
            block = jnp.where(where == d, blocks[d], block)
        block = jnp.concatenate([block, swap_halves(block)], axis=0)
        traj_ref[:, e, :] = jnp.transpose(block)[:H]
    for d in range(4):
        part = lax.rem(x + 4 - d, 4)
        for core in range(2):
            full_ref[pl.ds(pl.multiple_of((core * 4 + part) * 64, 64), 64), :] = pieces[d][core]
    in_ref[:, :LANES] = full_ref[0:192, :]
    in_ref[:, LANES:] = full_ref[192:384, :]
    rec_ref[:, :LANES] = full_ref[384:448, :]
    rec_ref[0:32, LANES:] = full_ref[448:480, :H]
    rec_ref[32:, LANES:] = full_ref[448:480, H:]
    one, two = full_ref[480:481, :], full_ref[481:482, :]
    scale_ref[...] = one[:, :H]
    bias_ref[...] = jnp.concatenate([one[:, H:], two[:, :H], two[:, H:]], axis=0)


def call(kernel, outs, kinds, *operands, scratch=()):
    spaces = {"s": SMEM, "v": VMEM, "h": pltpu.HBM}
    specs = [pl.BlockSpec(memory_space=spaces[kind]) for kind in kinds]
    return pl.pallas_call(
        kernel,
        out_shape=[jax.ShapeDtypeStruct(*out) for out in outs],
        in_specs=specs,
        out_specs=[pl.BlockSpec(memory_space=VMEM)] * len(outs),
        scratch_shapes=list(scratch),
        compiler_params=pltpu.CompilerParams(vmem_limit_bytes=16 * 1024 * 1024),
    )(*operands)


def local(planes, width, ys, inputs, w_in, u_rec, timescale, other_bias, h_init, cotangent):
    place, part = lax.axis_index("seq"), lax.axis_index("batch")
    z, x, core = place // width, place % width, part % 2
    where = jnp.stack([x % 2, core, z * 2 + core, x]).astype(jnp.int32)

    def at(z, x, y, core):
        return (z * width + x) * (2 * ys) + y * 2 + core

    there = []
    for m in range(2):
        pairs = [
            (at(z, x, y, c), at(z, 2 * c + ((x % 2) ^ m), y, x // 2))
            for z in range(planes) for x in range(width) for y in range(ys) for c in range(2)
        ]
        there.append(pairs)
    step_x = [
        [(z * width + x, z * width + (x + d) % width) for z in range(planes) for x in range(width)]
        for d in range(1, width)
    ]
    along_z = [[z * width + x for z in range(planes)] for x in range(width)]
    step_y = [[(b, (b + 2 * d) % (2 * ys)) for b in range(2 * ys)] for d in range(1, ys)]
    cores = [(b, b ^ 1) for b in range(2 * ys)]
    axes = ("seq", "batch")

    def exchange(value):
        own = lax.all_to_all(value, "seq", 0, 0, axis_index_groups=along_z, tiled=True)
        return own, lax.ppermute(own, "batch", cores)

    sems = pltpu.SemaphoreType.DMA((4,))
    one, two = call(
        pack_kernel, [((PART, LANES), F32)] * 2, "shhh", where, inputs, cotangent, h_init.T,
        scratch=[
            pltpu.VMEM(inputs.shape, BF16), pltpu.VMEM(cotangent.shape, F32), pltpu.VMEM((2, H), F32), sems
        ],
    )
    one = lax.ppermute(one, axes, there[0])
    two = lax.ppermute(two, axes, there[1])
    w3, ws, uth, utl, ud, bias, w = call(
        weights_kernel,
        [
            ((384, 384), BF16), ((384, 512), BF16), ((384, LANES), BF16), ((384, LANES), BF16),
            ((3, H, LANES), F32), ((8, LANES), F32), ((192, 256), BF16),
        ],
        "hhhh", u_rec, timescale[None, :], other_bias, w_in.T,
        scratch=[pltpu.VMEM((H, 192), F32), pltpu.VMEM((1, H), F32), pltpu.VMEM((3, H), F32), sems],
    )
    maps_t, prefix_t, send_t = ((STEPS, ROWS, LANES), F32), ((CHUNKS, 72, LANES), F32), ((planes, MAP, LANES), F32)
    x3, xin, cot, start, maps, prefix, send = call(
        first_kernel,
        [((3, 64, LANES), F32), ((128, 256), BF16), ((64, LANES), F32), ((8, LANES), F32), maps_t, prefix_t, send_t],
        "svvvvvvv", where, one, two, w, w3, ws, ud, bias,
    )
    spread_s = pltpu.VMEM((H * CHUNKS, LANES), F32)
    for _ in range(NEWTON - 1):
        own, other = exchange(send)
        maps, prefix, send = call(
            next_kernel, [maps_t, prefix_t, send_t], "svvvvvvvvvv",
            where, own, other, start, x3, bias, w3, ws, ud, maps, prefix, scratch=[spread_s],
        )
    own, other = exchange(send)
    states, coef, chunk, vector, half, send = call(
        turn_kernel,
        [
            ((64, LANES), F32), ((6, 64, LANES), F32), ((CHUNKS, H, LANES), F32),
            ((8, LANES), F32), ((72, LANES), F32), send_t,
        ],
        "svvvvvvvvvvv", where, own, other, start, x3, bias, w3, ws, ud, maps, prefix, cot,
        scratch=[
            spread_s, pltpu.VMEM(*maps_t), pltpu.VMEM(*prefix_t),
            pltpu.VMEM((H * CHUNKS, LANES), F32),
        ],
    )
    across = lax.ppermute(states, "batch", cores)
    own, other = exchange(send)
    keep, give, home = call(
        gradient_kernel, [((256, LANES), F32), ((256, LANES), F32), ((4, 32, LANES), F32)], "svvvvvvvvvvvvv",
        where, own, other, coef, chunk, vector, half, cot, uth, utl, xin, bias, states, across,
        scratch=[pltpu.VMEM((512, LANES), F32)],
    )

    def around(values, axis, pairs):
        return [lax.ppermute(value, axis, pair) for value, pair in zip(values, pairs)]

    parts = (keep + lax.ppermute(give, "batch", cores)).reshape(width, -1, LANES)
    early = around([jnp.concatenate([parts[d], home[d]], axis=0) for d in range(1, width)], "seq", step_x)
    part = parts[0] + sum(piece[:64] for piece in early)
    part = part + sum(around([part] * (ys - 1), "batch", step_y))
    wide = jnp.broadcast_to(part[None], (planes,) + part.shape)
    part = lax.all_to_all(wide, "seq", 0, 0, axis_index_groups=along_z, tiled=True).sum(0)
    other = lax.ppermute(part, "batch", cores)
    first = core == 0
    both = jnp.stack([jnp.where(first, part, other), jnp.where(first, other, part)])
    rest = around([both] * (width - 1), "seq", step_x)
    grad_in, grad_rec, grad_scale, grad_other, traj = call(
        unpack_kernel,
        [((192, 256), F32), ((H, 192), F32), ((1, H), F32), ((3, H), F32), ((H, 2, 64), F32)], "svvvvvvvv",
        where, *rest, both, home, *early, scratch=[pltpu.VMEM((512, LANES), F32)],
    )
    return traj, grad_in.T, grad_rec, grad_scale[0], grad_other


def solution(mesh):
    width = 4
    planes = mesh.shape["seq"] // width
    ys = mesh.shape["batch"] // 2
    return jax.shard_map(
        functools.partial(local, planes, width, ys),
        mesh=mesh,
        in_specs=(P("batch", "seq", None), P(), P(), P(), P(), P(None, "batch"), P(None, "batch", "seq")),
        out_specs=(P(None, "batch", "seq"), P(), P(), P(), P()),
        check_vma=False,
    )
```

```python
import functools

import jax
import jax.numpy as jnp
from jax import lax
from jax.experimental import pallas as pl
from jax.experimental.pallas import tpu as pltpu
from jax.sharding import PartitionSpec as P

NEWTON = 3
H = 64
LANES = 128
CHUNKS = 8
STEPS = 8
COLS = H + 1
ROWS = COLS * CHUNKS
BLOCK = 13
MAP = 40
PART = 168
F32 = jnp.float32
BF16 = jnp.bfloat16
VMEM = pltpu.VMEM
SMEM = pltpu.SMEM


def split(value):
    high = value.astype(BF16)
    return high, (value - high.astype(F32)).astype(BF16)


def mm(left, right):
    return jnp.dot(left, right, preferred_element_type=F32)


def mm_nt(left, right):
    return lax.dot_general(left, right, (((1,), (1,)), ((), ())), preferred_element_type=F32)


def mm_tn(left, right):
    return lax.dot_general(left, right, (((0,), (0,)), ((), ())), preferred_element_type=F32)


def left3(value):
    high, low = split(value)
    return jnp.concatenate([high, low, high], axis=1)


def right3(value):
    high, low = split(value)
    return jnp.concatenate([high, high, low], axis=0)


def lane_low(shape):
    return lax.broadcasted_iota(jnp.int32, shape, 1) < H


def swap_halves(value):
    return pltpu.roll(value, H, axis=1)


def doubled(value, half):
    low = lane_low(value.shape)
    other = swap_halves(value)
    return jnp.where(low, value, other) if half == 0 else jnp.where(low, other, value)


def right_doubled(matrix):
    high, low = split(matrix)
    return jnp.concatenate([high, low, high, low], axis=0)


def left_doubled(value):
    high, low = split(value)
    return jnp.concatenate([high, low], axis=1)


def block_diagonal(matrix):
    low = lane_low(matrix.shape)
    return jnp.concatenate([jnp.where(low, matrix, 0.0), jnp.where(low, 0.0, matrix)], axis=0)


def fetch(sources, targets, sems):
    copies = [pltpu.make_async_copy(a, b, sems.at[n]) for n, (a, b) in enumerate(zip(sources, targets))]
    for copy in copies:
        copy.start()
    for copy in copies:
        copy.wait()


def weights_kernel(
    u_hbm, scale_hbm, other_hbm, w_hbm, w3_ref, ws_ref, uth_ref, utl_ref, ud_ref, bias_ref, w_ref,
    u_ref, scale_ref, other_ref, sems,
):
    fetch((u_hbm, scale_hbm, other_hbm, w_hbm), (u_ref, scale_ref, other_ref, w_ref), sems)
    zero = jnp.zeros((H, H), F32)
    for g in range(3):
        block = u_ref[:, g * H : (g + 1) * H]
        ud_ref[g] = jnp.concatenate([block, block], axis=1)
        diag = jnp.concatenate(
            [jnp.concatenate([block, zero], axis=1), jnp.concatenate([zero, block], axis=1)], axis=0
        )
        at = slice(g * LANES, (g + 1) * LANES)
        high, low = split(diag)
        w3_ref[0:LANES, at] = high
        w3_ref[LANES : 2 * LANES, at] = high
        w3_ref[2 * LANES : 3 * LANES, at] = low
        ws_ref[0:LANES, at] = high
        ws_ref[LANES : 2 * LANES, at] = high
        ws_ref[2 * LANES : 3 * LANES, at] = low
        if g == 2:
            ws_ref[0:LANES, 3 * LANES :] = low
            ws_ref[LANES : 2 * LANES, 3 * LANES :] = low
            ws_ref[2 * LANES : 3 * LANES, 3 * LANES :] = low
        high, low = split(diag.T)
        uth_ref[at, :] = high
        utl_ref[at, :] = low
    scale = scale_ref[...]
    rows = [jnp.log(scale), other_ref[0:1, :], other_ref[1:2, :], other_ref[2:3, :], scale]
    rows = [jnp.concatenate([row, row], axis=1) for row in rows]
    bias_ref[...] = jnp.concatenate(rows + [jnp.zeros((3, LANES), F32)], axis=0)


def pack_kernel(where_ref, x_hbm, cot_hbm, h_hbm, one_ref, two_ref, x_ref, cot_ref, h_ref, sems):
    fetch((x_hbm, cot_hbm, h_hbm), (x_ref, cot_ref, h_ref), sems)
    odd = where_ref[0]
    zero = jnp.zeros((H, H), F32)
    cots = []
    for e in range(2):
        cots.append(jnp.transpose(jnp.concatenate([cot_ref[:, e, :], zero], axis=1))[:H])
    for m, out_ref in enumerate((one_ref, two_ref)):
        first = odd == m
        x = jnp.where(first, x_ref[0].astype(F32), x_ref[1].astype(F32))
        out_ref[0:64, :] = x[:, :LANES]
        out_ref[64:128, :] = x[:, LANES:]
        cot = jnp.where(first, cots[0], cots[1])
        out_ref[128:160, :] = jnp.concatenate([cot[:32], cot[32:]], axis=1)
        start = jnp.where(first, h_ref[0:1, :], h_ref[1:2, :])
        start = jnp.concatenate([start, start], axis=1)
        out_ref[160:168, :] = jnp.broadcast_to(start, (8, LANES))


def coefficients(prev, x3, bias, w3):
    mixed = mm(left3(prev), w3)
    mz, mr, mn = mixed[:, :LANES], mixed[:, LANES : 2 * LANES], mixed[:, 2 * LANES :]
    update = jax.nn.sigmoid(x3[0] + mz)
    reset = jax.nn.sigmoid(x3[1] + mr)
    recur = mn + bias[3:4, :]
    cand = jnp.tanh(x3[2] + reset * recur)
    fresh = (1.0 - update) * cand + update * prev
    slope = (1.0 - update) * (1.0 - cand * cand)
    cz = (prev - cand) * update * (1.0 - update)
    cr = slope * recur * reset * (1.0 - reset)
    cn = slope * reset
    offset = fresh - (update * prev + cz * mz + cr * mr + cn * mn)
    return update, cz, cr, cn, slope, offset


def gate_products(rows, ws_ref):
    high, low = split(rows)
    pair = jnp.concatenate([high, low], axis=1)
    both = mm(jnp.concatenate([pair, high], axis=1), ws_ref[:, : 2 * LANES])
    last = mm(pair, ws_ref[: 2 * LANES, 2 * LANES :])
    return both[:, :LANES], both[:, LANES:], last[:, :LANES] + last[:, LANES:]


def scan_maps(coef, ws_ref, ud_ref, maps_ref):
    update, cz, cr, cn, _, offset = coef
    shape = (BLOCK, CHUNKS, LANES)
    for j in range(STEPS):
        at = slice(j * CHUNKS, (j + 1) * CHUNKS)
        up_j, cz_j, cr_j, cn_j = (a[at][None] for a in (update, cz, cr, cn))
        for b in range(COLS // BLOCK):
            rows = slice(b * BLOCK * CHUNKS, (b + 1) * BLOCK * CHUNKS)
            last = b == COLS // BLOCK - 1
            if j == 0:
                real = BLOCK - 1 if last else BLOCK
                cols = slice(b * BLOCK, b * BLOCK + real)
                k = lax.broadcasted_iota(jnp.int32, (real, CHUNKS, LANES), 0) + b * BLOCK
                lane = lax.broadcasted_iota(jnp.int32, (real, CHUNKS, LANES), 2) % H
                new = jnp.where(k == lane, up_j, 0.0)
                for c, g in ((cz_j, 0), (cr_j, 1), (cn_j, 2)):
                    new = new + c * ud_ref[g, cols, :][:, None, :]
                if last:
                    new = jnp.concatenate([new, offset[at][None]], axis=0)
            else:
                old = maps_ref[j - 1, rows, :]
                mz, mr, mn = (part.reshape(shape) for part in gate_products(old, ws_ref))
                new = up_j * old.reshape(shape) + cz_j * mz + cr_j * mr + cn_j * mn
                if last:
                    new = jnp.concatenate([new[: BLOCK - 1], new[BLOCK - 1 :] + offset[at][None]], axis=0)
            maps_ref[j, rows, :] = new.reshape(BLOCK * CHUNKS, LANES)


def chunk_matrix(maps_ref, c):
    return maps_ref[STEPS - 1, pl.ds(c, H, stride=CHUNKS), :]


def chunk_vector(maps_ref, c):
    return maps_ref[STEPS - 1, H * CHUNKS + c : H * CHUNKS + c + 1, :]


def compose(earlier, later):
    row = lax.broadcasted_iota(jnp.int32, (72, LANES), 0)
    both = mm(left3(earlier), right3(block_diagonal(later[:H])))
    return both + jnp.where(row == H, later[H : H + 1], 0.0)


def compose_chunks(maps_ref):
    pad = jnp.zeros((7, LANES), F32)
    parts = [
        jnp.concatenate([chunk_matrix(maps_ref, c), chunk_vector(maps_ref, c), pad], axis=0) for c in range(CHUNKS)
    ]
    while len(parts) > 1:
        parts = [compose(a, b) for a, b in zip(parts[::2], parts[1::2])]
    return parts[0]


def flip_halves(matrix):
    turned = jnp.transpose(matrix)
    return jnp.concatenate([turned[:H], turned[H:]], axis=1)


def diagonal(rows):
    row = lax.broadcasted_iota(jnp.int32, (H, LANES), 0)
    lane = lax.broadcasted_iota(jnp.int32, (H, LANES), 1) % H
    return jnp.where(row == lane, rows, 0.0)


def to_column(row, matrix, vector):
    low = lane_low(matrix.shape)
    prod = matrix * row + diagonal(vector)
    first = jnp.sum(jnp.where(low, prod, 0.0), axis=1, keepdims=True)
    second = jnp.sum(jnp.where(low, 0.0, prod), axis=1, keepdims=True)
    return jnp.where(low, first, second)


def to_row(column, matrix, vector):
    return jnp.sum(column * matrix, axis=0, keepdims=True) + vector


def as_row(column):
    return jnp.sum(diagonal(column), axis=0, keepdims=True)


def join_halves(total):
    row = lax.broadcasted_iota(jnp.int32, (72, LANES), 0)
    second = doubled(total, 1)
    both = mm(left_doubled(doubled(total, 0)), right_doubled(second[:H]))
    return both + jnp.where(row == H, second, 0.0)


def send_map(total, flipped, where_ref, out_ref):
    low = lane_low((H // 2, LANES))
    matrix = jnp.where(where_ref[1] == 0, flipped, total[:H])
    packed = jnp.where(low, matrix[: H // 2], matrix[H // 2 :])
    for z in range(out_ref.shape[0]):
        out_ref[z, : H // 2, :] = packed
        out_ref[z, H // 2 :, :] = total[H:]


def flip(matrix):
    square = jnp.transpose(matrix)[:H]
    return jnp.concatenate([square, square], axis=1)


def unpack_map(packed, whole):
    body = packed[: H // 2]
    other = swap_halves(body)
    low = lane_low(body.shape)
    if whole:
        parts = [jnp.where(low, body, other), jnp.where(low, other, body)]
    else:
        parts = [jnp.where(low, body, 0.0), jnp.where(low, other, 0.0)]
    return jnp.concatenate(parts, axis=0), packed[H // 2 : H // 2 + 1]


def apply_row(state, matrix, vector):
    return mm(left_doubled(state), right_doubled(matrix)) + vector


def enter_device(where_ref, own_ref, other_ref, start, reverse):
    core, mine = where_ref[1], where_ref[2]
    planes = own_ref.shape[0]
    row = lax.broadcasted_iota(jnp.int32, (H, LANES), 0)
    lane = lax.broadcasted_iota(jnp.int32, (H, LANES), 1)
    eye = jnp.where(row == lane, 1.0, 0.0)
    eyes = jnp.where(row == lane % H, 1.0, 0.0)
    state = start[0:1]
    order = list(range(2 * planes))
    for n in reversed(order) if reverse else order:
        z, kappa = n // 2, n % 2
        reached = (mine < n) if reverse else (mine > n)
        packed = jnp.where(core == kappa, own_ref[z], other_ref[z])
        to_column = kappa == (1 if reverse else 0)
        matrix, vector = unpack_map(packed, not to_column)
        vector = jnp.where(reached, vector, 0.0)
        if to_column:
            matrix = jnp.where(reached, matrix, eye)
            summed = jnp.sum(matrix * state + eye * vector, axis=1, keepdims=True)
            state = jnp.broadcast_to(summed, (H, LANES))
        else:
            matrix = jnp.where(reached, matrix, eyes)
            state = jnp.sum(matrix * state, axis=0, keepdims=True) + vector
    return jnp.broadcast_to(state, (CHUNKS, LANES))


def spread(rows, count):
    k = lax.broadcasted_iota(jnp.int32, (count,) + rows.shape, 0)
    lane = lax.broadcasted_iota(jnp.int32, (count,) + rows.shape, 2) % H
    picked = jnp.where(k == lane, rows[None], 0.0).reshape(count * rows.shape[0], LANES)
    one = (
        lax.broadcasted_iota(jnp.int32, (LANES, LANES), 0) // H
        == lax.broadcasted_iota(jnp.int32, (LANES, LANES), 1) // H
    )
    one = jnp.where(one, 1.0, 0.0).astype(BF16)
    high, low = split(picked)
    rest = (picked - high.astype(F32) - low.astype(F32)).astype(BF16)
    return mm(jnp.concatenate([high, low, rest], axis=1), jnp.concatenate([one, one, one], axis=0))


def store_chunks(maps_ref, chunk_ref, flipped):
    for c in range(CHUNKS):
        matrix = chunk_matrix(maps_ref, c)
        chunk_ref[c] = flip_halves(matrix) if c % 2 == flipped else matrix


def enter_chunks(state, maps_ref, chunk_ref, ends_ref):
    low = lane_low((CHUNKS, LANES))
    first = doubled(ends_ref[...], 0)
    middle = apply_row(state, first[:H], first[H : H + 1])
    entering = jnp.where(low, state, middle)
    row = lax.broadcasted_iota(jnp.int32, (CHUNKS, LANES), 0)
    value = entering[0:1]
    for c in range(CHUNKS - 1):
        vector = chunk_vector(maps_ref, c)
        if c % 2 == 0:
            column = to_column(value, chunk_ref[c], vector)
            value = as_row(column)
        else:
            value = to_row(column, chunk_ref[c], vector)
        entering = jnp.where(row == c + 1, value, entering)
    return entering


def trajectory(entering, maps_ref, spread_ref):
    spread_ref[...] = spread(entering, H)
    states = [maps_ref[j, H * CHUNKS :, :] for j in range(STEPS)]
    for b in range(0, H * CHUNKS, 64):
        factor = spread_ref[b : b + 64, :].reshape(8, CHUNKS, LANES)
        for j in range(STEPS):
            block = maps_ref[j, b : b + 64, :].reshape(8, CHUNKS, LANES)
            states[j] = states[j] + jnp.sum(block * factor, axis=0)
    return states


def phase(where_ref, prev, x3_ref, bias_ref, w3_ref, ws_ref, ud_ref, maps_ref, chunk_ref, ends_ref, out_ref):
    coef = coefficients(prev, x3_ref, bias_ref[...], w3_ref[...])
    scan_maps(coef, ws_ref, ud_ref, maps_ref)
    total = compose_chunks(maps_ref)
    store_chunks(maps_ref, chunk_ref, 0)
    ends_ref[...] = total
    total = join_halves(total)
    send_map(total, flip(total[:H]), where_ref, out_ref)


def first_kernel(
    where_ref, a_ref, b_ref, w_ref, w3_ref, ws_ref, ud_ref, bias_ref,
    x3_ref, xin_ref, cot_ref, start_ref, maps_ref, chunk_ref, ends_ref, out_ref, natural_ref,
):
    odd, mine = where_ref[0], where_ref[2]
    pieces = []
    for v in range(2):
        for j in range(STEPS):
            rows = [
                jnp.where(odd == v, a_ref[pl.ds(o + j, 8, stride=8), :], b_ref[pl.ds(o + j, 8, stride=8), :])
                for o in (0, 64)
            ]
            pieces.append(jnp.concatenate(rows, axis=1))
    xin = jnp.concatenate(pieces, axis=0).astype(BF16)
    xin_ref[...] = xin
    cots = [jnp.where(odd == v, a_ref[128:160, :], b_ref[128:160, :]) for v in range(2)]
    low = lane_low((32, LANES))
    natural_ref[0:32, :] = jnp.where(low, cots[0], swap_halves(cots[1]))
    natural_ref[32:64, :] = jnp.where(low, swap_halves(cots[0]), cots[1])
    cot_ref[...] = jnp.concatenate([natural_ref[pl.ds(j, 8, stride=8), :] for j in range(STEPS)], axis=0)
    start = a_ref[160:168, :]
    start_ref[...] = start
    flat = mm_nt(xin, w_ref[...])
    bias = bias_ref[...]
    for g in range(3):
        cols = slice(g * H, (g + 1) * H)
        x3_ref[g] = jnp.concatenate([flat[:64, cols], flat[64:, cols]], axis=1) + bias[g : g + 1, :]
    row = lax.broadcasted_iota(jnp.int32, (64, LANES), 0)
    lane = lax.broadcasted_iota(jnp.int32, (64, LANES), 1)
    here = (row == 0) & (lane < H) & (mine == 0)
    prev = jnp.where(here, start[0:1, :], 0.0)
    phase(where_ref, prev, x3_ref, bias_ref, w3_ref, ws_ref, ud_ref, maps_ref, chunk_ref, ends_ref, out_ref)


def next_kernel(
    where_ref, own_ref, other_ref, start_ref, x3_ref, bias_ref, w3_ref, ws_ref, ud_ref, old_ref, pieces_ref, before_ref,
    maps_ref, chunk_ref, ends_ref, out_ref, spread_ref,
):
    state = enter_device(where_ref, own_ref, other_ref, start_ref[...], False)
    entering = enter_chunks(state, old_ref, pieces_ref, before_ref)
    states = trajectory(entering, old_ref, spread_ref)
    prev = jnp.concatenate([entering] + states[:-1], axis=0)
    phase(where_ref, prev, x3_ref, bias_ref, w3_ref, ws_ref, ud_ref, maps_ref, chunk_ref, ends_ref, out_ref)


def half_sums(value):
    row = lax.broadcasted_iota(jnp.int32, (8, LANES), 0)
    low = lane_low((8, LANES))
    pick = jnp.where((row == 0) & low, 1.0, 0.0) + jnp.where((row == 1) & ~low, 1.0, 0.0)
    pick = pick.astype(BF16)
    return mm_nt(jnp.concatenate([pick, pick], axis=1), left_doubled(value))


def turn_kernel(
    where_ref, own_ref, other_ref, start_ref, x3_ref, bias_ref, w3_ref, ws_ref, ud_ref, old_ref, pieces_ref, before_ref, cot_ref,
    states_ref, coef_ref, chunk_ref, vector_ref, half_ref, out_ref,
    spread_ref, maps_ref, acc_ref,
):
    state = enter_device(where_ref, own_ref, other_ref, start_ref[...], False)
    entering = enter_chunks(state, old_ref, pieces_ref, before_ref)
    states = trajectory(entering, old_ref, spread_ref)
    for j in range(STEPS):
        states_ref[pl.ds(j, CHUNKS, stride=STEPS), :] = states[j]
    prev = jnp.concatenate([entering] + states[:-1], axis=0)
    coef = coefficients(prev, x3_ref, bias_ref[...], w3_ref[...])
    coef_ref[0] = prev
    for n in range(5):
        coef_ref[n + 1] = coef[n]
    scan_maps(coef, ws_ref, ud_ref, maps_ref)
    total = compose_chunks(maps_ref)
    store_chunks(maps_ref, chunk_ref, 0)
    for b in range(0, H * CHUNKS, 64):
        acc = jnp.zeros((8, CHUNKS, LANES), F32)
        for j in range(STEPS):
            block = maps_ref[j, b : b + 64, :].reshape(8, CHUNKS, LANES)
            acc = acc + block * cot_ref[j * CHUNKS : (j + 1) * CHUNKS, :][None]
        acc_ref[b : b + 64, :] = acc.reshape(64, LANES)
    vectors = []
    for c in range(CHUNKS):
        sums = half_sums(acc_ref[pl.ds(c, H, stride=CHUNKS), :])
        vectors.append(jnp.concatenate([sums[0:1], sums[1:2]], axis=1))
    vector_ref[...] = jnp.concatenate(vectors, axis=0)
    ends = jnp.zeros((1, LANES), F32)
    for c in reversed(range(CHUNKS)):
        if c % 2 == 1:
            column = to_column(ends, chunk_ref[c], vectors[c])
        else:
            ends = to_row(column, chunk_ref[c], vectors[c])
    tail = doubled(ends, 1)
    low = lane_low((H, LANES))
    sums = half_sums(jnp.where(low, total[:H], 0.0) * tail)
    left = ends[:, :H] + sums[0:1]
    both = join_halves(total)
    pad = jnp.zeros((7, LANES), F32)
    left = jnp.concatenate([left, left], axis=1)
    send_map(jnp.concatenate([both[:H], left, pad], axis=0), flip(both[:H]), where_ref, out_ref)
    half_ref[...] = jnp.concatenate([flip(doubled(total[:H], 1)), tail, pad], axis=0)


def gradient_kernel(
    where_ref, own_ref, other_ref, coef_ref, chunk_ref, vector_ref, half_ref, cot_ref, uth_ref, utl_ref,
    xin_ref, bias_ref, states_ref, across_ref, keep_ref, give_ref, home_ref, full_ref,
):
    low = lane_low((CHUNKS, LANES))
    row = lax.broadcasted_iota(jnp.int32, (CHUNKS, LANES), 0)
    right = enter_device(where_ref, own_ref, other_ref, jnp.zeros((CHUNKS, LANES), F32), True)
    half = half_ref[...]
    middle = apply_row(right, half[:H], half[H : H + 1])
    passed = jnp.where(low, middle, right)
    value = passed[0:1]
    for c in reversed(range(1, CHUNKS)):
        vector = vector_ref[c : c + 1, :]
        if c % 2 == 1:
            column = to_column(value, chunk_ref[c], vector)
            value = as_row(column)
        else:
            value = to_row(column, chunk_ref[c], vector)
        passed = jnp.where(row < c, value, passed)
    dz, dr, dn, ds = [None] * STEPS, [None] * STEPS, [None] * STEPS, [None] * STEPS
    for j in reversed(range(STEPS)):
        at = slice(j * CHUNKS, (j + 1) * CHUNKS)
        lam = cot_ref[at, :] + passed
        dz[j], dr[j], dn[j] = coef_ref[2, at, :] * lam, coef_ref[3, at, :] * lam, coef_ref[4, at, :] * lam
        ds[j] = coef_ref[5, at, :] * lam
        if j > 0:
            high, low_part = split(jnp.concatenate([dz[j], dr[j], dn[j]], axis=1))
            both = mm(jnp.concatenate([high, low_part], axis=0), uth_ref[...])
            pulled = both[:CHUNKS] + both[CHUNKS:] + mm(high, utl_ref[...])
            passed = coef_ref[1, at, :] * lam + pulled
    dz, dr, dn, ds = (jnp.concatenate(part, axis=0) for part in (dz, dr, dn, ds))

    def stacked(value):
        return jnp.concatenate([value[:, :H], value[:, H:]], axis=0)

    sz, sr, sn, ss = (stacked(part) for part in (dz, dr, dn, ds))
    zero = jnp.zeros((2 * 64, H), F32)
    high, low_part = split(jnp.concatenate([sz, sr, ss, zero], axis=1))
    xin = xin_ref[...]
    grad_in = mm_tn(jnp.concatenate([high, low_part], axis=0), jnp.concatenate([xin, xin], axis=0))
    high, low_part = split(jnp.concatenate([sz, sr, sn, zero], axis=1))
    prev_high, prev_low = split(stacked(coef_ref[0]))
    grad_rec = mm_tn(
        jnp.concatenate([prev_high, prev_low, prev_high], axis=0),
        jnp.concatenate([high, high, low_part], axis=0),
    )
    full_ref[0:192, :] = grad_in[:192, :LANES]
    full_ref[192:384, :] = grad_in[:192, LANES:]
    full_ref[384:448, :] = grad_rec[:, :LANES]
    rest = grad_rec[:, LANES:]
    full_ref[448:480, :] = jnp.concatenate([rest[:32, :H], rest[32:, :H]], axis=1)
    sums = [jnp.sum(part, axis=0, keepdims=True) for part in (sz, sr, ss, sn)]
    scale = sums[0] / bias_ref[4:5, :H]
    tail = jnp.concatenate(
        [jnp.concatenate([scale, sums[1]], axis=1), jnp.concatenate([sums[2], sums[3]], axis=1)], axis=0
    )
    full_ref[480:512, :] = jnp.concatenate([tail, jnp.zeros((30, LANES), F32)], axis=0)
    core, x = where_ref[1], where_ref[3]
    for d in range(4):
        part = lax.rem(x + d, 4)
        rows = slice(d * 64, (d + 1) * 64)
        keep_ref[rows, :] = full_ref[pl.ds(pl.multiple_of((core * 4 + part) * 64, 64), 64), :]
        give_ref[rows, :] = full_ref[pl.ds(pl.multiple_of(((1 - core) * 4 + part) * 64, 64), 64), :]
    for d in range(4):
        part = lax.rem(x + d, 4)
        whole = jnp.where(part // 2 == core, states_ref[...], across_ref[...])
        block = jnp.where(lax.rem(part, 2) == 0, whole, swap_halves(whole))
        home_ref[d] = jnp.where(lane_low((32, LANES)), block[:32], swap_halves(block[32:]))


def home_kernel(where_ref, home_ref, one_ref, two_ref, three_ref, traj_ref):
    core, x = where_ref[1], where_ref[3]
    blocks = [home_ref[0]] + [ref[64:96, :] for ref in (one_ref, two_ref, three_ref)]
    for e in range(2):
        where = lax.rem(x + 4 - 2 * core - e, 4)
        block = blocks[0]
        for d in range(1, 4):
            block = jnp.where(where == d, blocks[d], block)
        block = jnp.concatenate([block, swap_halves(block)], axis=0)
        traj_ref[:, e, :] = jnp.transpose(block)[:H]


def unpack_kernel(
    where_ref, one_ref, two_ref, three_ref, both_ref, in_ref, rec_ref, scale_ref, bias_ref, full_ref
):
    x = where_ref[3]
    pieces = (both_ref, one_ref, two_ref, three_ref)
    for d in range(4):
        part = lax.rem(x + 4 - d, 4)
        for core in range(2):
            full_ref[pl.ds(pl.multiple_of((core * 4 + part) * 64, 64), 64), :] = pieces[d][core]
    in_ref[:, :LANES] = full_ref[0:192, :]
    in_ref[:, LANES:] = full_ref[192:384, :]
    rec_ref[:, :LANES] = full_ref[384:448, :]
    rec_ref[0:32, LANES:] = full_ref[448:480, :H]
    rec_ref[32:, LANES:] = full_ref[448:480, H:]
    one, two = full_ref[480:481, :], full_ref[481:482, :]
    scale_ref[...] = one[:, :H]
    bias_ref[...] = jnp.concatenate([one[:, H:], two[:, :H], two[:, H:]], axis=0)


def call(kernel, outs, kinds, *operands, scratch=()):
    spaces = {"s": SMEM, "v": VMEM, "h": pltpu.HBM}
    specs = [pl.BlockSpec(memory_space=spaces[kind]) for kind in kinds]
    operands = [
        pltpu.with_memory_space_constraint(operand, pltpu.HBM) if kind == "h" else operand
        for kind, operand in zip(kinds, operands)
    ]
    return pl.pallas_call(
        kernel,
        out_shape=[jax.ShapeDtypeStruct(*out) for out in outs],
        in_specs=specs,
        out_specs=[pl.BlockSpec(memory_space=VMEM)] * len(outs),
        scratch_shapes=list(scratch),
        compiler_params=pltpu.CompilerParams(vmem_limit_bytes=16 * 1024 * 1024),
    )(*operands)


def local(planes, width, ys, inputs, w_in, u_rec, timescale, other_bias, h_init, cotangent):
    place, part = lax.axis_index("seq"), lax.axis_index("batch")
    z, x, core = place // width, place % width, part % 2
    where = jnp.stack([x % 2, core, z * 2 + core, x]).astype(jnp.int32)

    def at(z, x, y, core):
        return (z * width + x) * (2 * ys) + y * 2 + core

    there = []
    for m in range(2):
        pairs = [
            (at(z, x, y, c), at(z, 2 * c + ((x % 2) ^ m), y, x // 2))
            for z in range(planes) for x in range(width) for y in range(ys) for c in range(2)
        ]
        there.append(pairs)
    step_x = [
        [(z * width + x, z * width + (x + d) % width) for z in range(planes) for x in range(width)]
        for d in range(1, width)
    ]
    along_z = [[z * width + x for z in range(planes)] for x in range(width)]
    step_y = [[(b, (b + 2 * d) % (2 * ys)) for b in range(2 * ys)] for d in range(1, ys)]
    cores = [(b, b ^ 1) for b in range(2 * ys)]
    axes = ("seq", "batch")

    def exchange(value):
        own = lax.all_to_all(value, "seq", 0, 0, axis_index_groups=along_z, tiled=True)
        return own, lax.ppermute(own, "batch", cores)

    sems = pltpu.SemaphoreType.DMA((4,))
    one, two = call(
        pack_kernel, [((PART, LANES), F32)] * 2, "shhh", where, inputs, cotangent, h_init.T,
        scratch=[
            pltpu.VMEM(inputs.shape, BF16), pltpu.VMEM(cotangent.shape, F32), pltpu.VMEM((2, H), F32), sems
        ],
    )
    one = lax.ppermute(one, axes, there[0])
    two = lax.ppermute(two, axes, there[1])
    w3, ws, uth, utl, ud, bias, w = call(
        weights_kernel,
        [
            ((384, 384), BF16), ((384, 512), BF16), ((384, LANES), BF16), ((384, LANES), BF16),
            ((3, H, LANES), F32), ((8, LANES), F32), ((192, 256), BF16),
        ],
        "hhhh", u_rec, timescale[None, :], other_bias, w_in.T,
        scratch=[pltpu.VMEM((H, 192), F32), pltpu.VMEM((1, H), F32), pltpu.VMEM((3, H), F32), sems],
    )
    maps_t, chunk_t = ((STEPS, ROWS, LANES), F32), ((CHUNKS, H, LANES), F32)
    ends_t, send_t = ((72, LANES), F32), ((planes, MAP, LANES), F32)
    x3, xin, cot, start, maps, chunk, ends, send = call(
        first_kernel,
        [((3, 64, LANES), F32), ((128, 256), BF16), ((64, LANES), F32), ((8, LANES), F32), maps_t, chunk_t, ends_t, send_t],
        "svvvvvvv", where, one, two, w, w3, ws, ud, bias,
        scratch=[pltpu.VMEM((64, LANES), F32)],
    )
    spread_s = pltpu.VMEM((H * CHUNKS, LANES), F32)
    for _ in range(NEWTON - 1):
        own, other = exchange(send)
        maps, chunk, ends, send = call(
            next_kernel, [maps_t, chunk_t, ends_t, send_t], "svvvvvvvvvvv",
            where, own, other, start, x3, bias, w3, ws, ud, maps, chunk, ends, scratch=[spread_s],
        )
    own, other = exchange(send)
    states, coef, chunk, vector, half, send = call(
        turn_kernel,
        [
            ((64, LANES), F32), ((6, 64, LANES), F32), chunk_t,
            ((8, LANES), F32), ((72, LANES), F32), send_t,
        ],
        "svvvvvvvvvvvv", where, own, other, start, x3, bias, w3, ws, ud, maps, chunk, ends, cot,
        scratch=[
            spread_s, pltpu.VMEM(*maps_t),
            pltpu.VMEM((H * CHUNKS, LANES), F32),
        ],
    )
    across = lax.ppermute(states, "batch", cores)
    own, other = exchange(send)
    keep, give, home = call(
        gradient_kernel, [((256, LANES), F32), ((256, LANES), F32), ((4, 32, LANES), F32)], "svvvvvvvvvvvvv",
        where, own, other, coef, chunk, vector, half, cot, uth, utl, xin, bias, states, across,
        scratch=[pltpu.VMEM((512, LANES), F32)],
    )

    def around(values, axis, pairs):
        return [lax.ppermute(value, axis, pair) for value, pair in zip(values, pairs)]

    parts = (keep + lax.ppermute(give, "batch", cores)).reshape(width, -1, LANES)
    early = around([jnp.concatenate([parts[d], home[d]], axis=0) for d in range(1, width)], "seq", step_x)
    part = parts[0] + sum(piece[:64] for piece in early)
    part = part + sum(around([part] * (ys - 1), "batch", step_y))
    wide = jnp.broadcast_to(part[None], (planes,) + part.shape)
    part = lax.all_to_all(wide, "seq", 0, 0, axis_index_groups=along_z, tiled=True).sum(0)
    other = lax.ppermute(part, "batch", cores)
    first = core == 0
    both = jnp.stack([jnp.where(first, part, other), jnp.where(first, other, part)])
    rest = around([both] * (width - 1), "seq", step_x)
    (traj,) = call(home_kernel, [((H, 2, 64), F32)], "svvvv", where, home, *early)
    grad_in, grad_rec, grad_scale, grad_other = call(
        unpack_kernel,
        [((192, 256), F32), ((H, 192), F32), ((1, H), F32), ((3, H), F32)], "svvvv",
        where, *rest, both, scratch=[pltpu.VMEM((512, LANES), F32)],
    )
    return traj, grad_in.T, grad_rec, grad_scale[0], grad_other


def solution(mesh):
    width = 4
    planes = mesh.shape["seq"] // width
    ys = mesh.shape["batch"] // 2
    return jax.shard_map(
        functools.partial(local, planes, width, ys),
        mesh=mesh,
        in_specs=(P("batch", "seq", None), P(), P(), P(), P(), P(None, "batch"), P(None, "batch", "seq")),
        out_specs=(P(None, "batch", "seq"), P(), P(), P(), P()),
        check_vma=False,
    )
```

```python
import functools

import jax
import jax.numpy as jnp
from jax import lax
from jax.experimental import pallas as pl
from jax.experimental.pallas import tpu as pltpu
from jax.sharding import PartitionSpec as P

NEWTON = 3
H = 64
LANES = 128
CHUNKS = 8
STEPS = 8
COLS = H + 1
ROWS = COLS * CHUNKS
BLOCK = 13
MAP = 40
PART = 168
F32 = jnp.float32
BF16 = jnp.bfloat16
VMEM = pltpu.VMEM
SMEM = pltpu.SMEM


def split(value):
    high = value.astype(BF16)
    return high, (value - high.astype(F32)).astype(BF16)


def mm(left, right):
    return jnp.dot(left, right, preferred_element_type=F32)


def mm_nt(left, right):
    return lax.dot_general(left, right, (((1,), (1,)), ((), ())), preferred_element_type=F32)


def mm_tn(left, right):
    return lax.dot_general(left, right, (((0,), (0,)), ((), ())), preferred_element_type=F32)


def left3(value):
    high, low = split(value)
    return jnp.concatenate([high, low, high], axis=1)


def right3(value):
    high, low = split(value)
    return jnp.concatenate([high, high, low], axis=0)


def lane_low(shape):
    return lax.broadcasted_iota(jnp.int32, shape, 1) < H


def swap_halves(value):
    return pltpu.roll(value, H, axis=1)


def doubled(value, half):
    low = lane_low(value.shape)
    other = swap_halves(value)
    return jnp.where(low, value, other) if half == 0 else jnp.where(low, other, value)


def right_doubled(matrix):
    high, low = split(matrix)
    return jnp.concatenate([high, low, high, low], axis=0)


def left_doubled(value):
    high, low = split(value)
    return jnp.concatenate([high, low], axis=1)


def block_diagonal(matrix):
    low = lane_low(matrix.shape)
    return jnp.concatenate([jnp.where(low, matrix, 0.0), jnp.where(low, 0.0, matrix)], axis=0)


def fetch(sources, targets, sems):
    copies = [pltpu.make_async_copy(a, b, sems.at[n]) for n, (a, b) in enumerate(zip(sources, targets))]
    for copy in copies:
        copy.start()
    for copy in copies:
        copy.wait()


def weights_kernel(
    u_hbm, scale_hbm, other_hbm, w_hbm, w3_ref, ws_ref, uth_ref, utl_ref, ud_ref, bias_ref, w_ref,
    u_ref, scale_ref, other_ref, sems,
):
    fetch((u_hbm, scale_hbm, other_hbm, w_hbm), (u_ref, scale_ref, other_ref, w_ref), sems)
    zero = jnp.zeros((H, H), F32)
    for g in range(3):
        block = u_ref[:, g * H : (g + 1) * H]
        ud_ref[g] = jnp.concatenate([block, block], axis=1)
        diag = jnp.concatenate(
            [jnp.concatenate([block, zero], axis=1), jnp.concatenate([zero, block], axis=1)], axis=0
        )
        at = slice(g * LANES, (g + 1) * LANES)
        high, low = split(diag)
        w3_ref[0:LANES, at] = high
        w3_ref[LANES : 2 * LANES, at] = high
        w3_ref[2 * LANES : 3 * LANES, at] = low
        ws_ref[0:LANES, at] = high
        ws_ref[LANES : 2 * LANES, at] = high
        ws_ref[2 * LANES : 3 * LANES, at] = low
        if g == 2:
            ws_ref[0:LANES, 3 * LANES :] = low
            ws_ref[LANES : 2 * LANES, 3 * LANES :] = low
            ws_ref[2 * LANES : 3 * LANES, 3 * LANES :] = low
        high, low = split(diag.T)
        uth_ref[at, :] = high
        utl_ref[at, :] = low
    scale = scale_ref[...]
    rows = [jnp.log(scale), other_ref[0:1, :], other_ref[1:2, :], other_ref[2:3, :], scale]
    rows = [jnp.concatenate([row, row], axis=1) for row in rows]
    bias_ref[...] = jnp.concatenate(rows + [jnp.zeros((3, LANES), F32)], axis=0)


def pack_kernel(where_ref, x_hbm, cot_hbm, h_hbm, one_ref, two_ref, x_ref, cot_ref, h_ref, sems):
    fetch((x_hbm, cot_hbm, h_hbm), (x_ref, cot_ref, h_ref), sems)
    odd = where_ref[0]
    zero = jnp.zeros((H, H), F32)
    cots = []
    for e in range(2):
        cots.append(jnp.transpose(jnp.concatenate([cot_ref[:, e, :], zero], axis=1))[:H])
    for m, out_ref in enumerate((one_ref, two_ref)):
        first = odd == m
        x = jnp.where(first, x_ref[0].astype(F32), x_ref[1].astype(F32))
        out_ref[0:64, :] = x[:, :LANES]
        out_ref[64:128, :] = x[:, LANES:]
        cot = jnp.where(first, cots[0], cots[1])
        out_ref[128:160, :] = jnp.concatenate([cot[:32], cot[32:]], axis=1)
        start = jnp.where(first, h_ref[0:1, :], h_ref[1:2, :])
        start = jnp.concatenate([start, start], axis=1)
        out_ref[160:168, :] = jnp.broadcast_to(start, (8, LANES))


def coefficients(prev, x3, bias, w3):
    mixed = mm(left3(prev), w3)
    mz, mr, mn = mixed[:, :LANES], mixed[:, LANES : 2 * LANES], mixed[:, 2 * LANES :]
    update = jax.nn.sigmoid(x3[0] + mz)
    reset = jax.nn.sigmoid(x3[1] + mr)
    recur = mn + bias[3:4, :]
    cand = jnp.tanh(x3[2] + reset * recur)
    fresh = (1.0 - update) * cand + update * prev
    slope = (1.0 - update) * (1.0 - cand * cand)
    cz = (prev - cand) * update * (1.0 - update)
    cr = slope * recur * reset * (1.0 - reset)
    cn = slope * reset
    offset = fresh - (update * prev + cz * mz + cr * mr + cn * mn)
    return update, cz, cr, cn, slope, offset


def gate_products(rows, ws_ref):
    high, low = split(rows)
    pair = jnp.concatenate([high, low], axis=1)
    both = mm(jnp.concatenate([pair, high], axis=1), ws_ref[:, : 2 * LANES])
    last = mm(pair, ws_ref[: 2 * LANES, 2 * LANES :])
    return both[:, :LANES], both[:, LANES:], last[:, :LANES] + last[:, LANES:]


def scan_maps(coef, ws_ref, ud_ref, maps_ref):
    update, cz, cr, cn, _, offset = coef
    shape = (BLOCK, CHUNKS, LANES)
    for j in range(STEPS):
        at = slice(j * CHUNKS, (j + 1) * CHUNKS)
        up_j, cz_j, cr_j, cn_j = (a[at][None] for a in (update, cz, cr, cn))
        for b in range(COLS // BLOCK):
            rows = slice(b * BLOCK * CHUNKS, (b + 1) * BLOCK * CHUNKS)
            last = b == COLS // BLOCK - 1
            if j == 0:
                real = BLOCK - 1 if last else BLOCK
                cols = slice(b * BLOCK, b * BLOCK + real)
                k = lax.broadcasted_iota(jnp.int32, (real, CHUNKS, LANES), 0) + b * BLOCK
                lane = lax.broadcasted_iota(jnp.int32, (real, CHUNKS, LANES), 2) % H
                new = jnp.where(k == lane, up_j, 0.0)
                for c, g in ((cz_j, 0), (cr_j, 1), (cn_j, 2)):
                    new = new + c * ud_ref[g, cols, :][:, None, :]
                if last:
                    new = jnp.concatenate([new, offset[at][None]], axis=0)
            else:
                old = maps_ref[j - 1, rows, :]
                mz, mr, mn = (part.reshape(shape) for part in gate_products(old, ws_ref))
                new = up_j * old.reshape(shape) + cz_j * mz + cr_j * mr + cn_j * mn
                if last:
                    new = jnp.concatenate([new[: BLOCK - 1], new[BLOCK - 1 :] + offset[at][None]], axis=0)
            maps_ref[j, rows, :] = new.reshape(BLOCK * CHUNKS, LANES)


def chunk_matrix(maps_ref, c):
    return maps_ref[STEPS - 1, pl.ds(c, H, stride=CHUNKS), :]


def chunk_vector(maps_ref, c):
    return maps_ref[STEPS - 1, H * CHUNKS + c : H * CHUNKS + c + 1, :]


def compose(earlier, later):
    row = lax.broadcasted_iota(jnp.int32, (72, LANES), 0)
    both = mm(left3(earlier), right3(block_diagonal(later[:H])))
    return both + jnp.where(row == H, later[H : H + 1], 0.0)


def chunk_levels(maps_ref):
    pad = jnp.zeros((7, LANES), F32)
    levels = [[
        jnp.concatenate([chunk_matrix(maps_ref, c), chunk_vector(maps_ref, c), pad], axis=0) for c in range(CHUNKS)
    ]]
    while len(levels[-1]) > 1:
        parts = levels[-1]
        levels.append([compose(a, b) for a, b in zip(parts[::2], parts[1::2])])
    return levels


def flip_halves(matrix):
    turned = jnp.transpose(matrix)
    return jnp.concatenate([turned[:H], turned[H:]], axis=1)


def diagonal(rows):
    row = lax.broadcasted_iota(jnp.int32, (H, LANES), 0)
    lane = lax.broadcasted_iota(jnp.int32, (H, LANES), 1) % H
    return jnp.where(row == lane, rows, 0.0)


def to_column(row, matrix, vector):
    low = lane_low(matrix.shape)
    prod = matrix * row + diagonal(vector)
    first = jnp.sum(jnp.where(low, prod, 0.0), axis=1, keepdims=True)
    second = jnp.sum(jnp.where(low, 0.0, prod), axis=1, keepdims=True)
    return jnp.where(low, first, second)


def to_row(column, matrix, vector):
    return jnp.sum(column * matrix, axis=0, keepdims=True) + vector


def as_row(column):
    return jnp.sum(diagonal(column), axis=0, keepdims=True)


def join_halves(total):
    row = lax.broadcasted_iota(jnp.int32, (72, LANES), 0)
    second = doubled(total, 1)
    both = mm(left_doubled(doubled(total, 0)), right_doubled(second[:H]))
    return both + jnp.where(row == H, second, 0.0)


def send_map(total, flipped, where_ref, out_ref):
    low = lane_low((H // 2, LANES))
    matrix = jnp.where(where_ref[1] == 0, flipped, total[:H])
    packed = jnp.where(low, matrix[: H // 2], matrix[H // 2 :])
    for z in range(out_ref.shape[0]):
        out_ref[z, : H // 2, :] = packed
        out_ref[z, H // 2 :, :] = total[H:]


def flip(matrix):
    square = jnp.transpose(matrix)[:H]
    return jnp.concatenate([square, square], axis=1)


def unpack_map(packed, whole):
    body = packed[: H // 2]
    other = swap_halves(body)
    low = lane_low(body.shape)
    if whole:
        parts = [jnp.where(low, body, other), jnp.where(low, other, body)]
    else:
        parts = [jnp.where(low, body, 0.0), jnp.where(low, other, 0.0)]
    return jnp.concatenate(parts, axis=0), packed[H // 2 : H // 2 + 1]


def apply_row(state, matrix, vector):
    return mm(left_doubled(state), right_doubled(matrix)) + vector


def enter_device(where_ref, own_ref, other_ref, start, reverse):
    core, mine = where_ref[1], where_ref[2]
    planes = own_ref.shape[0]
    row = lax.broadcasted_iota(jnp.int32, (H, LANES), 0)
    lane = lax.broadcasted_iota(jnp.int32, (H, LANES), 1)
    eye = jnp.where(row == lane, 1.0, 0.0)
    eyes = jnp.where(row == lane % H, 1.0, 0.0)
    state = start[0:1]
    order = list(range(2 * planes))
    for n in reversed(order) if reverse else order:
        z, kappa = n // 2, n % 2
        reached = (mine < n) if reverse else (mine > n)
        packed = jnp.where(core == kappa, own_ref[z], other_ref[z])
        to_column = kappa == (1 if reverse else 0)
        matrix, vector = unpack_map(packed, not to_column)
        vector = jnp.where(reached, vector, 0.0)
        if to_column:
            matrix = jnp.where(reached, matrix, eye)
            summed = jnp.sum(matrix * state + eye * vector, axis=1, keepdims=True)
            state = jnp.broadcast_to(summed, (H, LANES))
        else:
            matrix = jnp.where(reached, matrix, eyes)
            state = jnp.sum(matrix * state, axis=0, keepdims=True) + vector
    return jnp.broadcast_to(state, (CHUNKS, LANES))


def spread(rows, count):
    k = lax.broadcasted_iota(jnp.int32, (count,) + rows.shape, 0)
    lane = lax.broadcasted_iota(jnp.int32, (count,) + rows.shape, 2) % H
    picked = jnp.where(k == lane, rows[None], 0.0).reshape(count * rows.shape[0], LANES)
    one = (
        lax.broadcasted_iota(jnp.int32, (LANES, LANES), 0) // H
        == lax.broadcasted_iota(jnp.int32, (LANES, LANES), 1) // H
    )
    one = jnp.where(one, 1.0, 0.0).astype(BF16)
    high, low = split(picked)
    rest = (picked - high.astype(F32) - low.astype(F32)).astype(BF16)
    return mm(jnp.concatenate([high, low, rest], axis=1), jnp.concatenate([one, one, one], axis=0))


def store_chunks(levels, chunk_ref, vector_ref):
    ones, twos, fours, _ = levels
    parts = (ones[0], twos[0], fours[0], ones[6], ones[2], ones[4], twos[2])
    for n, part in enumerate(parts):
        chunk_ref[n] = flip_halves(part[:H]) if n < 4 else part[:H]
        vector_ref[n : n + 1, :] = part[H : H + 1]


def enter_chunks(state, chunk_ref, vector_ref, ends_ref):
    low = lane_low((CHUNKS, LANES))
    first = doubled(ends_ref[...], 0)
    middle = apply_row(state, first[:H], first[H : H + 1])
    entering = jnp.where(low, state, middle)
    vectors = vector_ref[...]
    row = entering[0:1]
    one, two, four = (to_column(row, chunk_ref[n], vectors[n : n + 1]) for n in range(3))
    three = to_row(two, chunk_ref[4], vectors[4:5])
    five = to_row(four, chunk_ref[5], vectors[5:6])
    six = to_row(four, chunk_ref[6], vectors[6:7])
    seven = to_column(six, chunk_ref[3], vectors[3:4])
    rows = [row, as_row(one), as_row(two), three, as_row(four), five, six, as_row(seven)]
    return jnp.concatenate(rows, axis=0)


def trajectory(entering, maps_ref, spread_ref):
    spread_ref[...] = spread(entering, H)
    states = [maps_ref[j, H * CHUNKS :, :] for j in range(STEPS)]
    for b in range(0, H * CHUNKS, 64):
        factor = spread_ref[b : b + 64, :].reshape(8, CHUNKS, LANES)
        for j in range(STEPS):
            block = maps_ref[j, b : b + 64, :].reshape(8, CHUNKS, LANES)
            states[j] = states[j] + jnp.sum(block * factor, axis=0)
    return states


def phase(where_ref, prev, x3_ref, bias_ref, w3_ref, ws_ref, ud_ref, maps_ref, chunk_ref, vector_ref, ends_ref, out_ref):
    coef = coefficients(prev, x3_ref, bias_ref[...], w3_ref[...])
    scan_maps(coef, ws_ref, ud_ref, maps_ref)
    levels = chunk_levels(maps_ref)
    store_chunks(levels, chunk_ref, vector_ref)
    total = levels[-1][0]
    ends_ref[...] = total
    total = join_halves(total)
    send_map(total, flip(total[:H]), where_ref, out_ref)


def first_kernel(
    where_ref, a_ref, b_ref, w_ref, w3_ref, ws_ref, ud_ref, bias_ref,
    x3_ref, xin_ref, cot_ref, start_ref, maps_ref, chunk_ref, vector_ref, ends_ref, out_ref, natural_ref,
):
    odd, mine = where_ref[0], where_ref[2]
    pieces = []
    for v in range(2):
        for j in range(STEPS):
            rows = [
                jnp.where(odd == v, a_ref[pl.ds(o + j, 8, stride=8), :], b_ref[pl.ds(o + j, 8, stride=8), :])
                for o in (0, 64)
            ]
            pieces.append(jnp.concatenate(rows, axis=1))
    xin = jnp.concatenate(pieces, axis=0).astype(BF16)
    xin_ref[...] = xin
    cots = [jnp.where(odd == v, a_ref[128:160, :], b_ref[128:160, :]) for v in range(2)]
    low = lane_low((32, LANES))
    natural_ref[0:32, :] = jnp.where(low, cots[0], swap_halves(cots[1]))
    natural_ref[32:64, :] = jnp.where(low, swap_halves(cots[0]), cots[1])
    cot_ref[...] = jnp.concatenate([natural_ref[pl.ds(j, 8, stride=8), :] for j in range(STEPS)], axis=0)
    start = a_ref[160:168, :]
    start_ref[...] = start
    flat = mm_nt(xin, w_ref[...])
    bias = bias_ref[...]
    for g in range(3):
        cols = slice(g * H, (g + 1) * H)
        x3_ref[g] = jnp.concatenate([flat[:64, cols], flat[64:, cols]], axis=1) + bias[g : g + 1, :]
    row = lax.broadcasted_iota(jnp.int32, (64, LANES), 0)
    lane = lax.broadcasted_iota(jnp.int32, (64, LANES), 1)
    here = (row == 0) & (lane < H) & (mine == 0)
    prev = jnp.where(here, start[0:1, :], 0.0)
    phase(where_ref, prev, x3_ref, bias_ref, w3_ref, ws_ref, ud_ref, maps_ref, chunk_ref, vector_ref, ends_ref, out_ref)


def next_kernel(
    where_ref, own_ref, other_ref, start_ref, x3_ref, bias_ref, w3_ref, ws_ref, ud_ref, old_ref, pieces_ref, rows_ref, before_ref,
    maps_ref, chunk_ref, vector_ref, ends_ref, out_ref, spread_ref,
):
    state = enter_device(where_ref, own_ref, other_ref, start_ref[...], False)
    entering = enter_chunks(state, pieces_ref, rows_ref, before_ref)
    states = trajectory(entering, old_ref, spread_ref)
    prev = jnp.concatenate([entering] + states[:-1], axis=0)
    phase(where_ref, prev, x3_ref, bias_ref, w3_ref, ws_ref, ud_ref, maps_ref, chunk_ref, vector_ref, ends_ref, out_ref)


def half_sums(value):
    row = lax.broadcasted_iota(jnp.int32, (8, LANES), 0)
    low = lane_low((8, LANES))
    pick = jnp.where((row == 0) & low, 1.0, 0.0) + jnp.where((row == 1) & ~low, 1.0, 0.0)
    pick = pick.astype(BF16)
    return mm_nt(jnp.concatenate([pick, pick], axis=1), left_doubled(value))


def turn_kernel(
    where_ref, own_ref, other_ref, start_ref, x3_ref, bias_ref, w3_ref, ws_ref, ud_ref, old_ref, pieces_ref, rows_ref, before_ref, cot_ref,
    states_ref, coef_ref, chunk_ref, vector_ref, half_ref, out_ref,
    spread_ref, maps_ref, acc_ref,
):
    state = enter_device(where_ref, own_ref, other_ref, start_ref[...], False)
    entering = enter_chunks(state, pieces_ref, rows_ref, before_ref)
    states = trajectory(entering, old_ref, spread_ref)
    for j in range(STEPS):
        states_ref[pl.ds(j, CHUNKS, stride=STEPS), :] = states[j]
    prev = jnp.concatenate([entering] + states[:-1], axis=0)
    coef = coefficients(prev, x3_ref, bias_ref[...], w3_ref[...])
    coef_ref[0] = prev
    for n in range(5):
        coef_ref[n + 1] = coef[n]
    scan_maps(coef, ws_ref, ud_ref, maps_ref)
    levels = chunk_levels(maps_ref)
    total = levels[-1][0]
    for b in range(0, H * CHUNKS, 64):
        acc = jnp.zeros((8, CHUNKS, LANES), F32)
        for j in range(STEPS):
            block = maps_ref[j, b : b + 64, :].reshape(8, CHUNKS, LANES)
            acc = acc + block * cot_ref[j * CHUNKS : (j + 1) * CHUNKS, :][None]
        acc_ref[b : b + 64, :] = acc.reshape(64, LANES)
    vectors = []
    for c in range(CHUNKS):
        sums = half_sums(acc_ref[pl.ds(c, H, stride=CHUNKS), :])
        vectors.append(jnp.concatenate([sums[0:1], sums[1:2]], axis=1))
    ones, twos, fours, _ = [[part[:H] for part in level] for level in levels]
    flip_23 = flip_halves(twos[1])
    pairs = [to_column(vectors[2 * n + 1], ones[2 * n], vectors[2 * n]) for n in range(4)]
    pair_rows = [as_row(pair) for pair in pairs]
    quad_low = to_row(pairs[1], flip_halves(twos[0]), pair_rows[0])
    quad_high = to_row(pairs[3], flip_halves(twos[2]), pair_rows[2])
    ends = as_row(to_column(quad_high, fours[0], quad_low))
    matrices = (fours[1], twos[3], ones[7], flip_23, flip_halves(ones[5]), flip_halves(ones[3]), ones[1])
    rows = (quad_high, pair_rows[3], vectors[7], pair_rows[1], vectors[5], vectors[3], vectors[1])
    for n, (matrix, vector) in enumerate(zip(matrices, rows)):
        chunk_ref[n] = matrix
        vector_ref[n : n + 1, :] = vector
    tail = doubled(ends, 1)
    low = lane_low((H, LANES))
    sums = half_sums(jnp.where(low, total[:H], 0.0) * tail)
    left = ends[:, :H] + sums[0:1]
    both = join_halves(total)
    pad = jnp.zeros((7, LANES), F32)
    left = jnp.concatenate([left, left], axis=1)
    send_map(jnp.concatenate([both[:H], left, pad], axis=0), flip(both[:H]), where_ref, out_ref)
    half_ref[...] = jnp.concatenate([flip(doubled(total[:H], 1)), tail, pad], axis=0)


def gradient_kernel(
    where_ref, own_ref, other_ref, coef_ref, chunk_ref, vector_ref, half_ref, cot_ref, uth_ref, utl_ref,
    xin_ref, bias_ref, states_ref, across_ref, keep_ref, give_ref, home_ref, full_ref,
):
    low = lane_low((CHUNKS, LANES))
    right = enter_device(where_ref, own_ref, other_ref, jnp.zeros((CHUNKS, LANES), F32), True)
    half = half_ref[...]
    middle = apply_row(right, half[:H], half[H : H + 1])
    last = jnp.where(low, middle, right)[0:1]
    vectors = vector_ref[...]
    three, five, six = (to_column(last, chunk_ref[n], vectors[n : n + 1]) for n in range(3))
    one = to_row(three, chunk_ref[3], vectors[3:4])
    four = to_row(five, chunk_ref[4], vectors[4:5])
    two = to_row(three, chunk_ref[5], vectors[5:6])
    zero = to_column(one, chunk_ref[6], vectors[6:7])
    passed = jnp.concatenate(
        [as_row(zero), one, two, as_row(three), four, as_row(five), as_row(six), last], axis=0
    )
    dz, dr, dn, ds = [None] * STEPS, [None] * STEPS, [None] * STEPS, [None] * STEPS
    for j in reversed(range(STEPS)):
        at = slice(j * CHUNKS, (j + 1) * CHUNKS)
        lam = cot_ref[at, :] + passed
        dz[j], dr[j], dn[j] = coef_ref[2, at, :] * lam, coef_ref[3, at, :] * lam, coef_ref[4, at, :] * lam
        ds[j] = coef_ref[5, at, :] * lam
        if j > 0:
            high, low_part = split(jnp.concatenate([dz[j], dr[j], dn[j]], axis=1))
            both = mm(jnp.concatenate([high, low_part], axis=0), uth_ref[...])
            pulled = both[:CHUNKS] + both[CHUNKS:] + mm(high, utl_ref[...])
            passed = coef_ref[1, at, :] * lam + pulled
    dz, dr, dn, ds = (jnp.concatenate(part, axis=0) for part in (dz, dr, dn, ds))

    def stacked(value):
        return jnp.concatenate([value[:, :H], value[:, H:]], axis=0)

    sz, sr, sn, ss = (stacked(part) for part in (dz, dr, dn, ds))
    zero = jnp.zeros((2 * 64, H), F32)
    high, low_part = split(jnp.concatenate([sz, sr, ss, zero], axis=1))
    xin = xin_ref[...]
    grad_in = mm_tn(jnp.concatenate([high, low_part], axis=0), jnp.concatenate([xin, xin], axis=0))
    high, low_part = split(jnp.concatenate([sz, sr, sn, zero], axis=1))
    prev_high, prev_low = split(stacked(coef_ref[0]))
    grad_rec = mm_tn(
        jnp.concatenate([prev_high, prev_low, prev_high], axis=0),
        jnp.concatenate([high, high, low_part], axis=0),
    )
    full_ref[0:192, :] = grad_in[:192, :LANES]
    full_ref[192:384, :] = grad_in[:192, LANES:]
    full_ref[384:448, :] = grad_rec[:, :LANES]
    rest = grad_rec[:, LANES:]
    full_ref[448:480, :] = jnp.concatenate([rest[:32, :H], rest[32:, :H]], axis=1)
    sums = [jnp.sum(part, axis=0, keepdims=True) for part in (sz, sr, ss, sn)]
    scale = sums[0] / bias_ref[4:5, :H]
    tail = jnp.concatenate(
        [jnp.concatenate([scale, sums[1]], axis=1), jnp.concatenate([sums[2], sums[3]], axis=1)], axis=0
    )
    full_ref[480:512, :] = jnp.concatenate([tail, jnp.zeros((30, LANES), F32)], axis=0)
    core, x = where_ref[1], where_ref[3]
    for d in range(4):
        part = lax.rem(x + d, 4)
        rows = slice(d * 64, (d + 1) * 64)
        keep_ref[rows, :] = full_ref[pl.ds(pl.multiple_of((core * 4 + part) * 64, 64), 64), :]
        give_ref[rows, :] = full_ref[pl.ds(pl.multiple_of(((1 - core) * 4 + part) * 64, 64), 64), :]
    for d in range(4):
        part = lax.rem(x + d, 4)
        whole = jnp.where(part // 2 == core, states_ref[...], across_ref[...])
        block = jnp.where(lax.rem(part, 2) == 0, whole, swap_halves(whole))
        home_ref[d] = jnp.where(lane_low((32, LANES)), block[:32], swap_halves(block[32:]))


def home_kernel(where_ref, home_ref, two_ref, one_ref, three_ref, traj_ref):
    core, x = where_ref[1], where_ref[3]
    blocks = [home_ref[0]] + [ref[64:96, :] for ref in (one_ref, two_ref, three_ref)]
    for e in range(2):
        where = lax.rem(x + 4 - 2 * core - e, 4)
        block = blocks[0]
        for d in range(1, 4):
            block = jnp.where(where == d, blocks[d], block)
        block = jnp.concatenate([block, swap_halves(block)], axis=0)
        traj_ref[:, e, :] = jnp.transpose(block)[:H]


def unpack_kernel(
    where_ref, three_ref, one_ref, two_ref, both_ref, in_ref, rec_ref, scale_ref, bias_ref, full_ref
):
    x = where_ref[3]
    pieces = (both_ref, one_ref, two_ref, three_ref)
    for d in range(4):
        part = lax.rem(x + 4 - d, 4)
        for core in range(2):
            full_ref[pl.ds(pl.multiple_of((core * 4 + part) * 64, 64), 64), :] = pieces[d][core]
    in_ref[:, :LANES] = full_ref[0:192, :]
    in_ref[:, LANES:] = full_ref[192:384, :]
    rec_ref[:, :LANES] = full_ref[384:448, :]
    rec_ref[0:32, LANES:] = full_ref[448:480, :H]
    rec_ref[32:, LANES:] = full_ref[448:480, H:]
    one, two = full_ref[480:481, :], full_ref[481:482, :]
    scale_ref[...] = one[:, :H]
    bias_ref[...] = jnp.concatenate([one[:, H:], two[:, :H], two[:, H:]], axis=0)


def call(kernel, outs, kinds, *operands, scratch=()):
    spaces = {"s": SMEM, "v": VMEM, "h": pltpu.HBM}
    specs = [pl.BlockSpec(memory_space=spaces[kind]) for kind in kinds]
    operands = [
        pltpu.with_memory_space_constraint(operand, pltpu.HBM) if kind == "h" else operand
        for kind, operand in zip(kinds, operands)
    ]
    return pl.pallas_call(
        kernel,
        out_shape=[jax.ShapeDtypeStruct(*out) for out in outs],
        in_specs=specs,
        out_specs=[pl.BlockSpec(memory_space=VMEM)] * len(outs),
        scratch_shapes=list(scratch),
        compiler_params=pltpu.CompilerParams(vmem_limit_bytes=16 * 1024 * 1024),
    )(*operands)


def local(planes, width, ys, inputs, w_in, u_rec, timescale, other_bias, h_init, cotangent):
    place, part = lax.axis_index("seq"), lax.axis_index("batch")
    z, x, core = place // width, place % width, part % 2
    where = jnp.stack([x % 2, core, z * 2 + core, x]).astype(jnp.int32)

    def at(z, x, y, core):
        return (z * width + x) * (2 * ys) + y * 2 + core

    there = []
    for m in range(2):
        pairs = [
            (at(z, x, y, c), at(z, 2 * c + ((x % 2) ^ m), y, x // 2))
            for z in range(planes) for x in range(width) for y in range(ys) for c in range(2)
        ]
        there.append(pairs)
    step_x = {
        d: [(z * width + x, z * width + (x + d) % width) for z in range(planes) for x in range(width)]
        for d in range(1, width)
    }
    along_z = [[z * width + x for z in range(planes)] for x in range(width)]
    step_y = {d: [(b, (b + 2 * d) % (2 * ys)) for b in range(2 * ys)] for d in range(1, ys)}
    cores = [(b, b ^ 1) for b in range(2 * ys)]
    axes = ("seq", "batch")

    def exchange(value):
        own = lax.all_to_all(value, "seq", 0, 0, axis_index_groups=along_z, tiled=True)
        return own, lax.ppermute(own, "batch", cores)

    sems = pltpu.SemaphoreType.DMA((4,))
    one, two = call(
        pack_kernel, [((PART, LANES), F32)] * 2, "shhh", where, inputs, cotangent, h_init.T,
        scratch=[
            pltpu.VMEM(inputs.shape, BF16), pltpu.VMEM(cotangent.shape, F32), pltpu.VMEM((2, H), F32), sems
        ],
    )
    one = lax.ppermute(one, axes, there[0])
    two = lax.ppermute(two, axes, there[1])
    w3, ws, uth, utl, ud, bias, w = call(
        weights_kernel,
        [
            ((384, 384), BF16), ((384, 512), BF16), ((384, LANES), BF16), ((384, LANES), BF16),
            ((3, H, LANES), F32), ((8, LANES), F32), ((192, 256), BF16),
        ],
        "hhhh", u_rec, timescale[None, :], other_bias, w_in.T,
        scratch=[pltpu.VMEM((H, 192), F32), pltpu.VMEM((1, H), F32), pltpu.VMEM((3, H), F32), sems],
    )
    maps_t, chunk_t = ((STEPS, ROWS, LANES), F32), ((CHUNKS, H, LANES), F32)
    rows_t, ends_t, send_t = ((8, LANES), F32), ((72, LANES), F32), ((planes, MAP, LANES), F32)
    x3, xin, cot, start, maps, chunk, vector, ends, send = call(
        first_kernel,
        [((3, 64, LANES), F32), ((128, 256), BF16), ((64, LANES), F32), ((8, LANES), F32), maps_t, chunk_t, rows_t, ends_t, send_t],
        "svvvvvvv", where, one, two, w, w3, ws, ud, bias,
        scratch=[pltpu.VMEM((64, LANES), F32)],
    )
    spread_s = pltpu.VMEM((H * CHUNKS, LANES), F32)
    for _ in range(NEWTON - 1):
        own, other = exchange(send)
        maps, chunk, vector, ends, send = call(
            next_kernel, [maps_t, chunk_t, rows_t, ends_t, send_t], "svvvvvvvvvvvv",
            where, own, other, start, x3, bias, w3, ws, ud, maps, chunk, vector, ends, scratch=[spread_s],
        )
    own, other = exchange(send)
    states, coef, chunk, vector, half, send = call(
        turn_kernel,
        [
            ((64, LANES), F32), ((6, 64, LANES), F32), chunk_t,
            ((8, LANES), F32), ((72, LANES), F32), send_t,
        ],
        "svvvvvvvvvvvvv", where, own, other, start, x3, bias, w3, ws, ud, maps, chunk, vector, ends, cot,
        scratch=[
            spread_s, pltpu.VMEM(*maps_t),
            pltpu.VMEM((H * CHUNKS, LANES), F32),
        ],
    )
    across = lax.ppermute(states, "batch", cores)
    own, other = exchange(send)
    keep, give, home = call(
        gradient_kernel, [((256, LANES), F32), ((256, LANES), F32), ((4, 32, LANES), F32)], "svvvvvvvvvvvvv",
        where, own, other, coef, chunk, vector, half, cot, uth, utl, xin, bias, states, across,
        scratch=[pltpu.VMEM((512, LANES), F32)],
    )

    def around(value_of, axis, steps, order):
        got = {d: lax.ppermute(value_of(d), axis, steps[d]) for d in order}
        return [got[d] for d in order]

    parts = (keep + lax.ppermute(give, "batch", cores)).reshape(width, -1, LANES)
    early = around(lambda d: jnp.concatenate([parts[d], home[d]], axis=0), "seq", step_x, (2, 1, 3))
    part = parts[0] + sum(piece[:64] for piece in early)
    part = part + sum(around(lambda d: part, "batch", step_y, (3, 1, 2)))
    wide = jnp.broadcast_to(part[None], (planes,) + part.shape)
    part = lax.all_to_all(wide, "seq", 0, 0, axis_index_groups=along_z, tiled=True).sum(0)
    other = lax.ppermute(part, "batch", cores)
    first = core == 0
    both = jnp.stack([jnp.where(first, part, other), jnp.where(first, other, part)])
    rest = around(lambda d: both, "seq", step_x, (3, 1, 2))
    (traj,) = call(home_kernel, [((H, 2, 64), F32)], "svvvv", where, home, *early)
    grad_in, grad_rec, grad_scale, grad_other = call(
        unpack_kernel,
        [((192, 256), F32), ((H, 192), F32), ((1, H), F32), ((3, H), F32)], "svvvv",
        where, *rest, both, scratch=[pltpu.VMEM((512, LANES), F32)],
    )
    return traj, grad_in.T, grad_rec, grad_scale[0], grad_other


def solution(mesh):
    width = 4
    planes = mesh.shape["seq"] // width
    ys = mesh.shape["batch"] // 2
    return jax.shard_map(
        functools.partial(local, planes, width, ys),
        mesh=mesh,
        in_specs=(P("batch", "seq", None), P(), P(), P(), P(), P(None, "batch"), P(None, "batch", "seq")),
        out_specs=(P(None, "batch", "seq"), P(), P(), P(), P()),
        check_vma=False,
    )
```

```python
import functools

import jax
import jax.numpy as jnp
from jax import lax
from jax.experimental import pallas as pl
from jax.experimental.pallas import tpu as pltpu
from jax.sharding import PartitionSpec as P

NEWTON = 3
H = 64
LANES = 128
CHUNKS = 8
STEPS = 8
COLS = H + 1
ROWS = COLS * CHUNKS
BLOCKS = (0, 22, 44, 65)
MAP = 40
PART = 168
F32 = jnp.float32
BF16 = jnp.bfloat16
VMEM = pltpu.VMEM
SMEM = pltpu.SMEM


def split(value):
    high = value.astype(BF16)
    return high, (value - high.astype(F32)).astype(BF16)


def mm(left, right):
    return jnp.dot(left, right, preferred_element_type=F32)


def mm_nt(left, right):
    return lax.dot_general(left, right, (((1,), (1,)), ((), ())), preferred_element_type=F32)


def mm_tn(left, right):
    return lax.dot_general(left, right, (((0,), (0,)), ((), ())), preferred_element_type=F32)


def left3(value):
    high, low = split(value)
    return jnp.concatenate([high, low, high], axis=1)


def right3(value):
    high, low = split(value)
    return jnp.concatenate([high, high, low], axis=0)


def lane_low(shape):
    return lax.broadcasted_iota(jnp.int32, shape, 1) < H


def swap_halves(value):
    return pltpu.roll(value, H, axis=1)


def doubled(value, half):
    low = lane_low(value.shape)
    other = swap_halves(value)
    return jnp.where(low, value, other) if half == 0 else jnp.where(low, other, value)


def stacked_rows(value):
    high = value.astype(BF16).astype(F32)
    return jnp.concatenate([high, value - high], axis=0).astype(BF16)


def times_doubled(value, matrix):
    count = value.shape[0]
    both = mm(stacked_rows(value), jnp.concatenate(split(matrix), axis=0))
    return both[:count] + both[count:]


def times_wide(value, wide):
    count, width = value.shape[0], wide.shape[1] // 2
    both = mm(stacked_rows(value), wide)
    return both[:count, :width] + both[count:, :width] + both[:count, width:]


def left_doubled(value):
    high, low = split(value)
    return jnp.concatenate([high, low], axis=1)


def block_diagonal(matrix):
    low = lane_low(matrix.shape)
    return jnp.concatenate([jnp.where(low, matrix, 0.0), jnp.where(low, 0.0, matrix)], axis=0)


def fetch(sources, targets, sems):
    copies = [pltpu.make_async_copy(a, b, sems.at[n]) for n, (a, b) in enumerate(zip(sources, targets))]
    for copy in copies:
        copy.start()
    for copy in copies:
        copy.wait()


def weights_kernel(
    u_hbm, scale_hbm, other_hbm, w_hbm, w3_ref, ws_ref, ut_ref, ud_ref, bias_ref, w_ref,
    u_ref, scale_ref, other_ref, sems,
):
    fetch((u_hbm, scale_hbm, other_hbm, w_hbm), (u_ref, scale_ref, other_ref, w_ref), sems)
    zero = jnp.zeros((H, H), F32)
    for g in range(3):
        block = u_ref[:, g * H : (g + 1) * H]
        ud_ref[g] = jnp.concatenate([block, block], axis=1)
        diag = jnp.concatenate(
            [jnp.concatenate([block, zero], axis=1), jnp.concatenate([zero, block], axis=1)], axis=0
        )
        at = slice(g * LANES, (g + 1) * LANES)
        high, low = split(diag)
        w3_ref[0:LANES, at] = high
        w3_ref[LANES : 2 * LANES, at] = high
        w3_ref[2 * LANES : 3 * LANES, at] = low
        ws_ref[0:LANES, at] = high
        ws_ref[LANES : 2 * LANES, at] = high
        ws_ref[2 * LANES : 3 * LANES, at] = low
        if g == 2:
            ws_ref[0:LANES, 3 * LANES :] = low
            ws_ref[LANES : 2 * LANES, 3 * LANES :] = low
            ws_ref[2 * LANES : 3 * LANES, 3 * LANES :] = low
        high, low = split(diag.T)
        ut_ref[at, :] = jnp.concatenate([high, low], axis=1)
    scale = scale_ref[...]
    rows = [jnp.log(scale), other_ref[0:1, :], other_ref[1:2, :], other_ref[2:3, :], scale]
    rows = [jnp.concatenate([row, row], axis=1) for row in rows]
    bias_ref[...] = jnp.concatenate(rows + [jnp.zeros((3, LANES), F32)], axis=0)


def pack_kernel(where_ref, x_hbm, cot_hbm, h_hbm, one_ref, two_ref, x_ref, cot_ref, h_ref, sems):
    fetch((x_hbm, cot_hbm, h_hbm), (x_ref, cot_ref, h_ref), sems)
    odd = where_ref[0]
    zero = jnp.zeros((H, H), F32)
    cots = []
    for e in range(2):
        cots.append(jnp.transpose(jnp.concatenate([cot_ref[:, e, :], zero], axis=1))[:H])
    for m, out_ref in enumerate((one_ref, two_ref)):
        first = odd == m
        x = jnp.where(first, x_ref[0].astype(F32), x_ref[1].astype(F32))
        out_ref[0:64, :] = x[:, :LANES]
        out_ref[64:128, :] = x[:, LANES:]
        cot = jnp.where(first, cots[0], cots[1])
        out_ref[128:160, :] = jnp.concatenate([cot[:32], cot[32:]], axis=1)
        start = jnp.where(first, h_ref[0:1, :], h_ref[1:2, :])
        start = jnp.concatenate([start, start], axis=1)
        out_ref[160:168, :] = jnp.broadcast_to(start, (8, LANES))


def coefficients(prev, x3, bias, w3):
    mixed = mm(left3(prev), w3)
    mz, mr, mn = mixed[:, :LANES], mixed[:, LANES : 2 * LANES], mixed[:, 2 * LANES :]
    update = jax.nn.sigmoid(x3[0] + mz)
    reset = jax.nn.sigmoid(x3[1] + mr)
    recur = mn + bias[3:4, :]
    cand = jnp.tanh(x3[2] + reset * recur)
    fresh = (1.0 - update) * cand + update * prev
    slope = (1.0 - update) * (1.0 - cand * cand)
    cz = (prev - cand) * update * (1.0 - update)
    cr = slope * recur * reset * (1.0 - reset)
    cn = slope * reset
    offset = fresh - (update * prev + cz * mz + cr * mr + cn * mn)
    return update, cz, cr, cn, slope, offset


def gate_products(rows, ws_ref):
    high, low = split(rows)
    pair = jnp.concatenate([high, low], axis=1)
    both = mm(jnp.concatenate([pair, high], axis=1), ws_ref[:, : 2 * LANES])
    last = mm(pair, ws_ref[: 2 * LANES, 2 * LANES :])
    return both[:, :LANES], both[:, LANES:], last[:, :LANES] + last[:, LANES:]


def scan_maps(coef, ws_ref, ud_ref, maps_ref):
    update, cz, cr, cn, _, offset = coef
    for j in range(STEPS):
        at = slice(j * CHUNKS, (j + 1) * CHUNKS)
        up_j, cz_j, cr_j, cn_j = (a[at][None] for a in (update, cz, cr, cn))
        for begin, end in zip(BLOCKS, BLOCKS[1:]):
            rows = slice(begin * CHUNKS, end * CHUNKS)
            last = end == COLS
            shape = (end - begin, CHUNKS, LANES)
            if j == 0:
                real = end - begin - 1 if last else end - begin
                cols = slice(begin, begin + real)
                k = lax.broadcasted_iota(jnp.int32, (real, CHUNKS, LANES), 0) + begin
                lane = lax.broadcasted_iota(jnp.int32, (real, CHUNKS, LANES), 2) % H
                new = jnp.where(k == lane, up_j, 0.0)
                for c, g in ((cz_j, 0), (cr_j, 1), (cn_j, 2)):
                    new = new + c * ud_ref[g, cols, :][:, None, :]
                if last:
                    new = jnp.concatenate([new, offset[at][None]], axis=0)
            else:
                old = maps_ref[j - 1, rows, :]
                mz, mr, mn = (part.reshape(shape) for part in gate_products(old, ws_ref))
                new = up_j * old.reshape(shape) + cz_j * mz + cr_j * mr + cn_j * mn
                if last:
                    new = jnp.concatenate([new[:-1], new[-1:] + offset[at][None]], axis=0)
            maps_ref[j, rows, :] = new.reshape((end - begin) * CHUNKS, LANES)


def chunk_matrix(maps_ref, c):
    return maps_ref[STEPS - 1, pl.ds(c, H, stride=CHUNKS), :]


def chunk_vector(maps_ref, c):
    return maps_ref[STEPS - 1, H * CHUNKS + c : H * CHUNKS + c + 1, :]


def compose(earlier, later):
    row = lax.broadcasted_iota(jnp.int32, (72, LANES), 0)
    both = times_wide(earlier, jnp.concatenate(split(block_diagonal(later[:H])), axis=1))
    return both + jnp.where(row == H, later[H : H + 1], 0.0)


def chunk_levels(maps_ref):
    pad = jnp.zeros((7, LANES), F32)
    levels = [[
        jnp.concatenate([chunk_matrix(maps_ref, c), chunk_vector(maps_ref, c), pad], axis=0) for c in range(CHUNKS)
    ]]
    while len(levels[-1]) > 1:
        parts = levels[-1]
        levels.append([compose(a, b) for a, b in zip(parts[::2], parts[1::2])])
    return levels


def flip_halves(matrix):
    turned = jnp.transpose(matrix)
    return jnp.concatenate([turned[:H], turned[H:]], axis=1)


def diagonal(rows):
    row = lax.broadcasted_iota(jnp.int32, (H, LANES), 0)
    lane = lax.broadcasted_iota(jnp.int32, (H, LANES), 1) % H
    return jnp.where(row == lane, rows, 0.0)


def to_column(row, matrix, vector):
    low = lane_low(matrix.shape)
    prod = matrix * row + diagonal(vector)
    first = jnp.sum(jnp.where(low, prod, 0.0), axis=1, keepdims=True)
    second = jnp.sum(jnp.where(low, 0.0, prod), axis=1, keepdims=True)
    return jnp.where(low, first, second)


def to_row(column, matrix, vector):
    return jnp.sum(column * matrix, axis=0, keepdims=True) + vector


def as_row(column):
    return jnp.sum(diagonal(column), axis=0, keepdims=True)


def join_halves(total):
    row = lax.broadcasted_iota(jnp.int32, (72, LANES), 0)
    second = doubled(total, 1)
    both = times_doubled(doubled(total, 0), second[:H])
    return both + jnp.where(row == H, second, 0.0)


def send_map(total, flipped, where_ref, out_ref):
    low = lane_low((H // 2, LANES))
    matrix = jnp.where(where_ref[1] == 0, flipped, total[:H])
    packed = jnp.where(low, matrix[: H // 2], matrix[H // 2 :])
    for z in range(out_ref.shape[0]):
        out_ref[z, : H // 2, :] = packed
        out_ref[z, H // 2 :, :] = total[H:]


def flip(matrix):
    square = jnp.transpose(matrix)[:H]
    return jnp.concatenate([square, square], axis=1)


def unpack_map(packed, whole):
    body = packed[: H // 2]
    other = swap_halves(body)
    low = lane_low(body.shape)
    if whole:
        parts = [jnp.where(low, body, other), jnp.where(low, other, body)]
    else:
        parts = [jnp.where(low, body, 0.0), jnp.where(low, other, 0.0)]
    return jnp.concatenate(parts, axis=0), packed[H // 2 : H // 2 + 1]


def apply_row(state, matrix, vector):
    return times_doubled(state, matrix) + vector


def enter_device(where_ref, own_ref, other_ref, start, reverse):
    core, mine = where_ref[1], where_ref[2]
    planes = own_ref.shape[0]
    row = lax.broadcasted_iota(jnp.int32, (H, LANES), 0)
    lane = lax.broadcasted_iota(jnp.int32, (H, LANES), 1)
    eye = jnp.where(row == lane, 1.0, 0.0)
    eyes = jnp.where(row == lane % H, 1.0, 0.0)
    state = start[0:1]
    order = list(range(2 * planes))
    for n in reversed(order) if reverse else order:
        z, kappa = n // 2, n % 2
        reached = (mine < n) if reverse else (mine > n)
        packed = jnp.where(core == kappa, own_ref[z], other_ref[z])
        to_column = kappa == (1 if reverse else 0)
        matrix, vector = unpack_map(packed, not to_column)
        vector = jnp.where(reached, vector, 0.0)
        if to_column:
            matrix = jnp.where(reached, matrix, eye)
            summed = jnp.sum(matrix * state + eye * vector, axis=1, keepdims=True)
            state = jnp.broadcast_to(summed, (H, LANES))
        else:
            matrix = jnp.where(reached, matrix, eyes)
            state = jnp.sum(matrix * state, axis=0, keepdims=True) + vector
    return jnp.broadcast_to(state, (CHUNKS, LANES))


def spread(rows, count):
    k = lax.broadcasted_iota(jnp.int32, (count,) + rows.shape, 0)
    lane = lax.broadcasted_iota(jnp.int32, (count,) + rows.shape, 2) % H
    picked = jnp.where(k == lane, rows[None], 0.0).reshape(count * rows.shape[0], LANES)
    one = (
        lax.broadcasted_iota(jnp.int32, (LANES, LANES), 0) // H
        == lax.broadcasted_iota(jnp.int32, (LANES, LANES), 1) // H
    )
    one = jnp.where(one, 1.0, 0.0).astype(BF16)
    high, low = split(picked)
    rest = (picked - high.astype(F32) - low.astype(F32)).astype(BF16)
    return mm(jnp.concatenate([high, low, rest], axis=1), jnp.concatenate([one, one, one], axis=0))


def store_chunks(levels, chunk_ref, vector_ref):
    ones, twos, fours, _ = levels
    parts = (ones[0], twos[0], fours[0], ones[6], ones[2], ones[4], twos[2])
    for n, part in enumerate(parts):
        chunk_ref[n] = flip_halves(part[:H]) if n < 4 else part[:H]
        vector_ref[n : n + 1, :] = part[H : H + 1]


def enter_chunks(state, chunk_ref, vector_ref, ends_ref):
    low = lane_low((CHUNKS, LANES))
    first = doubled(ends_ref[...], 0)
    middle = apply_row(state, first[:H], first[H : H + 1])
    entering = jnp.where(low, state, middle)
    vectors = vector_ref[...]
    row = entering[0:1]
    one, two, four = (to_column(row, chunk_ref[n], vectors[n : n + 1]) for n in range(3))
    three = to_row(two, chunk_ref[4], vectors[4:5])
    five = to_row(four, chunk_ref[5], vectors[5:6])
    six = to_row(four, chunk_ref[6], vectors[6:7])
    seven = to_column(six, chunk_ref[3], vectors[3:4])
    rows = [row, as_row(one), as_row(two), three, as_row(four), five, six, as_row(seven)]
    return jnp.concatenate(rows, axis=0)


def trajectory(entering, maps_ref, spread_ref):
    spread_ref[...] = spread(entering, H)
    states = [maps_ref[j, H * CHUNKS :, :] for j in range(STEPS)]
    for b in range(0, H * CHUNKS, 64):
        factor = spread_ref[b : b + 64, :].reshape(8, CHUNKS, LANES)
        for j in range(STEPS):
            block = maps_ref[j, b : b + 64, :].reshape(8, CHUNKS, LANES)
            states[j] = states[j] + jnp.sum(block * factor, axis=0)
    return states


def phase(where_ref, prev, x3_ref, bias_ref, w3_ref, ws_ref, ud_ref, maps_ref, chunk_ref, vector_ref, ends_ref, out_ref):
    coef = coefficients(prev, x3_ref, bias_ref[...], w3_ref[...])
    scan_maps(coef, ws_ref, ud_ref, maps_ref)
    levels = chunk_levels(maps_ref)
    store_chunks(levels, chunk_ref, vector_ref)
    total = levels[-1][0]
    ends_ref[...] = total
    total = join_halves(total)
    send_map(total, flip(total[:H]), where_ref, out_ref)


def first_kernel(
    where_ref, a_ref, b_ref, w_ref, w3_ref, ws_ref, ud_ref, bias_ref,
    x3_ref, xin_ref, cot_ref, start_ref, maps_ref, chunk_ref, vector_ref, ends_ref, out_ref, natural_ref,
):
    odd, mine = where_ref[0], where_ref[2]
    pieces = []
    for v in range(2):
        for j in range(STEPS):
            rows = [
                jnp.where(odd == v, a_ref[pl.ds(o + j, 8, stride=8), :], b_ref[pl.ds(o + j, 8, stride=8), :])
                for o in (0, 64)
            ]
            pieces.append(jnp.concatenate(rows, axis=1))
    xin = jnp.concatenate(pieces, axis=0).astype(BF16)
    xin_ref[...] = xin
    cots = [jnp.where(odd == v, a_ref[128:160, :], b_ref[128:160, :]) for v in range(2)]
    low = lane_low((32, LANES))
    natural_ref[0:32, :] = jnp.where(low, cots[0], swap_halves(cots[1]))
    natural_ref[32:64, :] = jnp.where(low, swap_halves(cots[0]), cots[1])
    cot_ref[...] = jnp.concatenate([natural_ref[pl.ds(j, 8, stride=8), :] for j in range(STEPS)], axis=0)
    start = a_ref[160:168, :]
    start_ref[...] = start
    flat = mm_nt(xin, w_ref[...])
    bias = bias_ref[...]
    for g in range(3):
        cols = slice(g * H, (g + 1) * H)
        x3_ref[g] = jnp.concatenate([flat[:64, cols], flat[64:, cols]], axis=1) + bias[g : g + 1, :]
    row = lax.broadcasted_iota(jnp.int32, (64, LANES), 0)
    lane = lax.broadcasted_iota(jnp.int32, (64, LANES), 1)
    here = (row == 0) & (lane < H) & (mine == 0)
    prev = jnp.where(here, start[0:1, :], 0.0)
    phase(where_ref, prev, x3_ref, bias_ref, w3_ref, ws_ref, ud_ref, maps_ref, chunk_ref, vector_ref, ends_ref, out_ref)


def next_kernel(
    where_ref, own_ref, other_ref, start_ref, x3_ref, bias_ref, w3_ref, ws_ref, ud_ref, old_ref, pieces_ref, rows_ref, before_ref,
    maps_ref, chunk_ref, vector_ref, ends_ref, out_ref, spread_ref,
):
    state = enter_device(where_ref, own_ref, other_ref, start_ref[...], False)
    entering = enter_chunks(state, pieces_ref, rows_ref, before_ref)
    states = trajectory(entering, old_ref, spread_ref)
    prev = jnp.concatenate([entering] + states[:-1], axis=0)
    phase(where_ref, prev, x3_ref, bias_ref, w3_ref, ws_ref, ud_ref, maps_ref, chunk_ref, vector_ref, ends_ref, out_ref)


def half_sums(value):
    row = lax.broadcasted_iota(jnp.int32, (8, LANES), 0)
    low = lane_low((8, LANES))
    pick = jnp.where((row == 0) & low, 1.0, 0.0) + jnp.where((row == 1) & ~low, 1.0, 0.0)
    pick = pick.astype(BF16)
    return mm_nt(jnp.concatenate([pick, pick], axis=1), left_doubled(value))


def turn_kernel(
    where_ref, own_ref, other_ref, start_ref, x3_ref, bias_ref, w3_ref, ws_ref, ud_ref, old_ref, pieces_ref, rows_ref, before_ref, cot_ref,
    states_ref, coef_ref, chunk_ref, vector_ref, half_ref, out_ref,
    spread_ref, maps_ref, acc_ref,
):
    state = enter_device(where_ref, own_ref, other_ref, start_ref[...], False)
    entering = enter_chunks(state, pieces_ref, rows_ref, before_ref)
    states = trajectory(entering, old_ref, spread_ref)
    for j in range(STEPS):
        states_ref[pl.ds(j, CHUNKS, stride=STEPS), :] = states[j]
    prev = jnp.concatenate([entering] + states[:-1], axis=0)
    coef = coefficients(prev, x3_ref, bias_ref[...], w3_ref[...])
    coef_ref[0] = prev
    for n in range(5):
        coef_ref[n + 1] = coef[n]
    scan_maps(coef, ws_ref, ud_ref, maps_ref)
    levels = chunk_levels(maps_ref)
    total = levels[-1][0]
    for b in range(0, H * CHUNKS, 64):
        acc = jnp.zeros((8, CHUNKS, LANES), F32)
        for j in range(STEPS):
            block = maps_ref[j, b : b + 64, :].reshape(8, CHUNKS, LANES)
            acc = acc + block * cot_ref[j * CHUNKS : (j + 1) * CHUNKS, :][None]
        acc_ref[b : b + 64, :] = acc.reshape(64, LANES)
    vectors = []
    for c in range(CHUNKS):
        sums = half_sums(acc_ref[pl.ds(c, H, stride=CHUNKS), :])
        vectors.append(jnp.concatenate([sums[0:1], sums[1:2]], axis=1))
    ones, twos, fours, _ = [[part[:H] for part in level] for level in levels]
    flip_23 = flip_halves(twos[1])
    pairs = [to_column(vectors[2 * n + 1], ones[2 * n], vectors[2 * n]) for n in range(4)]
    pair_rows = [as_row(pair) for pair in pairs]
    quad_low = to_row(pairs[1], flip_halves(twos[0]), pair_rows[0])
    quad_high = to_row(pairs[3], flip_halves(twos[2]), pair_rows[2])
    ends = as_row(to_column(quad_high, fours[0], quad_low))
    matrices = (fours[1], twos[3], ones[7], flip_23, flip_halves(ones[5]), flip_halves(ones[3]), ones[1])
    rows = (quad_high, pair_rows[3], vectors[7], pair_rows[1], vectors[5], vectors[3], vectors[1])
    for n, (matrix, vector) in enumerate(zip(matrices, rows)):
        chunk_ref[n] = matrix
        vector_ref[n : n + 1, :] = vector
    tail = doubled(ends, 1)
    low = lane_low((H, LANES))
    sums = half_sums(jnp.where(low, total[:H], 0.0) * tail)
    left = ends[:, :H] + sums[0:1]
    both = join_halves(total)
    pad = jnp.zeros((7, LANES), F32)
    left = jnp.concatenate([left, left], axis=1)
    send_map(jnp.concatenate([both[:H], left, pad], axis=0), flip(both[:H]), where_ref, out_ref)
    half_ref[...] = jnp.concatenate([flip(doubled(total[:H], 1)), tail, pad], axis=0)


def gradient_kernel(
    where_ref, own_ref, other_ref, coef_ref, chunk_ref, vector_ref, half_ref, cot_ref, ut_ref,
    xin_ref, bias_ref, states_ref, across_ref, keep_ref, give_ref, home_ref, full_ref,
):
    low = lane_low((CHUNKS, LANES))
    right = enter_device(where_ref, own_ref, other_ref, jnp.zeros((CHUNKS, LANES), F32), True)
    half = half_ref[...]
    middle = apply_row(right, half[:H], half[H : H + 1])
    last = jnp.where(low, middle, right)[0:1]
    vectors = vector_ref[...]
    three, five, six = (to_column(last, chunk_ref[n], vectors[n : n + 1]) for n in range(3))
    one = to_row(three, chunk_ref[3], vectors[3:4])
    four = to_row(five, chunk_ref[4], vectors[4:5])
    two = to_row(three, chunk_ref[5], vectors[5:6])
    zero = to_column(one, chunk_ref[6], vectors[6:7])
    passed = jnp.concatenate(
        [as_row(zero), one, two, as_row(three), four, as_row(five), as_row(six), last], axis=0
    )
    dz, dr, dn, ds = [None] * STEPS, [None] * STEPS, [None] * STEPS, [None] * STEPS
    for j in reversed(range(STEPS)):
        at = slice(j * CHUNKS, (j + 1) * CHUNKS)
        lam = cot_ref[at, :] + passed
        dz[j], dr[j], dn[j] = coef_ref[2, at, :] * lam, coef_ref[3, at, :] * lam, coef_ref[4, at, :] * lam
        ds[j] = coef_ref[5, at, :] * lam
        if j > 0:
            pulled = times_wide(jnp.concatenate([dz[j], dr[j], dn[j]], axis=1), ut_ref[...])
            passed = coef_ref[1, at, :] * lam + pulled
    dz, dr, dn, ds = (jnp.concatenate(part, axis=0) for part in (dz, dr, dn, ds))

    def stacked(value):
        return jnp.concatenate([value[:, :H], value[:, H:]], axis=0)

    sz, sr, sn, ss = (stacked(part) for part in (dz, dr, dn, ds))
    zero = jnp.zeros((2 * 64, H), F32)
    high, low_part = split(jnp.concatenate([sz, sr, ss, zero], axis=1))
    xin = xin_ref[...]
    grad_in = mm_tn(jnp.concatenate([high, low_part], axis=0), jnp.concatenate([xin, xin], axis=0))
    high, low_part = split(jnp.concatenate([sz, sr, sn, zero], axis=1))
    prev_high, prev_low = split(stacked(coef_ref[0]))
    grad_rec = mm_tn(
        jnp.concatenate([prev_high, prev_low, prev_high], axis=0),
        jnp.concatenate([high, high, low_part], axis=0),
    )
    full_ref[0:192, :] = grad_in[:192, :LANES]
    full_ref[192:384, :] = grad_in[:192, LANES:]
    full_ref[384:448, :] = grad_rec[:, :LANES]
    rest = grad_rec[:, LANES:]
    full_ref[448:480, :] = jnp.concatenate([rest[:32, :H], rest[32:, :H]], axis=1)
    sums = [jnp.sum(part, axis=0, keepdims=True) for part in (sz, sr, ss, sn)]
    scale = sums[0] / bias_ref[4:5, :H]
    tail = jnp.concatenate(
        [jnp.concatenate([scale, sums[1]], axis=1), jnp.concatenate([sums[2], sums[3]], axis=1)], axis=0
    )
    full_ref[480:512, :] = jnp.concatenate([tail, jnp.zeros((30, LANES), F32)], axis=0)
    core, x = where_ref[1], where_ref[3]
    for d in range(4):
        part = lax.rem(x + d, 4)
        rows = slice(d * 64, (d + 1) * 64)
        keep_ref[rows, :] = full_ref[pl.ds(pl.multiple_of((core * 4 + part) * 64, 64), 64), :]
        give_ref[rows, :] = full_ref[pl.ds(pl.multiple_of(((1 - core) * 4 + part) * 64, 64), 64), :]
    for d in range(4):
        part = lax.rem(x + d, 4)
        whole = jnp.where(part // 2 == core, states_ref[...], across_ref[...])
        block = jnp.where(lax.rem(part, 2) == 0, whole, swap_halves(whole))
        home_ref[d] = jnp.where(lane_low((32, LANES)), block[:32], swap_halves(block[32:]))


def home_kernel(where_ref, home_ref, two_ref, one_ref, three_ref, traj_ref):
    core, x = where_ref[1], where_ref[3]
    blocks = [home_ref[0]] + [ref[64:96, :] for ref in (one_ref, two_ref, three_ref)]
    for e in range(2):
        where = lax.rem(x + 4 - 2 * core - e, 4)
        block = blocks[0]
        for d in range(1, 4):
            block = jnp.where(where == d, blocks[d], block)
        block = jnp.concatenate([block, swap_halves(block)], axis=0)
        traj_ref[:, e, :] = jnp.transpose(block)[:H]


def unpack_kernel(
    where_ref, three_ref, one_ref, two_ref, both_ref, in_ref, rec_ref, scale_ref, bias_ref, full_ref
):
    x = where_ref[3]
    pieces = (both_ref, one_ref, two_ref, three_ref)
    for d in range(4):
        part = lax.rem(x + 4 - d, 4)
        for core in range(2):
            full_ref[pl.ds(pl.multiple_of((core * 4 + part) * 64, 64), 64), :] = pieces[d][core]
    in_ref[:, :LANES] = full_ref[0:192, :]
    in_ref[:, LANES:] = full_ref[192:384, :]
    rec_ref[:, :LANES] = full_ref[384:448, :]
    rec_ref[0:32, LANES:] = full_ref[448:480, :H]
    rec_ref[32:, LANES:] = full_ref[448:480, H:]
    one, two = full_ref[480:481, :], full_ref[481:482, :]
    scale_ref[...] = one[:, :H]
    bias_ref[...] = jnp.concatenate([one[:, H:], two[:, :H], two[:, H:]], axis=0)


def call(kernel, outs, kinds, *operands, scratch=()):
    spaces = {"s": SMEM, "v": VMEM, "h": pltpu.HBM}
    specs = [pl.BlockSpec(memory_space=spaces[kind]) for kind in kinds]
    operands = [
        pltpu.with_memory_space_constraint(operand, pltpu.HBM) if kind == "h" else operand
        for kind, operand in zip(kinds, operands)
    ]
    return pl.pallas_call(
        kernel,
        out_shape=[jax.ShapeDtypeStruct(*out) for out in outs],
        in_specs=specs,
        out_specs=[pl.BlockSpec(memory_space=VMEM)] * len(outs),
        scratch_shapes=list(scratch),
        compiler_params=pltpu.CompilerParams(vmem_limit_bytes=16 * 1024 * 1024),
    )(*operands)


def local(planes, width, ys, inputs, w_in, u_rec, timescale, other_bias, h_init, cotangent):
    place, part = lax.axis_index("seq"), lax.axis_index("batch")
    z, x, core = place // width, place % width, part % 2
    where = jnp.stack([x % 2, core, z * 2 + core, x]).astype(jnp.int32)

    def at(z, x, y, core):
        return (z * width + x) * (2 * ys) + y * 2 + core

    there = []
    for m in range(2):
        pairs = [
            (at(z, x, y, c), at(z, 2 * c + ((x % 2) ^ m), y, x // 2))
            for z in range(planes) for x in range(width) for y in range(ys) for c in range(2)
        ]
        there.append(pairs)
    step_x = {
        d: [(z * width + x, z * width + (x + d) % width) for z in range(planes) for x in range(width)]
        for d in range(1, width)
    }
    along_z = [[z * width + x for z in range(planes)] for x in range(width)]
    step_y = {d: [(b, (b + 2 * d) % (2 * ys)) for b in range(2 * ys)] for d in range(1, ys)}
    cores = [(b, b ^ 1) for b in range(2 * ys)]
    axes = ("seq", "batch")

    def exchange(value):
        own = lax.all_to_all(value, "seq", 0, 0, axis_index_groups=along_z, tiled=True)
        return own, lax.ppermute(own, "batch", cores)

    sems = pltpu.SemaphoreType.DMA((4,))
    one, two = call(
        pack_kernel, [((PART, LANES), F32)] * 2, "shhh", where, inputs, cotangent, h_init.T,
        scratch=[
            pltpu.VMEM(inputs.shape, BF16), pltpu.VMEM(cotangent.shape, F32), pltpu.VMEM((2, H), F32), sems
        ],
    )
    one = lax.ppermute(one, axes, there[0])
    two = lax.ppermute(two, axes, there[1])
    w3, ws, ut, ud, bias, w = call(
        weights_kernel,
        [
            ((384, 384), BF16), ((384, 512), BF16), ((384, 2 * LANES), BF16),
            ((3, H, LANES), F32), ((8, LANES), F32), ((192, 256), BF16),
        ],
        "hhhh", u_rec, timescale[None, :], other_bias, w_in.T,
        scratch=[pltpu.VMEM((H, 192), F32), pltpu.VMEM((1, H), F32), pltpu.VMEM((3, H), F32), sems],
    )
    maps_t, chunk_t = ((STEPS, ROWS, LANES), F32), ((CHUNKS, H, LANES), F32)
    rows_t, ends_t, send_t = ((8, LANES), F32), ((72, LANES), F32), ((planes, MAP, LANES), F32)
    x3, xin, cot, start, maps, chunk, vector, ends, send = call(
        first_kernel,
        [((3, 64, LANES), F32), ((128, 256), BF16), ((64, LANES), F32), ((8, LANES), F32), maps_t, chunk_t, rows_t, ends_t, send_t],
        "svvvvvvv", where, one, two, w, w3, ws, ud, bias,
        scratch=[pltpu.VMEM((64, LANES), F32)],
    )
    spread_s = pltpu.VMEM((H * CHUNKS, LANES), F32)
    for _ in range(NEWTON - 1):
        own, other = exchange(send)
        maps, chunk, vector, ends, send = call(
            next_kernel, [maps_t, chunk_t, rows_t, ends_t, send_t], "svvvvvvvvvvvv",
            where, own, other, start, x3, bias, w3, ws, ud, maps, chunk, vector, ends, scratch=[spread_s],
        )
    own, other = exchange(send)
    states, coef, chunk, vector, half, send = call(
        turn_kernel,
        [
            ((64, LANES), F32), ((6, 64, LANES), F32), chunk_t,
            ((8, LANES), F32), ((72, LANES), F32), send_t,
        ],
        "svvvvvvvvvvvvv", where, own, other, start, x3, bias, w3, ws, ud, maps, chunk, vector, ends, cot,
        scratch=[
            spread_s, pltpu.VMEM(*maps_t),
            pltpu.VMEM((H * CHUNKS, LANES), F32),
        ],
    )
    across = lax.ppermute(states, "batch", cores)
    own, other = exchange(send)
    keep, give, home = call(
        gradient_kernel, [((256, LANES), F32), ((256, LANES), F32), ((4, 32, LANES), F32)], "svvvvvvvvvvvv",
        where, own, other, coef, chunk, vector, half, cot, ut, xin, bias, states, across,
        scratch=[pltpu.VMEM((512, LANES), F32)],
    )

    def around(value_of, axis, steps, order):
        got = {d: lax.ppermute(value_of(d), axis, steps[d]) for d in order}
        return [got[d] for d in order]

    parts = (keep + lax.ppermute(give, "batch", cores)).reshape(width, -1, LANES)
    early = around(lambda d: jnp.concatenate([parts[d], home[d]], axis=0), "seq", step_x, (2, 1, 3))
    part = parts[0] + sum(piece[:64] for piece in early)
    part = part + sum(around(lambda d: part, "batch", step_y, (3, 1, 2)))
    wide = jnp.broadcast_to(part[None], (planes,) + part.shape)
    part = lax.all_to_all(wide, "seq", 0, 0, axis_index_groups=along_z, tiled=True).sum(0)
    other = lax.ppermute(part, "batch", cores)
    first = core == 0
    both = jnp.stack([jnp.where(first, part, other), jnp.where(first, other, part)])
    rest = around(lambda d: both, "seq", step_x, (3, 1, 2))
    (traj,) = call(home_kernel, [((H, 2, 64), F32)], "svvvv", where, home, *early)
    grad_in, grad_rec, grad_scale, grad_other = call(
        unpack_kernel,
        [((192, 256), F32), ((H, 192), F32), ((1, H), F32), ((3, H), F32)], "svvvv",
        where, *rest, both, scratch=[pltpu.VMEM((512, LANES), F32)],
    )
    return traj, grad_in.T, grad_rec, grad_scale[0], grad_other


def solution(mesh):
    width = 4
    planes = mesh.shape["seq"] // width
    ys = mesh.shape["batch"] // 2
    return jax.shard_map(
        functools.partial(local, planes, width, ys),
        mesh=mesh,
        in_specs=(P("batch", "seq", None), P(), P(), P(), P(), P(None, "batch"), P(None, "batch", "seq")),
        out_specs=(P(None, "batch", "seq"), P(), P(), P(), P()),
        check_vma=False,
    )
```

```python
import functools

import jax
import jax.numpy as jnp
from jax import lax
from jax.experimental import pallas as pl
from jax.experimental.pallas import tpu as pltpu
from jax.sharding import PartitionSpec as P

NEWTON = 3
H = 64
LANES = 128
CHUNKS = 8
STEPS = 8
COLS = H + 1
ROWS = COLS * CHUNKS
BLOCKS = (0, 22, 44, 65)
MAP = 40
PART = 168
F32 = jnp.float32
BF16 = jnp.bfloat16
VMEM = pltpu.VMEM
SMEM = pltpu.SMEM


def split(value):
    high = value.astype(BF16)
    return high, (value - high.astype(F32)).astype(BF16)


def mm(left, right):
    return jnp.dot(left, right, preferred_element_type=F32)


def mm_nt(left, right):
    return lax.dot_general(left, right, (((1,), (1,)), ((), ())), preferred_element_type=F32)


def mm_tn(left, right):
    return lax.dot_general(left, right, (((0,), (0,)), ((), ())), preferred_element_type=F32)


def left3(value):
    high, low = split(value)
    return jnp.concatenate([high, low, high], axis=1)


def right3(value):
    high, low = split(value)
    return jnp.concatenate([high, high, low], axis=0)


def lane_low(shape):
    return lax.broadcasted_iota(jnp.int32, shape, 1) < H


def swap_halves(value):
    return pltpu.roll(value, H, axis=1)


def doubled(value, half):
    low = lane_low(value.shape)
    other = swap_halves(value)
    return jnp.where(low, value, other) if half == 0 else jnp.where(low, other, value)


def stacked_rows(value):
    high = value.astype(BF16).astype(F32)
    return jnp.concatenate([high, value - high], axis=0).astype(BF16)


def times_doubled(value, matrix):
    count = value.shape[0]
    both = mm(stacked_rows(value), jnp.concatenate(split(matrix), axis=0))
    return both[:count] + both[count:]


def times_wide(value, wide):
    count, width = value.shape[0], wide.shape[1] // 2
    both = mm(stacked_rows(value), wide)
    return both[:count, :width] + both[count:, :width] + both[:count, width:]


def left_doubled(value):
    high, low = split(value)
    return jnp.concatenate([high, low], axis=1)


def block_diagonal(matrix):
    low = lane_low(matrix.shape)
    return jnp.concatenate([jnp.where(low, matrix, 0.0), jnp.where(low, 0.0, matrix)], axis=0)


def fetch(sources, targets, sems):
    copies = [pltpu.make_async_copy(a, b, sems.at[n]) for n, (a, b) in enumerate(zip(sources, targets))]
    for copy in copies:
        copy.start()
    for copy in copies:
        copy.wait()


def weights_kernel(
    u_hbm, scale_hbm, other_hbm, w_hbm, w3_ref, ws_ref, ut_ref, ud_ref, bias_ref, w_ref,
    u_ref, scale_ref, other_ref, sems,
):
    fetch((u_hbm, scale_hbm, other_hbm, w_hbm), (u_ref, scale_ref, other_ref, w_ref), sems)
    zero = jnp.zeros((H, H), F32)
    for g in range(3):
        block = u_ref[:, g * H : (g + 1) * H]
        ud_ref[g] = jnp.concatenate([block, block], axis=1)
        diag = jnp.concatenate(
            [jnp.concatenate([block, zero], axis=1), jnp.concatenate([zero, block], axis=1)], axis=0
        )
        at = slice(g * LANES, (g + 1) * LANES)
        high, low = split(diag)
        w3_ref[0:LANES, at] = high
        w3_ref[LANES : 2 * LANES, at] = high
        w3_ref[2 * LANES : 3 * LANES, at] = low
        ws_ref[0:LANES, at] = high
        ws_ref[LANES : 2 * LANES, at] = high
        ws_ref[2 * LANES : 3 * LANES, at] = low
        if g == 2:
            ws_ref[0:LANES, 3 * LANES :] = low
            ws_ref[LANES : 2 * LANES, 3 * LANES :] = low
            ws_ref[2 * LANES : 3 * LANES, 3 * LANES :] = low
        high, low = split(diag.T)
        ut_ref[at, :] = jnp.concatenate([high, low], axis=1)
    scale = scale_ref[...]
    rows = [jnp.log(scale), other_ref[0:1, :], other_ref[1:2, :], other_ref[2:3, :], scale]
    rows = [jnp.concatenate([row, row], axis=1) for row in rows]
    bias_ref[...] = jnp.concatenate(rows + [jnp.zeros((3, LANES), F32)], axis=0)


def pack_kernel(where_ref, x_hbm, cot_hbm, h_hbm, one_ref, two_ref, x_ref, cot_ref, h_ref, sems):
    fetch((x_hbm, cot_hbm, h_hbm), (x_ref, cot_ref, h_ref), sems)
    odd = where_ref[0]
    zero = jnp.zeros((H, H), F32)
    cots = []
    for e in range(2):
        cots.append(jnp.transpose(jnp.concatenate([cot_ref[:, e, :], zero], axis=1))[:H])
    for m, out_ref in enumerate((one_ref, two_ref)):
        first = odd == m
        x = jnp.where(first, x_ref[0].astype(F32), x_ref[1].astype(F32))
        out_ref[0:64, :] = x[:, :LANES]
        out_ref[64:128, :] = x[:, LANES:]
        cot = jnp.where(first, cots[0], cots[1])
        out_ref[128:160, :] = jnp.concatenate([cot[:32], cot[32:]], axis=1)
        start = jnp.where(first, h_ref[0:1, :], h_ref[1:2, :])
        start = jnp.concatenate([start, start], axis=1)
        out_ref[160:168, :] = jnp.broadcast_to(start, (8, LANES))


def coefficients(prev, x3, bias, w3):
    mixed = mm(left3(prev), w3)
    mz, mr, mn = mixed[:, :LANES], mixed[:, LANES : 2 * LANES], mixed[:, 2 * LANES :]
    update = jax.nn.sigmoid(x3[0] + mz)
    reset = jax.nn.sigmoid(x3[1] + mr)
    recur = mn + bias[3:4, :]
    cand = jnp.tanh(x3[2] + reset * recur)
    fresh = (1.0 - update) * cand + update * prev
    slope = (1.0 - update) * (1.0 - cand * cand)
    cz = (prev - cand) * update * (1.0 - update)
    cr = slope * recur * reset * (1.0 - reset)
    cn = slope * reset
    offset = fresh - (update * prev + cz * mz + cr * mr + cn * mn)
    return update, cz, cr, cn, slope, offset


def gate_products(rows, ws_ref):
    high, low = split(rows)
    pair = jnp.concatenate([high, low], axis=1)
    both = mm(jnp.concatenate([pair, high], axis=1), ws_ref[:, : 2 * LANES])
    last = mm(pair, ws_ref[: 2 * LANES, 2 * LANES :])
    return both[:, :LANES], both[:, LANES:], last[:, :LANES] + last[:, LANES:]


def scan_maps(coef, ws_ref, ud_ref, maps_ref):
    update, cz, cr, cn, _, offset = coef
    for j in range(STEPS):
        at = slice(j * CHUNKS, (j + 1) * CHUNKS)
        up_j, cz_j, cr_j, cn_j = (a[at][None] for a in (update, cz, cr, cn))
        for begin, end in zip(BLOCKS, BLOCKS[1:]):
            rows = slice(begin * CHUNKS, end * CHUNKS)
            last = end == COLS
            shape = (end - begin, CHUNKS, LANES)
            if j == 0:
                real = end - begin - 1 if last else end - begin
                cols = slice(begin, begin + real)
                k = lax.broadcasted_iota(jnp.int32, (real, CHUNKS, LANES), 0) + begin
                lane = lax.broadcasted_iota(jnp.int32, (real, CHUNKS, LANES), 2) % H
                new = jnp.where(k == lane, up_j, 0.0)
                for c, g in ((cz_j, 0), (cr_j, 1), (cn_j, 2)):
                    new = new + c * ud_ref[g, cols, :][:, None, :]
                if last:
                    new = jnp.concatenate([new, offset[at][None]], axis=0)
            else:
                old = maps_ref[j - 1, rows, :]
                mz, mr, mn = (part.reshape(shape) for part in gate_products(old, ws_ref))
                new = up_j * old.reshape(shape) + cz_j * mz + cr_j * mr + cn_j * mn
                if last:
                    new = jnp.concatenate([new[:-1], new[-1:] + offset[at][None]], axis=0)
            maps_ref[j, rows, :] = new.reshape((end - begin) * CHUNKS, LANES)


def chunk_matrix(maps_ref, c):
    return maps_ref[STEPS - 1, pl.ds(c, H, stride=CHUNKS), :]


def chunk_vector(maps_ref, c):
    return maps_ref[STEPS - 1, H * CHUNKS + c : H * CHUNKS + c + 1, :]


def compose(earlier, later):
    row = lax.broadcasted_iota(jnp.int32, (72, LANES), 0)
    both = times_wide(earlier, jnp.concatenate(split(block_diagonal(later[:H])), axis=1))
    return both + jnp.where(row == H, later[H : H + 1], 0.0)


def chunk_levels(maps_ref):
    pad = jnp.zeros((7, LANES), F32)
    levels = [[
        jnp.concatenate([chunk_matrix(maps_ref, c), chunk_vector(maps_ref, c), pad], axis=0) for c in range(CHUNKS)
    ]]
    while len(levels[-1]) > 1:
        parts = levels[-1]
        levels.append([compose(a, b) for a, b in zip(parts[::2], parts[1::2])])
    return levels


def flip_halves(matrix):
    turned = jnp.transpose(matrix)
    return jnp.concatenate([turned[:H], turned[H:]], axis=1)


def diagonal(rows):
    row = lax.broadcasted_iota(jnp.int32, (H, LANES), 0)
    lane = lax.broadcasted_iota(jnp.int32, (H, LANES), 1) % H
    return jnp.where(row == lane, rows, 0.0)


def to_column(row, matrix, vector):
    low = lane_low(matrix.shape)
    prod = matrix * row + diagonal(vector)
    first = jnp.sum(jnp.where(low, prod, 0.0), axis=1, keepdims=True)
    second = jnp.sum(jnp.where(low, 0.0, prod), axis=1, keepdims=True)
    return jnp.where(low, first, second)


def to_row(column, matrix, vector):
    return jnp.sum(column * matrix, axis=0, keepdims=True) + vector


def as_row(column):
    return jnp.sum(diagonal(column), axis=0, keepdims=True)


def join_halves(total):
    row = lax.broadcasted_iota(jnp.int32, (72, LANES), 0)
    second = doubled(total, 1)
    both = times_doubled(doubled(total, 0), second[:H])
    return both + jnp.where(row == H, second, 0.0)


def send_map(total, flipped, where_ref, out_ref):
    low = lane_low((H // 2, LANES))
    matrix = jnp.where(where_ref[1] == 0, flipped, total[:H])
    packed = jnp.where(low, matrix[: H // 2], matrix[H // 2 :])
    for z in range(out_ref.shape[0]):
        out_ref[z, : H // 2, :] = packed
        out_ref[z, H // 2 :, :] = total[H:]


def flip(matrix):
    square = jnp.transpose(matrix)[:H]
    return jnp.concatenate([square, square], axis=1)


def unpack_map(packed, whole):
    body = packed[: H // 2]
    other = swap_halves(body)
    low = lane_low(body.shape)
    if whole:
        parts = [jnp.where(low, body, other), jnp.where(low, other, body)]
    else:
        parts = [jnp.where(low, body, 0.0), jnp.where(low, other, 0.0)]
    return jnp.concatenate(parts, axis=0), packed[H // 2 : H // 2 + 1]


def apply_row(state, matrix, vector):
    return times_doubled(state, matrix) + vector


def enter_device(where_ref, own_ref, other_ref, start, reverse):
    core, mine = where_ref[1], where_ref[2]
    planes = own_ref.shape[0]
    row = lax.broadcasted_iota(jnp.int32, (H, LANES), 0)
    lane = lax.broadcasted_iota(jnp.int32, (H, LANES), 1)
    eye = jnp.where(row == lane, 1.0, 0.0)
    eyes = jnp.where(row == lane % H, 1.0, 0.0)
    state = start[0:1]
    order = list(range(2 * planes))
    for n in reversed(order) if reverse else order:
        z, kappa = n // 2, n % 2
        reached = (mine < n) if reverse else (mine > n)
        at = (z + planes // 2) % planes
        packed = jnp.where(core == kappa, own_ref[at], other_ref[at])
        to_column = kappa == (1 if reverse else 0)
        matrix, vector = unpack_map(packed, not to_column)
        vector = jnp.where(reached, vector, 0.0)
        if to_column:
            matrix = jnp.where(reached, matrix, eye)
            summed = jnp.sum(matrix * state + eye * vector, axis=1, keepdims=True)
            state = jnp.broadcast_to(summed, (H, LANES))
        else:
            matrix = jnp.where(reached, matrix, eyes)
            state = jnp.sum(matrix * state, axis=0, keepdims=True) + vector
    return jnp.broadcast_to(state, (CHUNKS, LANES))


def spread(rows, count):
    k = lax.broadcasted_iota(jnp.int32, (count,) + rows.shape, 0)
    lane = lax.broadcasted_iota(jnp.int32, (count,) + rows.shape, 2) % H
    picked = jnp.where(k == lane, rows[None], 0.0).reshape(count * rows.shape[0], LANES)
    one = (
        lax.broadcasted_iota(jnp.int32, (LANES, LANES), 0) // H
        == lax.broadcasted_iota(jnp.int32, (LANES, LANES), 1) // H
    )
    one = jnp.where(one, 1.0, 0.0).astype(BF16)
    high, low = split(picked)
    rest = (picked - high.astype(F32) - low.astype(F32)).astype(BF16)
    return mm(jnp.concatenate([high, low, rest], axis=1), jnp.concatenate([one, one, one], axis=0))


def store_chunks(levels, chunk_ref, vector_ref):
    ones, twos, fours, _ = levels
    parts = (ones[0], twos[0], fours[0], ones[6], ones[2], ones[4], twos[2])
    for n, part in enumerate(parts):
        chunk_ref[n] = flip_halves(part[:H]) if n < 4 else part[:H]
        vector_ref[n : n + 1, :] = part[H : H + 1]


def enter_chunks(state, chunk_ref, vector_ref, ends_ref):
    low = lane_low((CHUNKS, LANES))
    first = doubled(ends_ref[...], 0)
    middle = apply_row(state, first[:H], first[H : H + 1])
    entering = jnp.where(low, state, middle)
    vectors = vector_ref[...]
    row = entering[0:1]
    one, two, four = (to_column(row, chunk_ref[n], vectors[n : n + 1]) for n in range(3))
    three = to_row(two, chunk_ref[4], vectors[4:5])
    five = to_row(four, chunk_ref[5], vectors[5:6])
    six = to_row(four, chunk_ref[6], vectors[6:7])
    seven = to_column(six, chunk_ref[3], vectors[3:4])
    rows = [row, as_row(one), as_row(two), three, as_row(four), five, six, as_row(seven)]
    return jnp.concatenate(rows, axis=0)


def trajectory(entering, maps_ref, spread_ref):
    spread_ref[...] = spread(entering, H)
    states = [maps_ref[j, H * CHUNKS :, :] for j in range(STEPS)]
    for b in range(0, H * CHUNKS, 64):
        factor = spread_ref[b : b + 64, :].reshape(8, CHUNKS, LANES)
        for j in range(STEPS):
            block = maps_ref[j, b : b + 64, :].reshape(8, CHUNKS, LANES)
            states[j] = states[j] + jnp.sum(block * factor, axis=0)
    return states


def phase(where_ref, prev, x3_ref, bias_ref, w3_ref, ws_ref, ud_ref, maps_ref, chunk_ref, vector_ref, ends_ref, out_ref):
    coef = coefficients(prev, x3_ref, bias_ref[...], w3_ref[...])
    scan_maps(coef, ws_ref, ud_ref, maps_ref)
    levels = chunk_levels(maps_ref)
    store_chunks(levels, chunk_ref, vector_ref)
    total = levels[-1][0]
    ends_ref[...] = total
    total = join_halves(total)
    send_map(total, flip(total[:H]), where_ref, out_ref)


def first_kernel(
    where_ref, a_ref, b_ref, w_ref, w3_ref, ws_ref, ud_ref, bias_ref,
    x3_ref, xin_ref, cot_ref, start_ref, maps_ref, chunk_ref, vector_ref, ends_ref, out_ref, natural_ref,
):
    odd, mine = where_ref[0], where_ref[2]
    pieces = []
    for v in range(2):
        for j in range(STEPS):
            rows = [
                jnp.where(odd == v, a_ref[pl.ds(o + j, 8, stride=8), :], b_ref[pl.ds(o + j, 8, stride=8), :])
                for o in (0, 64)
            ]
            pieces.append(jnp.concatenate(rows, axis=1))
    xin = jnp.concatenate(pieces, axis=0).astype(BF16)
    xin_ref[...] = xin
    cots = [jnp.where(odd == v, a_ref[128:160, :], b_ref[128:160, :]) for v in range(2)]
    low = lane_low((32, LANES))
    natural_ref[0:32, :] = jnp.where(low, cots[0], swap_halves(cots[1]))
    natural_ref[32:64, :] = jnp.where(low, swap_halves(cots[0]), cots[1])
    cot_ref[...] = jnp.concatenate([natural_ref[pl.ds(j, 8, stride=8), :] for j in range(STEPS)], axis=0)
    start = a_ref[160:168, :]
    start_ref[...] = start
    flat = mm_nt(xin, w_ref[...])
    bias = bias_ref[...]
    for g in range(3):
        cols = slice(g * H, (g + 1) * H)
        x3_ref[g] = jnp.concatenate([flat[:64, cols], flat[64:, cols]], axis=1) + bias[g : g + 1, :]
    row = lax.broadcasted_iota(jnp.int32, (64, LANES), 0)
    lane = lax.broadcasted_iota(jnp.int32, (64, LANES), 1)
    here = (row == 0) & (lane < H) & (mine == 0)
    prev = jnp.where(here, start[0:1, :], 0.0)
    phase(where_ref, prev, x3_ref, bias_ref, w3_ref, ws_ref, ud_ref, maps_ref, chunk_ref, vector_ref, ends_ref, out_ref)


def next_kernel(
    where_ref, own_ref, other_ref, start_ref, x3_ref, bias_ref, w3_ref, ws_ref, ud_ref, old_ref, pieces_ref, rows_ref, before_ref,
    maps_ref, chunk_ref, vector_ref, ends_ref, out_ref, spread_ref,
):
    state = enter_device(where_ref, own_ref, other_ref, start_ref[...], False)
    entering = enter_chunks(state, pieces_ref, rows_ref, before_ref)
    states = trajectory(entering, old_ref, spread_ref)
    prev = jnp.concatenate([entering] + states[:-1], axis=0)
    phase(where_ref, prev, x3_ref, bias_ref, w3_ref, ws_ref, ud_ref, maps_ref, chunk_ref, vector_ref, ends_ref, out_ref)


def half_sums(value):
    row = lax.broadcasted_iota(jnp.int32, (8, LANES), 0)
    low = lane_low((8, LANES))
    pick = jnp.where((row == 0) & low, 1.0, 0.0) + jnp.where((row == 1) & ~low, 1.0, 0.0)
    pick = pick.astype(BF16)
    return mm_nt(jnp.concatenate([pick, pick], axis=1), left_doubled(value))


def turn_kernel(
    where_ref, own_ref, other_ref, start_ref, x3_ref, bias_ref, w3_ref, ws_ref, ud_ref, old_ref, pieces_ref, rows_ref, before_ref, cot_ref,
    states_ref, coef_ref, chunk_ref, vector_ref, half_ref, out_ref,
    spread_ref, maps_ref, acc_ref,
):
    state = enter_device(where_ref, own_ref, other_ref, start_ref[...], False)
    entering = enter_chunks(state, pieces_ref, rows_ref, before_ref)
    states = trajectory(entering, old_ref, spread_ref)
    for j in range(STEPS):
        states_ref[pl.ds(j, CHUNKS, stride=STEPS), :] = states[j]
    prev = jnp.concatenate([entering] + states[:-1], axis=0)
    coef = coefficients(prev, x3_ref, bias_ref[...], w3_ref[...])
    coef_ref[0] = prev
    for n in range(5):
        coef_ref[n + 1] = coef[n]
    scan_maps(coef, ws_ref, ud_ref, maps_ref)
    levels = chunk_levels(maps_ref)
    total = levels[-1][0]
    for b in range(0, H * CHUNKS, 64):
        acc = jnp.zeros((8, CHUNKS, LANES), F32)
        for j in range(STEPS):
            block = maps_ref[j, b : b + 64, :].reshape(8, CHUNKS, LANES)
            acc = acc + block * cot_ref[j * CHUNKS : (j + 1) * CHUNKS, :][None]
        acc_ref[b : b + 64, :] = acc.reshape(64, LANES)
    vectors = []
    for c in range(CHUNKS):
        sums = half_sums(acc_ref[pl.ds(c, H, stride=CHUNKS), :])
        vectors.append(jnp.concatenate([sums[0:1], sums[1:2]], axis=1))
    ones, twos, fours, _ = [[part[:H] for part in level] for level in levels]
    flip_23 = flip_halves(twos[1])
    pairs = [to_column(vectors[2 * n + 1], ones[2 * n], vectors[2 * n]) for n in range(4)]
    pair_rows = [as_row(pair) for pair in pairs]
    quad_low = to_row(pairs[1], flip_halves(twos[0]), pair_rows[0])
    quad_high = to_row(pairs[3], flip_halves(twos[2]), pair_rows[2])
    ends = as_row(to_column(quad_high, fours[0], quad_low))
    matrices = (fours[1], twos[3], ones[7], flip_23, flip_halves(ones[5]), flip_halves(ones[3]), ones[1])
    rows = (quad_high, pair_rows[3], vectors[7], pair_rows[1], vectors[5], vectors[3], vectors[1])
    for n, (matrix, vector) in enumerate(zip(matrices, rows)):
        chunk_ref[n] = matrix
        vector_ref[n : n + 1, :] = vector
    tail = doubled(ends, 1)
    low = lane_low((H, LANES))
    sums = half_sums(jnp.where(low, total[:H], 0.0) * tail)
    left = ends[:, :H] + sums[0:1]
    both = join_halves(total)
    pad = jnp.zeros((7, LANES), F32)
    left = jnp.concatenate([left, left], axis=1)
    send_map(jnp.concatenate([both[:H], left, pad], axis=0), flip(both[:H]), where_ref, out_ref)
    half_ref[...] = jnp.concatenate([flip(doubled(total[:H], 1)), tail, pad], axis=0)


def gradient_kernel(
    where_ref, own_ref, other_ref, coef_ref, chunk_ref, vector_ref, half_ref, cot_ref, ut_ref,
    xin_ref, bias_ref, states_ref, across_ref, keep_ref, give_ref, home_ref, full_ref,
):
    low = lane_low((CHUNKS, LANES))
    right = enter_device(where_ref, own_ref, other_ref, jnp.zeros((CHUNKS, LANES), F32), True)
    half = half_ref[...]
    middle = apply_row(right, half[:H], half[H : H + 1])
    last = jnp.where(low, middle, right)[0:1]
    vectors = vector_ref[...]
    three, five, six = (to_column(last, chunk_ref[n], vectors[n : n + 1]) for n in range(3))
    one = to_row(three, chunk_ref[3], vectors[3:4])
    four = to_row(five, chunk_ref[4], vectors[4:5])
    two = to_row(three, chunk_ref[5], vectors[5:6])
    zero = to_column(one, chunk_ref[6], vectors[6:7])
    passed = jnp.concatenate(
        [as_row(zero), one, two, as_row(three), four, as_row(five), as_row(six), last], axis=0
    )
    dz, dr, dn, ds = [None] * STEPS, [None] * STEPS, [None] * STEPS, [None] * STEPS
    for j in reversed(range(STEPS)):
        at = slice(j * CHUNKS, (j + 1) * CHUNKS)
        lam = cot_ref[at, :] + passed
        dz[j], dr[j], dn[j] = coef_ref[2, at, :] * lam, coef_ref[3, at, :] * lam, coef_ref[4, at, :] * lam
        ds[j] = coef_ref[5, at, :] * lam
        if j > 0:
            pulled = times_wide(jnp.concatenate([dz[j], dr[j], dn[j]], axis=1), ut_ref[...])
            passed = coef_ref[1, at, :] * lam + pulled
    dz, dr, dn, ds = (jnp.concatenate(part, axis=0) for part in (dz, dr, dn, ds))

    def stacked(value):
        return jnp.concatenate([value[:, :H], value[:, H:]], axis=0)

    sz, sr, sn, ss = (stacked(part) for part in (dz, dr, dn, ds))
    zero = jnp.zeros((2 * 64, H), F32)
    high, low_part = split(jnp.concatenate([sz, sr, ss, zero], axis=1))
    xin = xin_ref[...]
    grad_in = mm_tn(jnp.concatenate([high, low_part], axis=0), jnp.concatenate([xin, xin], axis=0))
    high, low_part = split(jnp.concatenate([sz, sr, sn, zero], axis=1))
    prev_high, prev_low = split(stacked(coef_ref[0]))
    grad_rec = mm_tn(
        jnp.concatenate([prev_high, prev_low, prev_high], axis=0),
        jnp.concatenate([high, high, low_part], axis=0),
    )
    full_ref[0:192, :] = grad_in[:192, :LANES]
    full_ref[192:384, :] = grad_in[:192, LANES:]
    full_ref[384:448, :] = grad_rec[:, :LANES]
    rest = grad_rec[:, LANES:]
    full_ref[448:480, :] = jnp.concatenate([rest[:32, :H], rest[32:, :H]], axis=1)
    sums = [jnp.sum(part, axis=0, keepdims=True) for part in (sz, sr, ss, sn)]
    scale = sums[0] / bias_ref[4:5, :H]
    tail = jnp.concatenate(
        [jnp.concatenate([scale, sums[1]], axis=1), jnp.concatenate([sums[2], sums[3]], axis=1)], axis=0
    )
    full_ref[480:512, :] = jnp.concatenate([tail, jnp.zeros((30, LANES), F32)], axis=0)
    core, x = where_ref[1], where_ref[3]
    for d in range(4):
        part = lax.rem(x + d, 4)
        rows = slice(d * 64, (d + 1) * 64)
        keep_ref[rows, :] = full_ref[pl.ds(pl.multiple_of((core * 4 + part) * 64, 64), 64), :]
        give_ref[rows, :] = full_ref[pl.ds(pl.multiple_of(((1 - core) * 4 + part) * 64, 64), 64), :]
    for d in range(4):
        part = lax.rem(x + d, 4)
        whole = jnp.where(part // 2 == core, states_ref[...], across_ref[...])
        block = jnp.where(lax.rem(part, 2) == 0, whole, swap_halves(whole))
        home_ref[d] = jnp.where(lane_low((32, LANES)), block[:32], swap_halves(block[32:]))


def home_kernel(where_ref, home_ref, two_ref, one_ref, three_ref, traj_ref):
    core, x = where_ref[1], where_ref[3]
    blocks = [home_ref[0]] + [ref[64:96, :] for ref in (one_ref, two_ref, three_ref)]
    for e in range(2):
        where = lax.rem(x + 4 - 2 * core - e, 4)
        block = blocks[0]
        for d in range(1, 4):
            block = jnp.where(where == d, blocks[d], block)
        block = jnp.concatenate([block, swap_halves(block)], axis=0)
        traj_ref[:, e, :] = jnp.transpose(block)[:H]


def unpack_kernel(
    where_ref, three_ref, one_ref, two_ref, both_ref, in_ref, rec_ref, scale_ref, bias_ref, full_ref
):
    x = where_ref[3]
    pieces = (both_ref, one_ref, two_ref, three_ref)
    for d in range(4):
        part = lax.rem(x + 4 - d, 4)
        for core in range(2):
            full_ref[pl.ds(pl.multiple_of((core * 4 + part) * 64, 64), 64), :] = pieces[d][core]
    in_ref[:, :LANES] = full_ref[0:192, :]
    in_ref[:, LANES:] = full_ref[192:384, :]
    rec_ref[:, :LANES] = full_ref[384:448, :]
    rec_ref[0:32, LANES:] = full_ref[448:480, :H]
    rec_ref[32:, LANES:] = full_ref[448:480, H:]
    one, two = full_ref[480:481, :], full_ref[481:482, :]
    scale_ref[...] = one[:, :H]
    bias_ref[...] = jnp.concatenate([one[:, H:], two[:, :H], two[:, H:]], axis=0)


def call(kernel, outs, kinds, *operands, scratch=()):
    spaces = {"s": SMEM, "v": VMEM, "h": pltpu.HBM}
    specs = [pl.BlockSpec(memory_space=spaces[kind]) for kind in kinds]
    operands = [
        pltpu.with_memory_space_constraint(operand, pltpu.HBM) if kind == "h" else operand
        for kind, operand in zip(kinds, operands)
    ]
    return pl.pallas_call(
        kernel,
        out_shape=[jax.ShapeDtypeStruct(*out) for out in outs],
        in_specs=specs,
        out_specs=[pl.BlockSpec(memory_space=VMEM)] * len(outs),
        scratch_shapes=list(scratch),
        compiler_params=pltpu.CompilerParams(vmem_limit_bytes=16 * 1024 * 1024),
    )(*operands)


def local(planes, width, ys, inputs, w_in, u_rec, timescale, other_bias, h_init, cotangent):
    place, part = lax.axis_index("seq"), lax.axis_index("batch")
    z, x, core = place // width, place % width, part % 2
    where = jnp.stack([x % 2, core, z * 2 + core, x]).astype(jnp.int32)

    def at(z, x, y, core):
        return (z * width + x) * (2 * ys) + y * 2 + core

    there = []
    for m in range(2):
        pairs = [
            (at(z, x, y, c), at(z, 2 * c + ((x % 2) ^ m), y, x // 2))
            for z in range(planes) for x in range(width) for y in range(ys) for c in range(2)
        ]
        there.append(pairs)
    step_x = {
        d: [(z * width + x, z * width + (x + d) % width) for z in range(planes) for x in range(width)]
        for d in range(1, width)
    }
    along_z = [[(z + planes // 2) % planes * width + x for z in range(planes)] for x in range(width)]
    step_y = {d: [(b, (b + 2 * d) % (2 * ys)) for b in range(2 * ys)] for d in range(1, ys)}
    cores = [(b, b ^ 1) for b in range(2 * ys)]
    axes = ("seq", "batch")

    def exchange(value):
        own = lax.all_to_all(value, "seq", 0, 0, axis_index_groups=along_z, tiled=True)
        return own, lax.ppermute(own, "batch", cores)

    sems = pltpu.SemaphoreType.DMA((4,))
    one, two = call(
        pack_kernel, [((PART, LANES), F32)] * 2, "shhh", where, inputs, cotangent, h_init.T,
        scratch=[
            pltpu.VMEM(inputs.shape, BF16), pltpu.VMEM(cotangent.shape, F32), pltpu.VMEM((2, H), F32), sems
        ],
    )
    one = lax.ppermute(one, axes, there[0])
    two = lax.ppermute(two, axes, there[1])
    w3, ws, ut, ud, bias, w = call(
        weights_kernel,
        [
            ((384, 384), BF16), ((384, 512), BF16), ((384, 2 * LANES), BF16),
            ((3, H, LANES), F32), ((8, LANES), F32), ((192, 256), BF16),
        ],
        "hhhh", u_rec, timescale[None, :], other_bias, w_in.T,
        scratch=[pltpu.VMEM((H, 192), F32), pltpu.VMEM((1, H), F32), pltpu.VMEM((3, H), F32), sems],
    )
    maps_t, chunk_t = ((STEPS, ROWS, LANES), F32), ((CHUNKS, H, LANES), F32)
    rows_t, ends_t, send_t = ((8, LANES), F32), ((72, LANES), F32), ((planes, MAP, LANES), F32)
    x3, xin, cot, start, maps, chunk, vector, ends, send = call(
        first_kernel,
        [((3, 64, LANES), F32), ((128, 256), BF16), ((64, LANES), F32), ((8, LANES), F32), maps_t, chunk_t, rows_t, ends_t, send_t],
        "svvvvvvv", where, one, two, w, w3, ws, ud, bias,
        scratch=[pltpu.VMEM((64, LANES), F32)],
    )
    spread_s = pltpu.VMEM((H * CHUNKS, LANES), F32)
    for _ in range(NEWTON - 1):
        own, other = exchange(send)
        maps, chunk, vector, ends, send = call(
            next_kernel, [maps_t, chunk_t, rows_t, ends_t, send_t], "svvvvvvvvvvvv",
            where, own, other, start, x3, bias, w3, ws, ud, maps, chunk, vector, ends, scratch=[spread_s],
        )
    own, other = exchange(send)
    states, coef, chunk, vector, half, send = call(
        turn_kernel,
        [
            ((64, LANES), F32), ((6, 64, LANES), F32), chunk_t,
            ((8, LANES), F32), ((72, LANES), F32), send_t,
        ],
        "svvvvvvvvvvvvv", where, own, other, start, x3, bias, w3, ws, ud, maps, chunk, vector, ends, cot,
        scratch=[
            spread_s, pltpu.VMEM(*maps_t),
            pltpu.VMEM((H * CHUNKS, LANES), F32),
        ],
    )
    across = lax.ppermute(states, "batch", cores)
    own, other = exchange(send)
    keep, give, home = call(
        gradient_kernel, [((256, LANES), F32), ((256, LANES), F32), ((4, 32, LANES), F32)], "svvvvvvvvvvvv",
        where, own, other, coef, chunk, vector, half, cot, ut, xin, bias, states, across,
        scratch=[pltpu.VMEM((512, LANES), F32)],
    )

    def around(value_of, axis, steps, order):
        got = {d: lax.ppermute(value_of(d), axis, steps[d]) for d in order}
        return [got[d] for d in order]

    parts = (keep + lax.ppermute(give, "batch", cores)).reshape(width, -1, LANES)
    early = around(lambda d: jnp.concatenate([parts[d], home[d]], axis=0), "seq", step_x, (2, 1, 3))
    part = parts[0] + sum(piece[:64] for piece in early)
    part = part + sum(around(lambda d: part, "batch", step_y, (3, 1, 2)))
    wide = jnp.broadcast_to(part[None], (planes,) + part.shape)
    part = lax.all_to_all(wide, "seq", 0, 0, axis_index_groups=along_z, tiled=True).sum(0)
    other = lax.ppermute(part, "batch", cores)
    first = core == 0
    both = jnp.stack([jnp.where(first, part, other), jnp.where(first, other, part)])
    rest = around(lambda d: both, "seq", step_x, (3, 1, 2))
    (traj,) = call(home_kernel, [((H, 2, 64), F32)], "svvvv", where, home, *early)
    grad_in, grad_rec, grad_scale, grad_other = call(
        unpack_kernel,
        [((192, 256), F32), ((H, 192), F32), ((1, H), F32), ((3, H), F32)], "svvvv",
        where, *rest, both, scratch=[pltpu.VMEM((512, LANES), F32)],
    )
    return traj, grad_in.T, grad_rec, grad_scale[0], grad_other


def solution(mesh):
    width = 4
    planes = mesh.shape["seq"] // width
    ys = mesh.shape["batch"] // 2
    return jax.shard_map(
        functools.partial(local, planes, width, ys),
        mesh=mesh,
        in_specs=(P("batch", "seq", None), P(), P(), P(), P(), P(None, "batch"), P(None, "batch", "seq")),
        out_specs=(P(None, "batch", "seq"), P(), P(), P(), P()),
        check_vma=False,
    )
```

```python
import functools

import jax
import jax.numpy as jnp
from jax import lax
from jax.experimental import pallas as pl
from jax.experimental.pallas import tpu as pltpu
from jax.sharding import PartitionSpec as P

NEWTON = 3
H = 64
LANES = 128
CHUNKS = 8
STEPS = 8
COLS = H + 1
ROWS = COLS * CHUNKS
BLOCKS = (0, 22, 44, 65)
MAP = 40
PART = 168
F32 = jnp.float32
BF16 = jnp.bfloat16
VMEM = pltpu.VMEM
SMEM = pltpu.SMEM


def split(value):
    high = value.astype(BF16)
    return high, (value - high.astype(F32)).astype(BF16)


def mm(left, right):
    return jnp.dot(left, right, preferred_element_type=F32)


def mm_nt(left, right):
    return lax.dot_general(left, right, (((1,), (1,)), ((), ())), preferred_element_type=F32)


def mm_tn(left, right):
    return lax.dot_general(left, right, (((0,), (0,)), ((), ())), preferred_element_type=F32)


def left3(value):
    high, low = split(value)
    return jnp.concatenate([high, low, high], axis=1)


def right3(value):
    high, low = split(value)
    return jnp.concatenate([high, high, low], axis=0)


def lane_low(shape):
    return lax.broadcasted_iota(jnp.int32, shape, 1) < H


def swap_halves(value):
    return pltpu.roll(value, H, axis=1)


def doubled(value, half):
    low = lane_low(value.shape)
    other = swap_halves(value)
    return jnp.where(low, value, other) if half == 0 else jnp.where(low, other, value)


def stacked_rows(value):
    high = value.astype(BF16).astype(F32)
    return jnp.concatenate([high, value - high], axis=0).astype(BF16)


def times_doubled(value, matrix):
    count = value.shape[0]
    both = mm(stacked_rows(value), jnp.concatenate(split(matrix), axis=0))
    return both[:count] + both[count:]


def times_wide(value, wide):
    count, width = value.shape[0], wide.shape[1] // 2
    both = mm(stacked_rows(value), wide)
    return both[:count, :width] + both[count:, :width] + both[:count, width:]


def left_doubled(value):
    high, low = split(value)
    return jnp.concatenate([high, low], axis=1)


def block_diagonal(matrix):
    low = lane_low(matrix.shape)
    return jnp.concatenate([jnp.where(low, matrix, 0.0), jnp.where(low, 0.0, matrix)], axis=0)


def fetch(sources, targets, sems):
    copies = [pltpu.make_async_copy(a, b, sems.at[n]) for n, (a, b) in enumerate(zip(sources, targets))]
    for copy in copies:
        copy.start()
    for copy in copies:
        copy.wait()


def weights_kernel(
    u_hbm, scale_hbm, other_hbm, w_hbm, w3_ref, ws_ref, ut_ref, ud_ref, bias_ref, w_ref,
    u_ref, scale_ref, other_ref, sems,
):
    fetch((u_hbm, scale_hbm, other_hbm, w_hbm), (u_ref, scale_ref, other_ref, w_ref), sems)
    zero = jnp.zeros((H, H), F32)
    for g in range(3):
        block = u_ref[:, g * H : (g + 1) * H]
        ud_ref[g] = jnp.concatenate([block, block], axis=1)
        diag = jnp.concatenate(
            [jnp.concatenate([block, zero], axis=1), jnp.concatenate([zero, block], axis=1)], axis=0
        )
        at = slice(g * LANES, (g + 1) * LANES)
        high, low = split(diag)
        w3_ref[0:LANES, at] = high
        w3_ref[LANES : 2 * LANES, at] = high
        w3_ref[2 * LANES : 3 * LANES, at] = low
        ws_ref[0:LANES, at] = high
        ws_ref[LANES : 2 * LANES, at] = high
        ws_ref[2 * LANES : 3 * LANES, at] = low
        if g == 2:
            ws_ref[0:LANES, 3 * LANES :] = low
            ws_ref[LANES : 2 * LANES, 3 * LANES :] = low
            ws_ref[2 * LANES : 3 * LANES, 3 * LANES :] = low
        high, low = split(diag.T)
        ut_ref[at, :] = jnp.concatenate([high, low], axis=1)
    scale = scale_ref[...]
    rows = [jnp.log(scale), other_ref[0:1, :], other_ref[1:2, :], other_ref[2:3, :], scale]
    rows = [jnp.concatenate([row, row], axis=1) for row in rows]
    bias_ref[...] = jnp.concatenate(rows + [jnp.zeros((3, LANES), F32)], axis=0)


def pack_kernel(where_ref, x_hbm, cot_hbm, h_hbm, one_ref, two_ref, x_ref, cot_ref, h_ref, sems):
    fetch((x_hbm, cot_hbm, h_hbm), (x_ref, cot_ref, h_ref), sems)
    odd = where_ref[0]
    zero = jnp.zeros((H, H), F32)
    cots = []
    for e in range(2):
        cots.append(jnp.transpose(jnp.concatenate([cot_ref[:, e, :], zero], axis=1))[:H])
    for m, out_ref in enumerate((one_ref, two_ref)):
        first = odd == m
        x = jnp.where(first, x_ref[0].astype(F32), x_ref[1].astype(F32))
        out_ref[0:64, :] = x[:, :LANES]
        out_ref[64:128, :] = x[:, LANES:]
        cot = jnp.where(first, cots[0], cots[1])
        out_ref[128:160, :] = jnp.concatenate([cot[:32], cot[32:]], axis=1)
        start = jnp.where(first, h_ref[0:1, :], h_ref[1:2, :])
        start = jnp.concatenate([start, start], axis=1)
        out_ref[160:168, :] = jnp.broadcast_to(start, (8, LANES))


def coefficients(prev, x3, bias, w3):
    mixed = mm(left3(prev), w3)
    mz, mr, mn = mixed[:, :LANES], mixed[:, LANES : 2 * LANES], mixed[:, 2 * LANES :]
    update = jax.nn.sigmoid(x3[0] + mz)
    reset = jax.nn.sigmoid(x3[1] + mr)
    recur = mn + bias[3:4, :]
    cand = jnp.tanh(x3[2] + reset * recur)
    fresh = (1.0 - update) * cand + update * prev
    slope = (1.0 - update) * (1.0 - cand * cand)
    cz = (prev - cand) * update * (1.0 - update)
    cr = slope * recur * reset * (1.0 - reset)
    cn = slope * reset
    offset = fresh - (update * prev + cz * mz + cr * mr + cn * mn)
    return update, cz, cr, cn, slope, offset


def gate_products(rows, ws_ref):
    high, low = split(rows)
    pair = jnp.concatenate([high, low], axis=1)
    both = mm(jnp.concatenate([pair, high], axis=1), ws_ref[:, : 2 * LANES])
    last = mm(pair, ws_ref[: 2 * LANES, 2 * LANES :])
    return both[:, :LANES], both[:, LANES:], last[:, :LANES] + last[:, LANES:]


def scan_maps(coef, ws_ref, ud_ref, maps_ref):
    update, cz, cr, cn, _, offset = coef
    for j in range(STEPS):
        at = slice(j * CHUNKS, (j + 1) * CHUNKS)
        up_j, cz_j, cr_j, cn_j = (a[at][None] for a in (update, cz, cr, cn))
        for begin, end in zip(BLOCKS, BLOCKS[1:]):
            rows = slice(begin * CHUNKS, end * CHUNKS)
            last = end == COLS
            shape = (end - begin, CHUNKS, LANES)
            if j == 0:
                real = end - begin - 1 if last else end - begin
                cols = slice(begin, begin + real)
                k = lax.broadcasted_iota(jnp.int32, (real, CHUNKS, LANES), 0) + begin
                lane = lax.broadcasted_iota(jnp.int32, (real, CHUNKS, LANES), 2) % H
                new = jnp.where(k == lane, up_j, 0.0)
                for c, g in ((cz_j, 0), (cr_j, 1), (cn_j, 2)):
                    new = new + c * ud_ref[g, cols, :][:, None, :]
                if last:
                    new = jnp.concatenate([new, offset[at][None]], axis=0)
            else:
                old = maps_ref[j - 1, rows, :]
                mz, mr, mn = (part.reshape(shape) for part in gate_products(old, ws_ref))
                new = up_j * old.reshape(shape) + cz_j * mz + cr_j * mr + cn_j * mn
                if last:
                    new = jnp.concatenate([new[:-1], new[-1:] + offset[at][None]], axis=0)
            maps_ref[j, rows, :] = new.reshape((end - begin) * CHUNKS, LANES)


def chunk_matrix(maps_ref, c):
    return maps_ref[STEPS - 1, pl.ds(c, H, stride=CHUNKS), :]


def chunk_vector(maps_ref, c):
    return maps_ref[STEPS - 1, H * CHUNKS + c : H * CHUNKS + c + 1, :]


def compose(earlier, later):
    row = lax.broadcasted_iota(jnp.int32, (72, LANES), 0)
    both = times_wide(earlier, jnp.concatenate(split(block_diagonal(later[:H])), axis=1))
    return both + jnp.where(row == H, later[H : H + 1], 0.0)


def chunk_levels(maps_ref):
    pad = jnp.zeros((7, LANES), F32)
    levels = [[
        jnp.concatenate([chunk_matrix(maps_ref, c), chunk_vector(maps_ref, c), pad], axis=0) for c in range(CHUNKS)
    ]]
    while len(levels[-1]) > 1:
        parts = levels[-1]
        levels.append([compose(a, b) for a, b in zip(parts[::2], parts[1::2])])
    return levels


def flip_halves(matrix):
    turned = jnp.transpose(matrix)
    return jnp.concatenate([turned[:H], turned[H:]], axis=1)


def diagonal(rows):
    row = lax.broadcasted_iota(jnp.int32, (H, LANES), 0)
    lane = lax.broadcasted_iota(jnp.int32, (H, LANES), 1) % H
    return jnp.where(row == lane, rows, 0.0)


def to_column(row, matrix, vector):
    low = lane_low(matrix.shape)
    prod = matrix * row + diagonal(vector)
    first = jnp.sum(jnp.where(low, prod, 0.0), axis=1, keepdims=True)
    second = jnp.sum(jnp.where(low, 0.0, prod), axis=1, keepdims=True)
    return jnp.where(low, first, second)


def to_row(column, matrix, vector):
    return jnp.sum(column * matrix, axis=0, keepdims=True) + vector


def as_row(column):
    return jnp.sum(diagonal(column), axis=0, keepdims=True)


def join_halves(total):
    row = lax.broadcasted_iota(jnp.int32, (72, LANES), 0)
    second = doubled(total, 1)
    both = times_doubled(doubled(total, 0), second[:H])
    return both + jnp.where(row == H, second, 0.0)


def send_map(total, flipped, where_ref, out_ref):
    low = lane_low((H // 2, LANES))
    matrix = jnp.where(where_ref[1] == 0, flipped, total[:H])
    packed = jnp.where(low, matrix[: H // 2], matrix[H // 2 :])
    for z in range(out_ref.shape[0]):
        out_ref[z, : H // 2, :] = packed
        out_ref[z, H // 2 :, :] = total[H:]


def flip(matrix):
    square = jnp.transpose(matrix)[:H]
    return jnp.concatenate([square, square], axis=1)


def unpack_map(packed, whole):
    body = packed[: H // 2]
    other = swap_halves(body)
    low = lane_low(body.shape)
    if whole:
        parts = [jnp.where(low, body, other), jnp.where(low, other, body)]
    else:
        parts = [jnp.where(low, body, 0.0), jnp.where(low, other, 0.0)]
    return jnp.concatenate(parts, axis=0), packed[H // 2 : H // 2 + 1]


def apply_row(state, matrix, vector):
    return times_doubled(state, matrix) + vector


def enter_device(where_ref, own_ref, other_ref, start, reverse):
    core, mine = where_ref[1], where_ref[2]
    planes = own_ref.shape[0]
    row = lax.broadcasted_iota(jnp.int32, (H, LANES), 0)
    lane = lax.broadcasted_iota(jnp.int32, (H, LANES), 1)
    eye = jnp.where(row == lane, 1.0, 0.0)
    eyes = jnp.where(row == lane % H, 1.0, 0.0)
    state = start[0:1]
    order = list(range(2 * planes))
    for n in reversed(order) if reverse else order:
        z, kappa = n // 2, n % 2
        reached = (mine < n) if reverse else (mine > n)
        at = (z + planes // 2) % planes
        packed = jnp.where(core == kappa, own_ref[at], other_ref[at])
        to_column = kappa == (1 if reverse else 0)
        matrix, vector = unpack_map(packed, not to_column)
        vector = jnp.where(reached, vector, 0.0)
        if to_column:
            matrix = jnp.where(reached, matrix, eye)
            summed = jnp.sum(matrix * state + eye * vector, axis=1, keepdims=True)
            state = jnp.broadcast_to(summed, (H, LANES))
        else:
            matrix = jnp.where(reached, matrix, eyes)
            state = jnp.sum(matrix * state, axis=0, keepdims=True) + vector
    return jnp.broadcast_to(state, (CHUNKS, LANES))


def spread(rows, count):
    k = lax.broadcasted_iota(jnp.int32, (count,) + rows.shape, 0)
    lane = lax.broadcasted_iota(jnp.int32, (count,) + rows.shape, 2) % H
    picked = jnp.where(k == lane, rows[None], 0.0).reshape(count * rows.shape[0], LANES)
    one = (
        lax.broadcasted_iota(jnp.int32, (LANES, LANES), 0) // H
        == lax.broadcasted_iota(jnp.int32, (LANES, LANES), 1) // H
    )
    one = jnp.where(one, 1.0, 0.0).astype(BF16)
    high, low = split(picked)
    rest = (picked - high.astype(F32) - low.astype(F32)).astype(BF16)
    return mm(jnp.concatenate([high, low, rest], axis=1), jnp.concatenate([one, one, one], axis=0))


def store_chunks(levels, chunk_ref, vector_ref):
    ones, twos, fours, _ = levels
    parts = (ones[0], twos[0], fours[0], ones[6], ones[2], ones[4], twos[2])
    for n, part in enumerate(parts):
        chunk_ref[n] = flip_halves(part[:H]) if n < 4 else part[:H]
        vector_ref[n : n + 1, :] = part[H : H + 1]


def enter_chunks(state, chunk_ref, vector_ref, ends_ref):
    low = lane_low((CHUNKS, LANES))
    first = doubled(ends_ref[...], 0)
    middle = apply_row(state, first[:H], first[H : H + 1])
    entering = jnp.where(low, state, middle)
    vectors = vector_ref[...]
    row = entering[0:1]
    one, two, four = (to_column(row, chunk_ref[n], vectors[n : n + 1]) for n in range(3))
    three = to_row(two, chunk_ref[4], vectors[4:5])
    five = to_row(four, chunk_ref[5], vectors[5:6])
    six = to_row(four, chunk_ref[6], vectors[6:7])
    seven = to_column(six, chunk_ref[3], vectors[3:4])
    rows = [row, as_row(one), as_row(two), three, as_row(four), five, six, as_row(seven)]
    return jnp.concatenate(rows, axis=0)


def trajectory(entering, maps_ref, spread_ref):
    spread_ref[...] = spread(entering, H)
    states = [maps_ref[j, H * CHUNKS :, :] for j in range(STEPS)]
    for b in range(0, H * CHUNKS, 64):
        factor = spread_ref[b : b + 64, :].reshape(8, CHUNKS, LANES)
        for j in range(STEPS):
            block = maps_ref[j, b : b + 64, :].reshape(8, CHUNKS, LANES)
            states[j] = states[j] + jnp.sum(block * factor, axis=0)
    return states


def phase(where_ref, prev, x3_ref, bias_ref, w3_ref, ws_ref, ud_ref, maps_ref, chunk_ref, vector_ref, ends_ref, out_ref):
    coef = coefficients(prev, x3_ref, bias_ref[...], w3_ref[...])
    scan_maps(coef, ws_ref, ud_ref, maps_ref)
    levels = chunk_levels(maps_ref)
    store_chunks(levels, chunk_ref, vector_ref)
    total = levels[-1][0]
    ends_ref[...] = total
    total = join_halves(total)
    send_map(total, flip(total[:H]), where_ref, out_ref)


def first_kernel(
    where_ref, a_ref, b_ref, w_ref, w3_ref, ws_ref, ud_ref, bias_ref,
    x3_ref, xin_ref, cot_ref, start_ref, maps_ref, chunk_ref, vector_ref, ends_ref, out_ref, natural_ref,
):
    odd, mine = where_ref[0], where_ref[2]
    pieces = []
    for v in range(2):
        for j in range(STEPS):
            rows = [
                jnp.where(odd == v, a_ref[pl.ds(o + j, 8, stride=8), :], b_ref[pl.ds(o + j, 8, stride=8), :])
                for o in (0, 64)
            ]
            pieces.append(jnp.concatenate(rows, axis=1))
    xin = jnp.concatenate(pieces, axis=0).astype(BF16)
    xin_ref[...] = xin
    cots = [jnp.where(odd == v, a_ref[128:160, :], b_ref[128:160, :]) for v in range(2)]
    low = lane_low((32, LANES))
    natural_ref[0:32, :] = jnp.where(low, cots[0], swap_halves(cots[1]))
    natural_ref[32:64, :] = jnp.where(low, swap_halves(cots[0]), cots[1])
    cot_ref[...] = jnp.concatenate([natural_ref[pl.ds(j, 8, stride=8), :] for j in range(STEPS)], axis=0)
    start = a_ref[160:168, :]
    start_ref[...] = start
    flat = mm_nt(xin, w_ref[...])
    bias = bias_ref[...]
    for g in range(3):
        cols = slice(g * H, (g + 1) * H)
        x3_ref[g] = jnp.concatenate([flat[:64, cols], flat[64:, cols]], axis=1) + bias[g : g + 1, :]
    row = lax.broadcasted_iota(jnp.int32, (64, LANES), 0)
    lane = lax.broadcasted_iota(jnp.int32, (64, LANES), 1)
    here = (row == 0) & (lane < H) & (mine == 0)
    prev = jnp.where(here, start[0:1, :], 0.0)
    phase(where_ref, prev, x3_ref, bias_ref, w3_ref, ws_ref, ud_ref, maps_ref, chunk_ref, vector_ref, ends_ref, out_ref)


def next_kernel(
    where_ref, own_ref, other_ref, start_ref, x3_ref, bias_ref, w3_ref, ws_ref, ud_ref, old_ref, pieces_ref, rows_ref, before_ref,
    maps_ref, chunk_ref, vector_ref, ends_ref, out_ref, spread_ref,
):
    state = enter_device(where_ref, own_ref, other_ref, start_ref[...], False)
    entering = enter_chunks(state, pieces_ref, rows_ref, before_ref)
    states = trajectory(entering, old_ref, spread_ref)
    prev = jnp.concatenate([entering] + states[:-1], axis=0)
    phase(where_ref, prev, x3_ref, bias_ref, w3_ref, ws_ref, ud_ref, maps_ref, chunk_ref, vector_ref, ends_ref, out_ref)


def half_sums(value):
    row = lax.broadcasted_iota(jnp.int32, (8, LANES), 0)
    low = lane_low((8, LANES))
    pick = jnp.where((row == 0) & low, 1.0, 0.0) + jnp.where((row == 1) & ~low, 1.0, 0.0)
    pick = pick.astype(BF16)
    return mm_nt(jnp.concatenate([pick, pick], axis=1), left_doubled(value))


def turn_kernel(
    where_ref, own_ref, other_ref, start_ref, x3_ref, bias_ref, w3_ref, ws_ref, ud_ref, old_ref, pieces_ref, rows_ref, before_ref, cot_ref,
    states_ref, coef_ref, chunk_ref, vector_ref, half_ref, out_ref,
    spread_ref, maps_ref, acc_ref,
):
    state = enter_device(where_ref, own_ref, other_ref, start_ref[...], False)
    entering = enter_chunks(state, pieces_ref, rows_ref, before_ref)
    states = trajectory(entering, old_ref, spread_ref)
    for j in range(STEPS):
        states_ref[pl.ds(j, CHUNKS, stride=STEPS), :] = states[j]
    prev = jnp.concatenate([entering] + states[:-1], axis=0)
    coef = coefficients(prev, x3_ref, bias_ref[...], w3_ref[...])
    coef_ref[0] = prev
    for n in range(5):
        coef_ref[n + 1] = coef[n]
    scan_maps(coef, ws_ref, ud_ref, maps_ref)
    levels = chunk_levels(maps_ref)
    total = levels[-1][0]
    for b in range(0, H * CHUNKS, 64):
        acc = jnp.zeros((8, CHUNKS, LANES), F32)
        for j in range(STEPS):
            block = maps_ref[j, b : b + 64, :].reshape(8, CHUNKS, LANES)
            acc = acc + block * cot_ref[j * CHUNKS : (j + 1) * CHUNKS, :][None]
        acc_ref[b : b + 64, :] = acc.reshape(64, LANES)
    vectors = []
    for c in range(CHUNKS):
        sums = half_sums(acc_ref[pl.ds(c, H, stride=CHUNKS), :])
        vectors.append(jnp.concatenate([sums[0:1], sums[1:2]], axis=1))
    ones, twos, fours, _ = [[part[:H] for part in level] for level in levels]
    flip_23 = flip_halves(twos[1])
    pairs = [to_column(vectors[2 * n + 1], ones[2 * n], vectors[2 * n]) for n in range(4)]
    pair_rows = [as_row(pair) for pair in pairs]
    quad_low = to_row(pairs[1], flip_halves(twos[0]), pair_rows[0])
    quad_high = to_row(pairs[3], flip_halves(twos[2]), pair_rows[2])
    ends = as_row(to_column(quad_high, fours[0], quad_low))
    matrices = (fours[1], twos[3], ones[7], flip_23, flip_halves(ones[5]), flip_halves(ones[3]), ones[1])
    rows = (quad_high, pair_rows[3], vectors[7], pair_rows[1], vectors[5], vectors[3], vectors[1])
    for n, (matrix, vector) in enumerate(zip(matrices, rows)):
        chunk_ref[n] = matrix
        vector_ref[n : n + 1, :] = vector
    tail = doubled(ends, 1)
    low = lane_low((H, LANES))
    sums = half_sums(jnp.where(low, total[:H], 0.0) * tail)
    left = ends[:, :H] + sums[0:1]
    both = join_halves(total)
    pad = jnp.zeros((7, LANES), F32)
    left = jnp.concatenate([left, left], axis=1)
    send_map(jnp.concatenate([both[:H], left, pad], axis=0), flip(both[:H]), where_ref, out_ref)
    half_ref[...] = jnp.concatenate([flip(doubled(total[:H], 1)), tail, pad], axis=0)


def gradient_kernel(
    where_ref, own_ref, other_ref, coef_ref, chunk_ref, vector_ref, half_ref, cot_ref, ut_ref,
    xin_ref, bias_ref, states_ref, across_ref, keep_ref, give_ref, home_ref, full_ref,
):
    low = lane_low((CHUNKS, LANES))
    right = enter_device(where_ref, own_ref, other_ref, jnp.zeros((CHUNKS, LANES), F32), True)
    half = half_ref[...]
    middle = apply_row(right, half[:H], half[H : H + 1])
    last = jnp.where(low, middle, right)[0:1]
    vectors = vector_ref[...]
    three, five, six = (to_column(last, chunk_ref[n], vectors[n : n + 1]) for n in range(3))
    one = to_row(three, chunk_ref[3], vectors[3:4])
    four = to_row(five, chunk_ref[4], vectors[4:5])
    two = to_row(three, chunk_ref[5], vectors[5:6])
    zero = to_column(one, chunk_ref[6], vectors[6:7])
    passed = jnp.concatenate(
        [as_row(zero), one, two, as_row(three), four, as_row(five), as_row(six), last], axis=0
    )
    dz, dr, dn, ds = [None] * STEPS, [None] * STEPS, [None] * STEPS, [None] * STEPS
    for j in reversed(range(STEPS)):
        at = slice(j * CHUNKS, (j + 1) * CHUNKS)
        lam = cot_ref[at, :] + passed
        dz[j], dr[j], dn[j] = coef_ref[2, at, :] * lam, coef_ref[3, at, :] * lam, coef_ref[4, at, :] * lam
        ds[j] = coef_ref[5, at, :] * lam
        if j > 0:
            pulled = times_wide(jnp.concatenate([dz[j], dr[j], dn[j]], axis=1), ut_ref[...])
            passed = coef_ref[1, at, :] * lam + pulled
    dz, dr, dn, ds = (jnp.concatenate(part, axis=0) for part in (dz, dr, dn, ds))

    def stacked(value):
        return jnp.concatenate([value[:, :H], value[:, H:]], axis=0)

    sz, sr, sn, ss = (stacked(part) for part in (dz, dr, dn, ds))
    zero = jnp.zeros((2 * 64, H), F32)
    high, low_part = split(jnp.concatenate([sz, sr, ss, zero], axis=1))
    xin = xin_ref[...]
    grad_in = mm_tn(jnp.concatenate([high, low_part], axis=0), jnp.concatenate([xin, xin], axis=0))
    high, low_part = split(jnp.concatenate([sz, sr, sn, zero], axis=1))
    prev_high, prev_low = split(stacked(coef_ref[0]))
    grad_rec = mm_tn(
        jnp.concatenate([prev_high, prev_low, prev_high], axis=0),
        jnp.concatenate([high, high, low_part], axis=0),
    )
    full_ref[0:192, :] = grad_in[:192, :LANES]
    full_ref[192:384, :] = grad_in[:192, LANES:]
    full_ref[384:448, :] = grad_rec[:, :LANES]
    rest = grad_rec[:, LANES:]
    full_ref[448:480, :] = jnp.concatenate([rest[:32, :H], rest[32:, :H]], axis=1)
    sums = [jnp.sum(part, axis=0, keepdims=True) for part in (sz, sr, ss, sn)]
    scale = sums[0] / bias_ref[4:5, :H]
    tail = jnp.concatenate(
        [jnp.concatenate([scale, sums[1]], axis=1), jnp.concatenate([sums[2], sums[3]], axis=1)], axis=0
    )
    full_ref[480:512, :] = jnp.concatenate([tail, jnp.zeros((30, LANES), F32)], axis=0)
    core, x = where_ref[1], where_ref[3]
    for d in range(4):
        part = lax.bitwise_xor(x, d)
        rows = slice(d * 64, (d + 1) * 64)
        keep_ref[rows, :] = full_ref[pl.ds(pl.multiple_of((core * 4 + part) * 64, 64), 64), :]
        give_ref[rows, :] = full_ref[pl.ds(pl.multiple_of(((1 - core) * 4 + part) * 64, 64), 64), :]
    for d in range(4):
        part = lax.bitwise_xor(x, d)
        whole = jnp.where(part // 2 == core, states_ref[...], across_ref[...])
        block = jnp.where(lax.rem(part, 2) == 0, whole, swap_halves(whole))
        home_ref[d] = jnp.where(lane_low((32, LANES)), block[:32], swap_halves(block[32:]))


def home_kernel(where_ref, home_ref, two_ref, three_ref, one_ref, traj_ref):
    core, x = where_ref[1], where_ref[3]
    blocks = [home_ref[0]] + [ref[64:96, :] for ref in (one_ref, two_ref, three_ref)]
    for e in range(2):
        where = lax.bitwise_xor(x, 2 * core + e)
        block = blocks[0]
        for d in range(1, 4):
            block = jnp.where(where == d, blocks[d], block)
        block = jnp.concatenate([block, swap_halves(block)], axis=0)
        traj_ref[:, e, :] = jnp.transpose(block)[:H]


def unpack_kernel(
    where_ref, one_ref, three_ref, two_ref, both_ref, in_ref, rec_ref, scale_ref, bias_ref, full_ref
):
    x = where_ref[3]
    pieces = (both_ref, one_ref, two_ref, three_ref)
    for d in range(4):
        part = lax.bitwise_xor(x, d)
        for core in range(2):
            full_ref[pl.ds(pl.multiple_of((core * 4 + part) * 64, 64), 64), :] = pieces[d][core]
    in_ref[:, :LANES] = full_ref[0:192, :]
    in_ref[:, LANES:] = full_ref[192:384, :]
    rec_ref[:, :LANES] = full_ref[384:448, :]
    rec_ref[0:32, LANES:] = full_ref[448:480, :H]
    rec_ref[32:, LANES:] = full_ref[448:480, H:]
    one, two = full_ref[480:481, :], full_ref[481:482, :]
    scale_ref[...] = one[:, :H]
    bias_ref[...] = jnp.concatenate([one[:, H:], two[:, :H], two[:, H:]], axis=0)


def call(kernel, outs, kinds, *operands, scratch=()):
    spaces = {"s": SMEM, "v": VMEM, "h": pltpu.HBM}
    specs = [pl.BlockSpec(memory_space=spaces[kind]) for kind in kinds]
    operands = [
        pltpu.with_memory_space_constraint(operand, pltpu.HBM) if kind == "h" else operand
        for kind, operand in zip(kinds, operands)
    ]
    return pl.pallas_call(
        kernel,
        out_shape=[jax.ShapeDtypeStruct(*out) for out in outs],
        in_specs=specs,
        out_specs=[pl.BlockSpec(memory_space=VMEM)] * len(outs),
        scratch_shapes=list(scratch),
        compiler_params=pltpu.CompilerParams(vmem_limit_bytes=16 * 1024 * 1024),
    )(*operands)


def local(planes, width, ys, inputs, w_in, u_rec, timescale, other_bias, h_init, cotangent):
    place, part = lax.axis_index("seq"), lax.axis_index("batch")
    z, x, core = place // width, place % width, part % 2
    where = jnp.stack([x % 2, core, z * 2 + core, x]).astype(jnp.int32)

    def at(z, x, y, core):
        return (z * width + x) * (2 * ys) + y * 2 + core

    there = []
    for m in range(2):
        pairs = [
            (at(z, x, y, c), at(z, 2 * c + ((x % 2) ^ m), y, x // 2))
            for z in range(planes) for x in range(width) for y in range(ys) for c in range(2)
        ]
        there.append(pairs)
    step_x = {
        d: [(z * width + x, z * width + (x ^ d)) for z in range(planes) for x in range(width)]
        for d in range(1, width)
    }
    along_z = [[(z + planes // 2) % planes * width + x for z in range(planes)] for x in range(width)]
    step_y = {d: [(b, b ^ (2 * d)) for b in range(2 * ys)] for d in range(1, ys)}
    cores = [(b, b ^ 1) for b in range(2 * ys)]
    axes = ("seq", "batch")

    def exchange(value):
        own = lax.all_to_all(value, "seq", 0, 0, axis_index_groups=along_z, tiled=True)
        return own, lax.ppermute(own, "batch", cores)

    sems = pltpu.SemaphoreType.DMA((4,))
    one, two = call(
        pack_kernel, [((PART, LANES), F32)] * 2, "shhh", where, inputs, cotangent, h_init.T,
        scratch=[
            pltpu.VMEM(inputs.shape, BF16), pltpu.VMEM(cotangent.shape, F32), pltpu.VMEM((2, H), F32), sems
        ],
    )
    one = lax.ppermute(one, axes, there[0])
    two = lax.ppermute(two, axes, there[1])
    w3, ws, ut, ud, bias, w = call(
        weights_kernel,
        [
            ((384, 384), BF16), ((384, 512), BF16), ((384, 2 * LANES), BF16),
            ((3, H, LANES), F32), ((8, LANES), F32), ((192, 256), BF16),
        ],
        "hhhh", u_rec, timescale[None, :], other_bias, w_in.T,
        scratch=[pltpu.VMEM((H, 192), F32), pltpu.VMEM((1, H), F32), pltpu.VMEM((3, H), F32), sems],
    )
    maps_t, chunk_t = ((STEPS, ROWS, LANES), F32), ((CHUNKS, H, LANES), F32)
    rows_t, ends_t, send_t = ((8, LANES), F32), ((72, LANES), F32), ((planes, MAP, LANES), F32)
    x3, xin, cot, start, maps, chunk, vector, ends, send = call(
        first_kernel,
        [((3, 64, LANES), F32), ((128, 256), BF16), ((64, LANES), F32), ((8, LANES), F32), maps_t, chunk_t, rows_t, ends_t, send_t],
        "svvvvvvv", where, one, two, w, w3, ws, ud, bias,
        scratch=[pltpu.VMEM((64, LANES), F32)],
    )
    spread_s = pltpu.VMEM((H * CHUNKS, LANES), F32)
    for _ in range(NEWTON - 1):
        own, other = exchange(send)
        maps, chunk, vector, ends, send = call(
            next_kernel, [maps_t, chunk_t, rows_t, ends_t, send_t], "svvvvvvvvvvvv",
            where, own, other, start, x3, bias, w3, ws, ud, maps, chunk, vector, ends, scratch=[spread_s],
        )
    own, other = exchange(send)
    states, coef, chunk, vector, half, send = call(
        turn_kernel,
        [
            ((64, LANES), F32), ((6, 64, LANES), F32), chunk_t,
            ((8, LANES), F32), ((72, LANES), F32), send_t,
        ],
        "svvvvvvvvvvvvv", where, own, other, start, x3, bias, w3, ws, ud, maps, chunk, vector, ends, cot,
        scratch=[
            spread_s, pltpu.VMEM(*maps_t),
            pltpu.VMEM((H * CHUNKS, LANES), F32),
        ],
    )
    across = lax.ppermute(states, "batch", cores)
    own, other = exchange(send)
    keep, give, home = call(
        gradient_kernel, [((256, LANES), F32), ((256, LANES), F32), ((4, 32, LANES), F32)], "svvvvvvvvvvvv",
        where, own, other, coef, chunk, vector, half, cot, ut, xin, bias, states, across,
        scratch=[pltpu.VMEM((512, LANES), F32)],
    )

    def around(value_of, axis, steps, order):
        got = {d: lax.ppermute(value_of(d), axis, steps[d]) for d in order}
        return [got[d] for d in order]

    parts = (keep + lax.ppermute(give, "batch", cores)).reshape(width, -1, LANES)
    early = around(lambda d: jnp.concatenate([parts[d], home[d]], axis=0), "seq", step_x, (2, 3, 1))
    part = parts[0] + sum(piece[:64] for piece in early)
    part = part + sum(around(lambda d: part, "batch", step_y, (1, 3, 2)))
    wide = jnp.broadcast_to(part[None], (planes,) + part.shape)
    part = lax.all_to_all(wide, "seq", 0, 0, axis_index_groups=along_z, tiled=True).sum(0)
    other = lax.ppermute(part, "batch", cores)
    first = core == 0
    both = jnp.stack([jnp.where(first, part, other), jnp.where(first, other, part)])
    rest = around(lambda d: both, "seq", step_x, (1, 3, 2))
    (traj,) = call(home_kernel, [((H, 2, 64), F32)], "svvvv", where, home, *early)
    grad_in, grad_rec, grad_scale, grad_other = call(
        unpack_kernel,
        [((192, 256), F32), ((H, 192), F32), ((1, H), F32), ((3, H), F32)], "svvvv",
        where, *rest, both, scratch=[pltpu.VMEM((512, LANES), F32)],
    )
    return traj, grad_in.T, grad_rec, grad_scale[0], grad_other


def solution(mesh):
    width = 4
    planes = mesh.shape["seq"] // width
    ys = mesh.shape["batch"] // 2
    return jax.shard_map(
        functools.partial(local, planes, width, ys),
        mesh=mesh,
        in_specs=(P("batch", "seq", None), P(), P(), P(), P(), P(None, "batch"), P(None, "batch", "seq")),
        out_specs=(P(None, "batch", "seq"), P(), P(), P(), P()),
        check_vma=False,
    )
```

```python
import functools

import jax
import jax.numpy as jnp
from jax import lax
from jax.experimental import pallas as pl
from jax.experimental.pallas import tpu as pltpu
from jax.sharding import PartitionSpec as P

NEWTON = 3
H = 64
LANES = 128
CHUNKS = 8
STEPS = 8
COLS = H + 1
ROWS = COLS * CHUNKS
BLOCKS = (0, 22, 44, 65)
MAP = 40
PART = 168
F32 = jnp.float32
BF16 = jnp.bfloat16
VMEM = pltpu.VMEM
SMEM = pltpu.SMEM


def split(value):
    high = value.astype(BF16)
    return high, (value - high.astype(F32)).astype(BF16)


def mm(left, right):
    return jnp.dot(left, right, preferred_element_type=F32)


def mm_nt(left, right):
    return lax.dot_general(left, right, (((1,), (1,)), ((), ())), preferred_element_type=F32)


def mm_tn(left, right):
    return lax.dot_general(left, right, (((0,), (0,)), ((), ())), preferred_element_type=F32)


def left3(value):
    high, low = split(value)
    return jnp.concatenate([high, low, high], axis=1)


def right3(value):
    high, low = split(value)
    return jnp.concatenate([high, high, low], axis=0)


def lane_low(shape):
    return lax.broadcasted_iota(jnp.int32, shape, 1) < H


def swap_halves(value):
    return pltpu.roll(value, H, axis=1)


def doubled(value, half):
    low = lane_low(value.shape)
    other = swap_halves(value)
    return jnp.where(low, value, other) if half == 0 else jnp.where(low, other, value)


def stacked_rows(value):
    high = value.astype(BF16).astype(F32)
    return jnp.concatenate([high, value - high], axis=0).astype(BF16)


def times_doubled(value, matrix):
    count = value.shape[0]
    both = mm(stacked_rows(value), jnp.concatenate(split(matrix), axis=0))
    return both[:count] + both[count:]


def times_wide(value, wide):
    count, width = value.shape[0], wide.shape[1] // 2
    both = mm(stacked_rows(value), wide)
    return both[:count, :width] + both[count:, :width] + both[:count, width:]


def left_doubled(value):
    high, low = split(value)
    return jnp.concatenate([high, low], axis=1)


def block_diagonal(matrix):
    low = lane_low(matrix.shape)
    return jnp.concatenate([jnp.where(low, matrix, 0.0), jnp.where(low, 0.0, matrix)], axis=0)


def fetch(sources, targets, sems):
    copies = [pltpu.make_async_copy(a, b, sems.at[n]) for n, (a, b) in enumerate(zip(sources, targets))]
    for copy in copies:
        copy.start()
    for copy in copies:
        copy.wait()


def weights_kernel(
    u_hbm, scale_hbm, other_hbm, w_hbm, w3_ref, ws_ref, ut_ref, ud_ref, bias_ref, w_ref,
    u_ref, scale_ref, other_ref, sems,
):
    fetch((u_hbm, scale_hbm, other_hbm, w_hbm), (u_ref, scale_ref, other_ref, w_ref), sems)
    zero = jnp.zeros((H, H), F32)
    for g in range(3):
        block = u_ref[:, g * H : (g + 1) * H]
        ud_ref[g] = jnp.concatenate([block, block], axis=1)
        diag = jnp.concatenate(
            [jnp.concatenate([block, zero], axis=1), jnp.concatenate([zero, block], axis=1)], axis=0
        )
        at = slice(g * LANES, (g + 1) * LANES)
        high, low = split(diag)
        w3_ref[0:LANES, at] = high
        w3_ref[LANES : 2 * LANES, at] = high
        w3_ref[2 * LANES : 3 * LANES, at] = low
        ws_ref[0:LANES, at] = high
        ws_ref[LANES : 2 * LANES, at] = high
        ws_ref[2 * LANES : 3 * LANES, at] = low
        if g == 2:
            ws_ref[0:LANES, 3 * LANES :] = low
            ws_ref[LANES : 2 * LANES, 3 * LANES :] = low
            ws_ref[2 * LANES : 3 * LANES, 3 * LANES :] = low
        high, low = split(diag.T)
        ut_ref[at, :] = jnp.concatenate([high, low], axis=1)
    scale = scale_ref[...]
    rows = [jnp.log(scale), other_ref[0:1, :], other_ref[1:2, :], other_ref[2:3, :], scale]
    rows = [jnp.concatenate([row, row], axis=1) for row in rows]
    bias_ref[...] = jnp.concatenate(rows + [jnp.zeros((3, LANES), F32)], axis=0)


def pack_kernel(where_ref, x_hbm, cot_hbm, h_hbm, one_ref, two_ref, x_ref, cot_ref, h_ref, sems):
    fetch((x_hbm, cot_hbm, h_hbm), (x_ref, cot_ref, h_ref), sems)
    odd = where_ref[0]
    zero = jnp.zeros((H, H), F32)
    cots = []
    for e in range(2):
        cots.append(jnp.transpose(jnp.concatenate([cot_ref[:, e, :], zero], axis=1))[:H])
    for m, out_ref in enumerate((one_ref, two_ref)):
        first = odd == m
        x = jnp.where(first, x_ref[0].astype(F32), x_ref[1].astype(F32))
        out_ref[0:64, :] = x[:, :LANES]
        out_ref[64:128, :] = x[:, LANES:]
        cot = jnp.where(first, cots[0], cots[1])
        out_ref[128:160, :] = jnp.concatenate([cot[:32], cot[32:]], axis=1)
        start = jnp.where(first, h_ref[0:1, :], h_ref[1:2, :])
        start = jnp.concatenate([start, start], axis=1)
        out_ref[160:168, :] = jnp.broadcast_to(start, (8, LANES))


def coefficients(prev, x3, bias, w3):
    mixed = mm(left3(prev), w3)
    mz, mr, mn = mixed[:, :LANES], mixed[:, LANES : 2 * LANES], mixed[:, 2 * LANES :]
    update = jax.nn.sigmoid(x3[0] + mz)
    reset = jax.nn.sigmoid(x3[1] + mr)
    recur = mn + bias[3:4, :]
    cand = jnp.tanh(x3[2] + reset * recur)
    fresh = (1.0 - update) * cand + update * prev
    slope = (1.0 - update) * (1.0 - cand * cand)
    cz = (prev - cand) * update * (1.0 - update)
    cr = slope * recur * reset * (1.0 - reset)
    cn = slope * reset
    offset = fresh - (update * prev + cz * mz + cr * mr + cn * mn)
    return update, cz, cr, cn, slope, offset


def gate_products(rows, ws_ref):
    high, low = split(rows)
    pair = jnp.concatenate([high, low], axis=1)
    both = mm(jnp.concatenate([pair, high], axis=1), ws_ref[:, : 2 * LANES])
    last = mm(pair, ws_ref[: 2 * LANES, 2 * LANES :])
    return both[:, :LANES], both[:, LANES:], last[:, :LANES] + last[:, LANES:]


def scan_maps(coef, ws_ref, ud_ref, maps_ref):
    update, cz, cr, cn, _, offset = coef
    for j in range(STEPS):
        at = slice(j * CHUNKS, (j + 1) * CHUNKS)
        up_j, cz_j, cr_j, cn_j = (a[at][None] for a in (update, cz, cr, cn))
        for begin, end in zip(BLOCKS, BLOCKS[1:]):
            rows = slice(begin * CHUNKS, end * CHUNKS)
            last = end == COLS
            shape = (end - begin, CHUNKS, LANES)
            if j == 0:
                real = end - begin - 1 if last else end - begin
                cols = slice(begin, begin + real)
                k = lax.broadcasted_iota(jnp.int32, (real, CHUNKS, LANES), 0) + begin
                lane = lax.broadcasted_iota(jnp.int32, (real, CHUNKS, LANES), 2) % H
                new = jnp.where(k == lane, up_j, 0.0)
                for c, g in ((cz_j, 0), (cr_j, 1), (cn_j, 2)):
                    new = new + c * ud_ref[g, cols, :][:, None, :]
                if last:
                    new = jnp.concatenate([new, offset[at][None]], axis=0)
            else:
                old = maps_ref[j - 1, rows, :]
                mz, mr, mn = (part.reshape(shape) for part in gate_products(old, ws_ref))
                new = up_j * old.reshape(shape) + cz_j * mz + cr_j * mr + cn_j * mn
                if last:
                    new = jnp.concatenate([new[:-1], new[-1:] + offset[at][None]], axis=0)
            maps_ref[j, rows, :] = new.reshape((end - begin) * CHUNKS, LANES)


def chunk_matrix(maps_ref, c):
    return maps_ref[STEPS - 1, pl.ds(c, H, stride=CHUNKS), :]


def chunk_vector(maps_ref, c):
    return maps_ref[STEPS - 1, H * CHUNKS + c : H * CHUNKS + c + 1, :]


def compose(earlier, later):
    row = lax.broadcasted_iota(jnp.int32, (72, LANES), 0)
    both = times_wide(earlier, jnp.concatenate(split(block_diagonal(later[:H])), axis=1))
    return both + jnp.where(row == H, later[H : H + 1], 0.0)


def chunk_levels(maps_ref):
    pad = jnp.zeros((7, LANES), F32)
    levels = [[
        jnp.concatenate([chunk_matrix(maps_ref, c), chunk_vector(maps_ref, c), pad], axis=0) for c in range(CHUNKS)
    ]]
    while len(levels[-1]) > 1:
        parts = levels[-1]
        levels.append([compose(a, b) for a, b in zip(parts[::2], parts[1::2])])
    return levels


def flip_halves(matrix):
    turned = jnp.transpose(matrix)
    return jnp.concatenate([turned[:H], turned[H:]], axis=1)


def diagonal(rows):
    row = lax.broadcasted_iota(jnp.int32, (H, LANES), 0)
    lane = lax.broadcasted_iota(jnp.int32, (H, LANES), 1) % H
    return jnp.where(row == lane, rows, 0.0)


def to_column(row, matrix, vector):
    low = lane_low(matrix.shape)
    prod = matrix * row + diagonal(vector)
    first = jnp.sum(jnp.where(low, prod, 0.0), axis=1, keepdims=True)
    second = jnp.sum(jnp.where(low, 0.0, prod), axis=1, keepdims=True)
    return jnp.where(low, first, second)


def to_row(column, matrix, vector):
    return jnp.sum(column * matrix, axis=0, keepdims=True) + vector


def as_row(column):
    return jnp.sum(diagonal(column), axis=0, keepdims=True)


def join_halves(total):
    row = lax.broadcasted_iota(jnp.int32, (72, LANES), 0)
    second = doubled(total, 1)
    both = times_doubled(doubled(total, 0), second[:H])
    return both + jnp.where(row == H, second, 0.0)


def send_map(total, flipped, where_ref, out_ref):
    low = lane_low((H // 2, LANES))
    matrix = jnp.where(where_ref[1] == 0, flipped, total[:H])
    packed = jnp.where(low, matrix[: H // 2], matrix[H // 2 :])
    for z in range(out_ref.shape[0]):
        out_ref[z, : H // 2, :] = packed
        out_ref[z, H // 2 :, :] = total[H:]


def flip(matrix):
    square = jnp.transpose(matrix)[:H]
    return jnp.concatenate([square, square], axis=1)


def unpack_map(packed, whole):
    body = packed[: H // 2]
    other = swap_halves(body)
    low = lane_low(body.shape)
    if whole:
        parts = [jnp.where(low, body, other), jnp.where(low, other, body)]
    else:
        parts = [jnp.where(low, body, 0.0), jnp.where(low, other, 0.0)]
    return jnp.concatenate(parts, axis=0), packed[H // 2 : H // 2 + 1]


def apply_row(state, matrix, vector):
    return times_doubled(state, matrix) + vector


def enter_device(where_ref, own_ref, other_ref, start, reverse):
    core, mine = where_ref[1], where_ref[2]
    planes = own_ref.shape[0]
    row = lax.broadcasted_iota(jnp.int32, (H, LANES), 0)
    lane = lax.broadcasted_iota(jnp.int32, (H, LANES), 1)
    eye = jnp.where(row == lane, 1.0, 0.0)
    eyes = jnp.where(row == lane % H, 1.0, 0.0)
    state = start[0:1]
    order = list(range(2 * planes))
    for n in reversed(order) if reverse else order:
        z, kappa = n // 2, n % 2
        reached = (mine < n) if reverse else (mine > n)
        at = (z + 3) % planes
        packed = jnp.where(core == kappa, own_ref[at], other_ref[at])
        to_column = kappa == (1 if reverse else 0)
        matrix, vector = unpack_map(packed, not to_column)
        vector = jnp.where(reached, vector, 0.0)
        if to_column:
            matrix = jnp.where(reached, matrix, eye)
            summed = jnp.sum(matrix * state + eye * vector, axis=1, keepdims=True)
            state = jnp.broadcast_to(summed, (H, LANES))
        else:
            matrix = jnp.where(reached, matrix, eyes)
            state = jnp.sum(matrix * state, axis=0, keepdims=True) + vector
    return jnp.broadcast_to(state, (CHUNKS, LANES))


def spread(rows, count):
    k = lax.broadcasted_iota(jnp.int32, (count,) + rows.shape, 0)
    lane = lax.broadcasted_iota(jnp.int32, (count,) + rows.shape, 2) % H
    picked = jnp.where(k == lane, rows[None], 0.0).reshape(count * rows.shape[0], LANES)
    one = (
        lax.broadcasted_iota(jnp.int32, (LANES, LANES), 0) // H
        == lax.broadcasted_iota(jnp.int32, (LANES, LANES), 1) // H
    )
    one = jnp.where(one, 1.0, 0.0).astype(BF16)
    high, low = split(picked)
    rest = (picked - high.astype(F32) - low.astype(F32)).astype(BF16)
    return mm(jnp.concatenate([high, low, rest], axis=1), jnp.concatenate([one, one, one], axis=0))


def store_chunks(levels, chunk_ref, vector_ref):
    ones, twos, fours, _ = levels
    parts = (ones[0], twos[0], fours[0], ones[6], ones[2], ones[4], twos[2])
    for n, part in enumerate(parts):
        chunk_ref[n] = flip_halves(part[:H]) if n < 4 else part[:H]
        vector_ref[n : n + 1, :] = part[H : H + 1]


def enter_chunks(state, chunk_ref, vector_ref, ends_ref):
    low = lane_low((CHUNKS, LANES))
    first = doubled(ends_ref[...], 0)
    middle = apply_row(state, first[:H], first[H : H + 1])
    entering = jnp.where(low, state, middle)
    vectors = vector_ref[...]
    row = entering[0:1]
    one, two, four = (to_column(row, chunk_ref[n], vectors[n : n + 1]) for n in range(3))
    three = to_row(two, chunk_ref[4], vectors[4:5])
    five = to_row(four, chunk_ref[5], vectors[5:6])
    six = to_row(four, chunk_ref[6], vectors[6:7])
    seven = to_column(six, chunk_ref[3], vectors[3:4])
    rows = [row, as_row(one), as_row(two), three, as_row(four), five, six, as_row(seven)]
    return jnp.concatenate(rows, axis=0)


def trajectory(entering, maps_ref, spread_ref):
    spread_ref[...] = spread(entering, H)
    states = [maps_ref[j, H * CHUNKS :, :] for j in range(STEPS)]
    for b in range(0, H * CHUNKS, 64):
        factor = spread_ref[b : b + 64, :].reshape(8, CHUNKS, LANES)
        for j in range(STEPS):
            block = maps_ref[j, b : b + 64, :].reshape(8, CHUNKS, LANES)
            states[j] = states[j] + jnp.sum(block * factor, axis=0)
    return states


def phase(where_ref, prev, x3_ref, bias_ref, w3_ref, ws_ref, ud_ref, maps_ref, chunk_ref, vector_ref, ends_ref, out_ref):
    coef = coefficients(prev, x3_ref, bias_ref[...], w3_ref[...])
    scan_maps(coef, ws_ref, ud_ref, maps_ref)
    levels = chunk_levels(maps_ref)
    store_chunks(levels, chunk_ref, vector_ref)
    total = levels[-1][0]
    ends_ref[...] = total
    total = join_halves(total)
    send_map(total, flip(total[:H]), where_ref, out_ref)


def first_kernel(
    where_ref, a_ref, b_ref, w_ref, w3_ref, ws_ref, ud_ref, bias_ref,
    x3_ref, xin_ref, cot_ref, start_ref, maps_ref, chunk_ref, vector_ref, ends_ref, out_ref, natural_ref,
):
    odd, mine = where_ref[0], where_ref[2]
    pieces = []
    for v in range(2):
        for j in range(STEPS):
            rows = [
                jnp.where(odd == v, a_ref[pl.ds(o + j, 8, stride=8), :], b_ref[pl.ds(o + j, 8, stride=8), :])
                for o in (0, 64)
            ]
            pieces.append(jnp.concatenate(rows, axis=1))
    xin = jnp.concatenate(pieces, axis=0).astype(BF16)
    xin_ref[...] = xin
    cots = [jnp.where(odd == v, a_ref[128:160, :], b_ref[128:160, :]) for v in range(2)]
    low = lane_low((32, LANES))
    natural_ref[0:32, :] = jnp.where(low, cots[0], swap_halves(cots[1]))
    natural_ref[32:64, :] = jnp.where(low, swap_halves(cots[0]), cots[1])
    cot_ref[...] = jnp.concatenate([natural_ref[pl.ds(j, 8, stride=8), :] for j in range(STEPS)], axis=0)
    start = a_ref[160:168, :]
    start_ref[...] = start
    flat = mm_nt(xin, w_ref[...])
    bias = bias_ref[...]
    for g in range(3):
        cols = slice(g * H, (g + 1) * H)
        x3_ref[g] = jnp.concatenate([flat[:64, cols], flat[64:, cols]], axis=1) + bias[g : g + 1, :]
    row = lax.broadcasted_iota(jnp.int32, (64, LANES), 0)
    lane = lax.broadcasted_iota(jnp.int32, (64, LANES), 1)
    here = (row == 0) & (lane < H) & (mine == 0)
    prev = jnp.where(here, start[0:1, :], 0.0)
    phase(where_ref, prev, x3_ref, bias_ref, w3_ref, ws_ref, ud_ref, maps_ref, chunk_ref, vector_ref, ends_ref, out_ref)


def next_kernel(
    where_ref, own_ref, other_ref, start_ref, x3_ref, bias_ref, w3_ref, ws_ref, ud_ref, old_ref, pieces_ref, rows_ref, before_ref,
    maps_ref, chunk_ref, vector_ref, ends_ref, out_ref, spread_ref,
):
    state = enter_device(where_ref, own_ref, other_ref, start_ref[...], False)
    entering = enter_chunks(state, pieces_ref, rows_ref, before_ref)
    states = trajectory(entering, old_ref, spread_ref)
    prev = jnp.concatenate([entering] + states[:-1], axis=0)
    phase(where_ref, prev, x3_ref, bias_ref, w3_ref, ws_ref, ud_ref, maps_ref, chunk_ref, vector_ref, ends_ref, out_ref)


def half_sums(value):
    row = lax.broadcasted_iota(jnp.int32, (8, LANES), 0)
    low = lane_low((8, LANES))
    pick = jnp.where((row == 0) & low, 1.0, 0.0) + jnp.where((row == 1) & ~low, 1.0, 0.0)
    pick = pick.astype(BF16)
    return mm_nt(jnp.concatenate([pick, pick], axis=1), left_doubled(value))


def turn_kernel(
    where_ref, own_ref, other_ref, start_ref, x3_ref, bias_ref, w3_ref, ws_ref, ud_ref, old_ref, pieces_ref, rows_ref, before_ref, cot_ref,
    states_ref, coef_ref, chunk_ref, vector_ref, half_ref, out_ref,
    spread_ref, maps_ref, acc_ref,
):
    state = enter_device(where_ref, own_ref, other_ref, start_ref[...], False)
    entering = enter_chunks(state, pieces_ref, rows_ref, before_ref)
    states = trajectory(entering, old_ref, spread_ref)
    for j in range(STEPS):
        states_ref[pl.ds(j, CHUNKS, stride=STEPS), :] = states[j]
    prev = jnp.concatenate([entering] + states[:-1], axis=0)
    coef = coefficients(prev, x3_ref, bias_ref[...], w3_ref[...])
    coef_ref[0] = prev
    for n in range(5):
        coef_ref[n + 1] = coef[n]
    scan_maps(coef, ws_ref, ud_ref, maps_ref)
    levels = chunk_levels(maps_ref)
    total = levels[-1][0]
    for b in range(0, H * CHUNKS, 64):
        acc = jnp.zeros((8, CHUNKS, LANES), F32)
        for j in range(STEPS):
            block = maps_ref[j, b : b + 64, :].reshape(8, CHUNKS, LANES)
            acc = acc + block * cot_ref[j * CHUNKS : (j + 1) * CHUNKS, :][None]
        acc_ref[b : b + 64, :] = acc.reshape(64, LANES)
    vectors = []
    for c in range(CHUNKS):
        sums = half_sums(acc_ref[pl.ds(c, H, stride=CHUNKS), :])
        vectors.append(jnp.concatenate([sums[0:1], sums[1:2]], axis=1))
    ones, twos, fours, _ = [[part[:H] for part in level] for level in levels]
    flip_23 = flip_halves(twos[1])
    pairs = [to_column(vectors[2 * n + 1], ones[2 * n], vectors[2 * n]) for n in range(4)]
    pair_rows = [as_row(pair) for pair in pairs]
    quad_low = to_row(pairs[1], flip_halves(twos[0]), pair_rows[0])
    quad_high = to_row(pairs[3], flip_halves(twos[2]), pair_rows[2])
    ends = as_row(to_column(quad_high, fours[0], quad_low))
    matrices = (fours[1], twos[3], ones[7], flip_23, flip_halves(ones[5]), flip_halves(ones[3]), ones[1])
    rows = (quad_high, pair_rows[3], vectors[7], pair_rows[1], vectors[5], vectors[3], vectors[1])
    for n, (matrix, vector) in enumerate(zip(matrices, rows)):
        chunk_ref[n] = matrix
        vector_ref[n : n + 1, :] = vector
    tail = doubled(ends, 1)
    low = lane_low((H, LANES))
    sums = half_sums(jnp.where(low, total[:H], 0.0) * tail)
    left = ends[:, :H] + sums[0:1]
    both = join_halves(total)
    pad = jnp.zeros((7, LANES), F32)
    left = jnp.concatenate([left, left], axis=1)
    send_map(jnp.concatenate([both[:H], left, pad], axis=0), flip(both[:H]), where_ref, out_ref)
    half_ref[...] = jnp.concatenate([flip(doubled(total[:H], 1)), tail, pad], axis=0)


def gradient_kernel(
    where_ref, own_ref, other_ref, coef_ref, chunk_ref, vector_ref, half_ref, cot_ref, ut_ref,
    xin_ref, bias_ref, states_ref, across_ref, keep_ref, give_ref, home_ref, full_ref,
):
    low = lane_low((CHUNKS, LANES))
    right = enter_device(where_ref, own_ref, other_ref, jnp.zeros((CHUNKS, LANES), F32), True)
    half = half_ref[...]
    middle = apply_row(right, half[:H], half[H : H + 1])
    last = jnp.where(low, middle, right)[0:1]
    vectors = vector_ref[...]
    three, five, six = (to_column(last, chunk_ref[n], vectors[n : n + 1]) for n in range(3))
    one = to_row(three, chunk_ref[3], vectors[3:4])
    four = to_row(five, chunk_ref[4], vectors[4:5])
    two = to_row(three, chunk_ref[5], vectors[5:6])
    zero = to_column(one, chunk_ref[6], vectors[6:7])
    passed = jnp.concatenate(
        [as_row(zero), one, two, as_row(three), four, as_row(five), as_row(six), last], axis=0
    )
    dz, dr, dn, ds = [None] * STEPS, [None] * STEPS, [None] * STEPS, [None] * STEPS
    for j in reversed(range(STEPS)):
        at = slice(j * CHUNKS, (j + 1) * CHUNKS)
        lam = cot_ref[at, :] + passed
        dz[j], dr[j], dn[j] = coef_ref[2, at, :] * lam, coef_ref[3, at, :] * lam, coef_ref[4, at, :] * lam
        ds[j] = coef_ref[5, at, :] * lam
        if j > 0:
            pulled = times_wide(jnp.concatenate([dz[j], dr[j], dn[j]], axis=1), ut_ref[...])
            passed = coef_ref[1, at, :] * lam + pulled
    dz, dr, dn, ds = (jnp.concatenate(part, axis=0) for part in (dz, dr, dn, ds))

    def stacked(value):
        return jnp.concatenate([value[:, :H], value[:, H:]], axis=0)

    sz, sr, sn, ss = (stacked(part) for part in (dz, dr, dn, ds))
    zero = jnp.zeros((2 * 64, H), F32)
    high, low_part = split(jnp.concatenate([sz, sr, ss, zero], axis=1))
    xin = xin_ref[...]
    grad_in = mm_tn(jnp.concatenate([high, low_part], axis=0), jnp.concatenate([xin, xin], axis=0))
    high, low_part = split(jnp.concatenate([sz, sr, sn, zero], axis=1))
    prev_high, prev_low = split(stacked(coef_ref[0]))
    grad_rec = mm_tn(
        jnp.concatenate([prev_high, prev_low, prev_high], axis=0),
        jnp.concatenate([high, high, low_part], axis=0),
    )
    full_ref[0:192, :] = grad_in[:192, :LANES]
    full_ref[192:384, :] = grad_in[:192, LANES:]
    full_ref[384:448, :] = grad_rec[:, :LANES]
    rest = grad_rec[:, LANES:]
    full_ref[448:480, :] = jnp.concatenate([rest[:32, :H], rest[32:, :H]], axis=1)
    sums = [jnp.sum(part, axis=0, keepdims=True) for part in (sz, sr, ss, sn)]
    scale = sums[0] / bias_ref[4:5, :H]
    tail = jnp.concatenate(
        [jnp.concatenate([scale, sums[1]], axis=1), jnp.concatenate([sums[2], sums[3]], axis=1)], axis=0
    )
    full_ref[480:512, :] = jnp.concatenate([tail, jnp.zeros((30, LANES), F32)], axis=0)
    core, x = where_ref[1], where_ref[3]
    for d in range(4):
        part = lax.bitwise_xor(x, d)
        rows = slice(d * 64, (d + 1) * 64)
        keep_ref[rows, :] = full_ref[pl.ds(pl.multiple_of((core * 4 + part) * 64, 64), 64), :]
        give_ref[rows, :] = full_ref[pl.ds(pl.multiple_of(((1 - core) * 4 + part) * 64, 64), 64), :]
    for d in range(4):
        part = lax.bitwise_xor(x, d)
        whole = jnp.where(part // 2 == core, states_ref[...], across_ref[...])
        block = jnp.where(lax.rem(part, 2) == 0, whole, swap_halves(whole))
        home_ref[d] = jnp.where(lane_low((32, LANES)), block[:32], swap_halves(block[32:]))


def home_kernel(where_ref, home_ref, two_ref, three_ref, one_ref, traj_ref):
    core, x = where_ref[1], where_ref[3]
    blocks = [home_ref[0]] + [ref[64:96, :] for ref in (one_ref, two_ref, three_ref)]
    for e in range(2):
        where = lax.bitwise_xor(x, 2 * core + e)
        block = blocks[0]
        for d in range(1, 4):
            block = jnp.where(where == d, blocks[d], block)
        block = jnp.concatenate([block, swap_halves(block)], axis=0)
        traj_ref[:, e, :] = jnp.transpose(block)[:H]


def unpack_kernel(
    where_ref, one_ref, three_ref, two_ref, both_ref, in_ref, rec_ref, scale_ref, bias_ref, full_ref
):
    x = where_ref[3]
    pieces = (both_ref, one_ref, two_ref, three_ref)
    for d in range(4):
        part = lax.bitwise_xor(x, d)
        for core in range(2):
            full_ref[pl.ds(pl.multiple_of((core * 4 + part) * 64, 64), 64), :] = pieces[d][core]
    in_ref[:, :LANES] = full_ref[0:192, :]
    in_ref[:, LANES:] = full_ref[192:384, :]
    rec_ref[:, :LANES] = full_ref[384:448, :]
    rec_ref[0:32, LANES:] = full_ref[448:480, :H]
    rec_ref[32:, LANES:] = full_ref[448:480, H:]
    one, two = full_ref[480:481, :], full_ref[481:482, :]
    scale_ref[...] = one[:, :H]
    bias_ref[...] = jnp.concatenate([one[:, H:], two[:, :H], two[:, H:]], axis=0)


def call(kernel, outs, kinds, *operands, scratch=()):
    spaces = {"s": SMEM, "v": VMEM, "h": pltpu.HBM}
    specs = [pl.BlockSpec(memory_space=spaces[kind]) for kind in kinds]
    operands = [
        pltpu.with_memory_space_constraint(operand, pltpu.HBM) if kind == "h" else operand
        for kind, operand in zip(kinds, operands)
    ]
    return pl.pallas_call(
        kernel,
        out_shape=[jax.ShapeDtypeStruct(*out) for out in outs],
        in_specs=specs,
        out_specs=[pl.BlockSpec(memory_space=VMEM)] * len(outs),
        scratch_shapes=list(scratch),
        compiler_params=pltpu.CompilerParams(vmem_limit_bytes=16 * 1024 * 1024),
    )(*operands)


def local(planes, width, ys, inputs, w_in, u_rec, timescale, other_bias, h_init, cotangent):
    place, part = lax.axis_index("seq"), lax.axis_index("batch")
    z, x, core = place // width, place % width, part % 2
    where = jnp.stack([x % 2, core, z * 2 + core, x]).astype(jnp.int32)

    def at(z, x, y, core):
        return (z * width + x) * (2 * ys) + y * 2 + core

    there = []
    for m in range(2):
        pairs = [
            (at(z, x, y, c), at(z, 2 * c + ((x % 2) ^ m), y, x // 2))
            for z in range(planes) for x in range(width) for y in range(ys) for c in range(2)
        ]
        there.append(pairs)
    step_x = {
        d: [(z * width + x, z * width + (x ^ d)) for z in range(planes) for x in range(width)]
        for d in range(1, width)
    }
    along_z = [[(z + 5) % planes * width + x for z in range(planes)] for x in range(width)]
    step_y = {d: [(b, b ^ (2 * d)) for b in range(2 * ys)] for d in range(1, ys)}
    cores = [(b, b ^ 1) for b in range(2 * ys)]
    axes = ("seq", "batch")

    def exchange(value):
        own = lax.all_to_all(value, "seq", 0, 0, axis_index_groups=along_z, tiled=True)
        return own, lax.ppermute(own, "batch", cores)

    sems = pltpu.SemaphoreType.DMA((4,))
    one, two = call(
        pack_kernel, [((PART, LANES), F32)] * 2, "shhh", where, inputs, cotangent, h_init.T,
        scratch=[
            pltpu.VMEM(inputs.shape, BF16), pltpu.VMEM(cotangent.shape, F32), pltpu.VMEM((2, H), F32), sems
        ],
    )
    one = lax.ppermute(one, axes, there[0])
    two = lax.ppermute(two, axes, there[1])
    w3, ws, ut, ud, bias, w = call(
        weights_kernel,
        [
            ((384, 384), BF16), ((384, 512), BF16), ((384, 2 * LANES), BF16),
            ((3, H, LANES), F32), ((8, LANES), F32), ((192, 256), BF16),
        ],
        "hhhh", u_rec, timescale[None, :], other_bias, w_in.T,
        scratch=[pltpu.VMEM((H, 192), F32), pltpu.VMEM((1, H), F32), pltpu.VMEM((3, H), F32), sems],
    )
    maps_t, chunk_t = ((STEPS, ROWS, LANES), F32), ((CHUNKS, H, LANES), F32)
    rows_t, ends_t, send_t = ((8, LANES), F32), ((72, LANES), F32), ((planes, MAP, LANES), F32)
    x3, xin, cot, start, maps, chunk, vector, ends, send = call(
        first_kernel,
        [((3, 64, LANES), F32), ((128, 256), BF16), ((64, LANES), F32), ((8, LANES), F32), maps_t, chunk_t, rows_t, ends_t, send_t],
        "svvvvvvv", where, one, two, w, w3, ws, ud, bias,
        scratch=[pltpu.VMEM((64, LANES), F32)],
    )
    spread_s = pltpu.VMEM((H * CHUNKS, LANES), F32)
    for _ in range(NEWTON - 1):
        own, other = exchange(send)
        maps, chunk, vector, ends, send = call(
            next_kernel, [maps_t, chunk_t, rows_t, ends_t, send_t], "svvvvvvvvvvvv",
            where, own, other, start, x3, bias, w3, ws, ud, maps, chunk, vector, ends, scratch=[spread_s],
        )
    own, other = exchange(send)
    states, coef, chunk, vector, half, send = call(
        turn_kernel,
        [
            ((64, LANES), F32), ((6, 64, LANES), F32), chunk_t,
            ((8, LANES), F32), ((72, LANES), F32), send_t,
        ],
        "svvvvvvvvvvvvv", where, own, other, start, x3, bias, w3, ws, ud, maps, chunk, vector, ends, cot,
        scratch=[
            spread_s, pltpu.VMEM(*maps_t),
            pltpu.VMEM((H * CHUNKS, LANES), F32),
        ],
    )
    across = lax.ppermute(states, "batch", cores)
    own, other = exchange(send)
    keep, give, home = call(
        gradient_kernel, [((256, LANES), F32), ((256, LANES), F32), ((4, 32, LANES), F32)], "svvvvvvvvvvvv",
        where, own, other, coef, chunk, vector, half, cot, ut, xin, bias, states, across,
        scratch=[pltpu.VMEM((512, LANES), F32)],
    )

    def around(value_of, axis, steps, order):
        got = {d: lax.ppermute(value_of(d), axis, steps[d]) for d in order}
        return [got[d] for d in order]

    parts = (keep + lax.ppermute(give, "batch", cores)).reshape(width, -1, LANES)
    early = around(lambda d: jnp.concatenate([parts[d], home[d]], axis=0), "seq", step_x, (2, 3, 1))
    part = parts[0] + sum(piece[:64] for piece in early)
    part = part + sum(around(lambda d: part, "batch", step_y, (1, 3, 2)))
    wide = jnp.broadcast_to(part[None], (planes,) + part.shape)
    part = lax.all_to_all(wide, "seq", 0, 0, axis_index_groups=along_z, tiled=True).sum(0)
    other = lax.ppermute(part, "batch", cores)
    first = core == 0
    both = jnp.stack([jnp.where(first, part, other), jnp.where(first, other, part)])
    rest = around(lambda d: both, "seq", step_x, (1, 3, 2))
    (traj,) = call(home_kernel, [((H, 2, 64), F32)], "svvvv", where, home, *early)
    grad_in, grad_rec, grad_scale, grad_other = call(
        unpack_kernel,
        [((192, 256), F32), ((H, 192), F32), ((1, H), F32), ((3, H), F32)], "svvvv",
        where, *rest, both, scratch=[pltpu.VMEM((512, LANES), F32)],
    )
    return traj, grad_in.T, grad_rec, grad_scale[0], grad_other


def solution(mesh):
    width = 4
    planes = mesh.shape["seq"] // width
    ys = mesh.shape["batch"] // 2
    return jax.shard_map(
        functools.partial(local, planes, width, ys),
        mesh=mesh,
        in_specs=(P("batch", "seq", None), P(), P(), P(), P(), P(None, "batch"), P(None, "batch", "seq")),
        out_specs=(P(None, "batch", "seq"), P(), P(), P(), P()),
        check_vma=False,
    )
```

```python
import functools

import jax
import jax.numpy as jnp
from jax import lax
from jax.experimental import pallas as pl
from jax.experimental.pallas import tpu as pltpu
from jax.sharding import PartitionSpec as P

NEWTON = 3
H = 64
LANES = 128
CHUNKS = 8
STEPS = 8
COLS = H + 1
ROWS = COLS * CHUNKS
BLOCKS = (0, 22, 44, 65)
MAP = 40
PART = 168
ORDER = (5, 4, 6, 7, 3, 2, 1, 0)
F32 = jnp.float32
BF16 = jnp.bfloat16
VMEM = pltpu.VMEM
SMEM = pltpu.SMEM


def split(value):
    high = value.astype(BF16)
    return high, (value - high.astype(F32)).astype(BF16)


def mm(left, right):
    return jnp.dot(left, right, preferred_element_type=F32)


def mm_nt(left, right):
    return lax.dot_general(left, right, (((1,), (1,)), ((), ())), preferred_element_type=F32)


def mm_tn(left, right):
    return lax.dot_general(left, right, (((0,), (0,)), ((), ())), preferred_element_type=F32)


def left3(value):
    high, low = split(value)
    return jnp.concatenate([high, low, high], axis=1)


def right3(value):
    high, low = split(value)
    return jnp.concatenate([high, high, low], axis=0)


def lane_low(shape):
    return lax.broadcasted_iota(jnp.int32, shape, 1) < H


def swap_halves(value):
    return pltpu.roll(value, H, axis=1)


def doubled(value, half):
    low = lane_low(value.shape)
    other = swap_halves(value)
    return jnp.where(low, value, other) if half == 0 else jnp.where(low, other, value)


def stacked_rows(value):
    high = value.astype(BF16).astype(F32)
    return jnp.concatenate([high, value - high], axis=0).astype(BF16)


def times_doubled(value, matrix):
    count = value.shape[0]
    both = mm(stacked_rows(value), jnp.concatenate(split(matrix), axis=0))
    return both[:count] + both[count:]


def times_wide(value, wide):
    count, width = value.shape[0], wide.shape[1] // 2
    both = mm(stacked_rows(value), wide)
    return both[:count, :width] + both[count:, :width] + both[:count, width:]


def left_doubled(value):
    high, low = split(value)
    return jnp.concatenate([high, low], axis=1)


def block_diagonal(matrix):
    low = lane_low(matrix.shape)
    return jnp.concatenate([jnp.where(low, matrix, 0.0), jnp.where(low, 0.0, matrix)], axis=0)


def fetch(sources, targets, sems):
    copies = [pltpu.make_async_copy(a, b, sems.at[n]) for n, (a, b) in enumerate(zip(sources, targets))]
    for copy in copies:
        copy.start()
    for copy in copies:
        copy.wait()


def weights_kernel(
    u_hbm, scale_hbm, other_hbm, w_hbm, w3_ref, ws_ref, ut_ref, ud_ref, bias_ref, w_ref,
    u_ref, scale_ref, other_ref, sems,
):
    fetch((u_hbm, scale_hbm, other_hbm, w_hbm), (u_ref, scale_ref, other_ref, w_ref), sems)
    zero = jnp.zeros((H, H), F32)
    for g in range(3):
        block = u_ref[:, g * H : (g + 1) * H]
        ud_ref[g] = jnp.concatenate([block, block], axis=1)
        diag = jnp.concatenate(
            [jnp.concatenate([block, zero], axis=1), jnp.concatenate([zero, block], axis=1)], axis=0
        )
        at = slice(g * LANES, (g + 1) * LANES)
        high, low = split(diag)
        w3_ref[0:LANES, at] = high
        w3_ref[LANES : 2 * LANES, at] = high
        w3_ref[2 * LANES : 3 * LANES, at] = low
        ws_ref[0:LANES, at] = high
        ws_ref[LANES : 2 * LANES, at] = high
        ws_ref[2 * LANES : 3 * LANES, at] = low
        if g == 2:
            ws_ref[0:LANES, 3 * LANES :] = low
            ws_ref[LANES : 2 * LANES, 3 * LANES :] = low
            ws_ref[2 * LANES : 3 * LANES, 3 * LANES :] = low
        high, low = split(diag.T)
        ut_ref[at, :] = jnp.concatenate([high, low], axis=1)
    scale = scale_ref[...]
    rows = [jnp.log(scale), other_ref[0:1, :], other_ref[1:2, :], other_ref[2:3, :], scale]
    rows = [jnp.concatenate([row, row], axis=1) for row in rows]
    bias_ref[...] = jnp.concatenate(rows + [jnp.zeros((3, LANES), F32)], axis=0)


def pack_kernel(where_ref, x_hbm, cot_hbm, h_hbm, one_ref, two_ref, x_ref, cot_ref, h_ref, sems):
    fetch((x_hbm, cot_hbm, h_hbm), (x_ref, cot_ref, h_ref), sems)
    odd = where_ref[0]
    zero = jnp.zeros((H, H), F32)
    cots = []
    for e in range(2):
        cots.append(jnp.transpose(jnp.concatenate([cot_ref[:, e, :], zero], axis=1))[:H])
    for m, out_ref in enumerate((one_ref, two_ref)):
        first = odd == m
        x = jnp.where(first, x_ref[0].astype(F32), x_ref[1].astype(F32))
        out_ref[0:64, :] = x[:, :LANES]
        out_ref[64:128, :] = x[:, LANES:]
        cot = jnp.where(first, cots[0], cots[1])
        out_ref[128:160, :] = jnp.concatenate([cot[:32], cot[32:]], axis=1)
        start = jnp.where(first, h_ref[0:1, :], h_ref[1:2, :])
        start = jnp.concatenate([start, start], axis=1)
        out_ref[160:168, :] = jnp.broadcast_to(start, (8, LANES))


def coefficients(prev, x3, bias, w3):
    mixed = mm(left3(prev), w3)
    mz, mr, mn = mixed[:, :LANES], mixed[:, LANES : 2 * LANES], mixed[:, 2 * LANES :]
    update = jax.nn.sigmoid(x3[0] + mz)
    reset = jax.nn.sigmoid(x3[1] + mr)
    recur = mn + bias[3:4, :]
    cand = jnp.tanh(x3[2] + reset * recur)
    fresh = (1.0 - update) * cand + update * prev
    slope = (1.0 - update) * (1.0 - cand * cand)
    cz = (prev - cand) * update * (1.0 - update)
    cr = slope * recur * reset * (1.0 - reset)
    cn = slope * reset
    offset = fresh - (update * prev + cz * mz + cr * mr + cn * mn)
    return update, cz, cr, cn, slope, offset


def gate_products(rows, ws_ref):
    high, low = split(rows)
    pair = jnp.concatenate([high, low], axis=1)
    both = mm(jnp.concatenate([pair, high], axis=1), ws_ref[:, : 2 * LANES])
    last = mm(pair, ws_ref[: 2 * LANES, 2 * LANES :])
    return both[:, :LANES], both[:, LANES:], last[:, :LANES] + last[:, LANES:]


def scan_maps(coef, ws_ref, ud_ref, maps_ref):
    update, cz, cr, cn, _, offset = coef
    for j in range(STEPS):
        at = slice(j * CHUNKS, (j + 1) * CHUNKS)
        up_j, cz_j, cr_j, cn_j = (a[at][None] for a in (update, cz, cr, cn))
        for begin, end in zip(BLOCKS, BLOCKS[1:]):
            rows = slice(begin * CHUNKS, end * CHUNKS)
            last = end == COLS
            shape = (end - begin, CHUNKS, LANES)
            if j == 0:
                real = end - begin - 1 if last else end - begin
                cols = slice(begin, begin + real)
                k = lax.broadcasted_iota(jnp.int32, (real, CHUNKS, LANES), 0) + begin
                lane = lax.broadcasted_iota(jnp.int32, (real, CHUNKS, LANES), 2) % H
                new = jnp.where(k == lane, up_j, 0.0)
                for c, g in ((cz_j, 0), (cr_j, 1), (cn_j, 2)):
                    new = new + c * ud_ref[g, cols, :][:, None, :]
                if last:
                    new = jnp.concatenate([new, offset[at][None]], axis=0)
            else:
                old = maps_ref[j - 1, rows, :]
                mz, mr, mn = (part.reshape(shape) for part in gate_products(old, ws_ref))
                new = up_j * old.reshape(shape) + cz_j * mz + cr_j * mr + cn_j * mn
                if last:
                    new = jnp.concatenate([new[:-1], new[-1:] + offset[at][None]], axis=0)
            maps_ref[j, rows, :] = new.reshape((end - begin) * CHUNKS, LANES)


def chunk_matrix(maps_ref, c):
    return maps_ref[STEPS - 1, pl.ds(c, H, stride=CHUNKS), :]


def chunk_vector(maps_ref, c):
    return maps_ref[STEPS - 1, H * CHUNKS + c : H * CHUNKS + c + 1, :]


def compose(earlier, later):
    row = lax.broadcasted_iota(jnp.int32, (72, LANES), 0)
    both = times_wide(earlier, jnp.concatenate(split(block_diagonal(later[:H])), axis=1))
    return both + jnp.where(row == H, later[H : H + 1], 0.0)


def chunk_levels(maps_ref):
    pad = jnp.zeros((7, LANES), F32)
    levels = [[
        jnp.concatenate([chunk_matrix(maps_ref, c), chunk_vector(maps_ref, c), pad], axis=0) for c in range(CHUNKS)
    ]]
    while len(levels[-1]) > 1:
        parts = levels[-1]
        levels.append([compose(a, b) for a, b in zip(parts[::2], parts[1::2])])
    return levels


def flip_halves(matrix):
    turned = jnp.transpose(matrix)
    return jnp.concatenate([turned[:H], turned[H:]], axis=1)


def diagonal(rows):
    row = lax.broadcasted_iota(jnp.int32, (H, LANES), 0)
    lane = lax.broadcasted_iota(jnp.int32, (H, LANES), 1) % H
    return jnp.where(row == lane, rows, 0.0)


def to_column(row, matrix, vector):
    low = lane_low(matrix.shape)
    prod = matrix * row + diagonal(vector)
    first = jnp.sum(jnp.where(low, prod, 0.0), axis=1, keepdims=True)
    second = jnp.sum(jnp.where(low, 0.0, prod), axis=1, keepdims=True)
    return jnp.where(low, first, second)


def to_row(column, matrix, vector):
    return jnp.sum(column * matrix, axis=0, keepdims=True) + vector


def as_row(column):
    return jnp.sum(diagonal(column), axis=0, keepdims=True)


def join_halves(total):
    row = lax.broadcasted_iota(jnp.int32, (72, LANES), 0)
    second = doubled(total, 1)
    both = times_doubled(doubled(total, 0), second[:H])
    return both + jnp.where(row == H, second, 0.0)


def send_map(total, flipped, where_ref, out_ref):
    low = lane_low((H // 2, LANES))
    matrix = jnp.where(where_ref[1] == 0, flipped, total[:H])
    packed = jnp.where(low, matrix[: H // 2], matrix[H // 2 :])
    for z in range(out_ref.shape[0]):
        out_ref[z, : H // 2, :] = packed
        out_ref[z, H // 2 :, :] = total[H:]


def flip(matrix):
    square = jnp.transpose(matrix)[:H]
    return jnp.concatenate([square, square], axis=1)


def unpack_map(packed, whole):
    body = packed[: H // 2]
    other = swap_halves(body)
    low = lane_low(body.shape)
    if whole:
        parts = [jnp.where(low, body, other), jnp.where(low, other, body)]
    else:
        parts = [jnp.where(low, body, 0.0), jnp.where(low, other, 0.0)]
    return jnp.concatenate(parts, axis=0), packed[H // 2 : H // 2 + 1]


def apply_row(state, matrix, vector):
    return times_doubled(state, matrix) + vector


def enter_device(where_ref, own_ref, other_ref, start, reverse):
    core, mine = where_ref[1], where_ref[2]
    planes = own_ref.shape[0]
    row = lax.broadcasted_iota(jnp.int32, (H, LANES), 0)
    lane = lax.broadcasted_iota(jnp.int32, (H, LANES), 1)
    eye = jnp.where(row == lane, 1.0, 0.0)
    eyes = jnp.where(row == lane % H, 1.0, 0.0)
    state = start[0:1]
    order = list(range(2 * planes))
    for n in reversed(order) if reverse else order:
        z, kappa = n // 2, n % 2
        reached = (mine < n) if reverse else (mine > n)
        at = ORDER.index(z)
        packed = jnp.where(core == kappa, own_ref[at], other_ref[at])
        to_column = kappa == (1 if reverse else 0)
        matrix, vector = unpack_map(packed, not to_column)
        vector = jnp.where(reached, vector, 0.0)
        if to_column:
            matrix = jnp.where(reached, matrix, eye)
            summed = jnp.sum(matrix * state + eye * vector, axis=1, keepdims=True)
            state = jnp.broadcast_to(summed, (H, LANES))
        else:
            matrix = jnp.where(reached, matrix, eyes)
            state = jnp.sum(matrix * state, axis=0, keepdims=True) + vector
    return jnp.broadcast_to(state, (CHUNKS, LANES))


def spread(rows, count):
    k = lax.broadcasted_iota(jnp.int32, (count,) + rows.shape, 0)
    lane = lax.broadcasted_iota(jnp.int32, (count,) + rows.shape, 2) % H
    picked = jnp.where(k == lane, rows[None], 0.0).reshape(count * rows.shape[0], LANES)
    one = (
        lax.broadcasted_iota(jnp.int32, (LANES, LANES), 0) // H
        == lax.broadcasted_iota(jnp.int32, (LANES, LANES), 1) // H
    )
    one = jnp.where(one, 1.0, 0.0).astype(BF16)
    high, low = split(picked)
    rest = (picked - high.astype(F32) - low.astype(F32)).astype(BF16)
    return mm(jnp.concatenate([high, low, rest], axis=1), jnp.concatenate([one, one, one], axis=0))


def store_chunks(levels, chunk_ref, vector_ref):
    ones, twos, fours, _ = levels
    parts = (ones[0], twos[0], fours[0], ones[6], ones[2], ones[4], twos[2])
    for n, part in enumerate(parts):
        chunk_ref[n] = flip_halves(part[:H]) if n < 4 else part[:H]
        vector_ref[n : n + 1, :] = part[H : H + 1]


def enter_chunks(state, chunk_ref, vector_ref, ends_ref):
    low = lane_low((CHUNKS, LANES))
    first = doubled(ends_ref[...], 0)
    middle = apply_row(state, first[:H], first[H : H + 1])
    entering = jnp.where(low, state, middle)
    vectors = vector_ref[...]
    row = entering[0:1]
    one, two, four = (to_column(row, chunk_ref[n], vectors[n : n + 1]) for n in range(3))
    three = to_row(two, chunk_ref[4], vectors[4:5])
    five = to_row(four, chunk_ref[5], vectors[5:6])
    six = to_row(four, chunk_ref[6], vectors[6:7])
    seven = to_column(six, chunk_ref[3], vectors[3:4])
    rows = [row, as_row(one), as_row(two), three, as_row(four), five, six, as_row(seven)]
    return jnp.concatenate(rows, axis=0)


def trajectory(entering, maps_ref, spread_ref):
    spread_ref[...] = spread(entering, H)
    states = [maps_ref[j, H * CHUNKS :, :] for j in range(STEPS)]
    for b in range(0, H * CHUNKS, 64):
        factor = spread_ref[b : b + 64, :].reshape(8, CHUNKS, LANES)
        for j in range(STEPS):
            block = maps_ref[j, b : b + 64, :].reshape(8, CHUNKS, LANES)
            states[j] = states[j] + jnp.sum(block * factor, axis=0)
    return states


def phase(where_ref, prev, x3_ref, bias_ref, w3_ref, ws_ref, ud_ref, maps_ref, chunk_ref, vector_ref, ends_ref, out_ref):
    coef = coefficients(prev, x3_ref, bias_ref[...], w3_ref[...])
    scan_maps(coef, ws_ref, ud_ref, maps_ref)
    levels = chunk_levels(maps_ref)
    store_chunks(levels, chunk_ref, vector_ref)
    total = levels[-1][0]
    ends_ref[...] = total
    total = join_halves(total)
    send_map(total, flip(total[:H]), where_ref, out_ref)


def first_kernel(
    where_ref, a_ref, b_ref, w_ref, w3_ref, ws_ref, ud_ref, bias_ref,
    x3_ref, xin_ref, cot_ref, start_ref, maps_ref, chunk_ref, vector_ref, ends_ref, out_ref, natural_ref,
):
    odd, mine = where_ref[0], where_ref[2]
    pieces = []
    for v in range(2):
        for j in range(STEPS):
            rows = [
                jnp.where(odd == v, a_ref[pl.ds(o + j, 8, stride=8), :], b_ref[pl.ds(o + j, 8, stride=8), :])
                for o in (0, 64)
            ]
            pieces.append(jnp.concatenate(rows, axis=1))
    xin = jnp.concatenate(pieces, axis=0).astype(BF16)
    xin_ref[...] = xin
    cots = [jnp.where(odd == v, a_ref[128:160, :], b_ref[128:160, :]) for v in range(2)]
    low = lane_low((32, LANES))
    natural_ref[0:32, :] = jnp.where(low, cots[0], swap_halves(cots[1]))
    natural_ref[32:64, :] = jnp.where(low, swap_halves(cots[0]), cots[1])
    cot_ref[...] = jnp.concatenate([natural_ref[pl.ds(j, 8, stride=8), :] for j in range(STEPS)], axis=0)
    start = a_ref[160:168, :]
    start_ref[...] = start
    flat = mm_nt(xin, w_ref[...])
    bias = bias_ref[...]
    for g in range(3):
        cols = slice(g * H, (g + 1) * H)
        x3_ref[g] = jnp.concatenate([flat[:64, cols], flat[64:, cols]], axis=1) + bias[g : g + 1, :]
    row = lax.broadcasted_iota(jnp.int32, (64, LANES), 0)
    lane = lax.broadcasted_iota(jnp.int32, (64, LANES), 1)
    here = (row == 0) & (lane < H) & (mine == 0)
    prev = jnp.where(here, start[0:1, :], 0.0)
    phase(where_ref, prev, x3_ref, bias_ref, w3_ref, ws_ref, ud_ref, maps_ref, chunk_ref, vector_ref, ends_ref, out_ref)


def next_kernel(
    where_ref, own_ref, other_ref, start_ref, x3_ref, bias_ref, w3_ref, ws_ref, ud_ref, old_ref, pieces_ref, rows_ref, before_ref,
    maps_ref, chunk_ref, vector_ref, ends_ref, out_ref, spread_ref,
):
    state = enter_device(where_ref, own_ref, other_ref, start_ref[...], False)
    entering = enter_chunks(state, pieces_ref, rows_ref, before_ref)
    states = trajectory(entering, old_ref, spread_ref)
    prev = jnp.concatenate([entering] + states[:-1], axis=0)
    phase(where_ref, prev, x3_ref, bias_ref, w3_ref, ws_ref, ud_ref, maps_ref, chunk_ref, vector_ref, ends_ref, out_ref)


def half_sums(value):
    row = lax.broadcasted_iota(jnp.int32, (8, LANES), 0)
    low = lane_low((8, LANES))
    pick = jnp.where((row == 0) & low, 1.0, 0.0) + jnp.where((row == 1) & ~low, 1.0, 0.0)
    pick = pick.astype(BF16)
    return mm_nt(jnp.concatenate([pick, pick], axis=1), left_doubled(value))


def turn_kernel(
    where_ref, own_ref, other_ref, start_ref, x3_ref, bias_ref, w3_ref, ws_ref, ud_ref, old_ref, pieces_ref, rows_ref, before_ref, cot_ref,
    states_ref, coef_ref, chunk_ref, vector_ref, half_ref, out_ref,
    spread_ref, maps_ref, acc_ref,
):
    state = enter_device(where_ref, own_ref, other_ref, start_ref[...], False)
    entering = enter_chunks(state, pieces_ref, rows_ref, before_ref)
    states = trajectory(entering, old_ref, spread_ref)
    for j in range(STEPS):
        states_ref[pl.ds(j, CHUNKS, stride=STEPS), :] = states[j]
    prev = jnp.concatenate([entering] + states[:-1], axis=0)
    coef = coefficients(prev, x3_ref, bias_ref[...], w3_ref[...])
    coef_ref[0] = prev
    for n in range(5):
        coef_ref[n + 1] = coef[n]
    scan_maps(coef, ws_ref, ud_ref, maps_ref)
    levels = chunk_levels(maps_ref)
    total = levels[-1][0]
    for b in range(0, H * CHUNKS, 64):
        acc = jnp.zeros((8, CHUNKS, LANES), F32)
        for j in range(STEPS):
            block = maps_ref[j, b : b + 64, :].reshape(8, CHUNKS, LANES)
            acc = acc + block * cot_ref[j * CHUNKS : (j + 1) * CHUNKS, :][None]
        acc_ref[b : b + 64, :] = acc.reshape(64, LANES)
    vectors = []
    for c in range(CHUNKS):
        sums = half_sums(acc_ref[pl.ds(c, H, stride=CHUNKS), :])
        vectors.append(jnp.concatenate([sums[0:1], sums[1:2]], axis=1))
    ones, twos, fours, _ = [[part[:H] for part in level] for level in levels]
    flip_23 = flip_halves(twos[1])
    pairs = [to_column(vectors[2 * n + 1], ones[2 * n], vectors[2 * n]) for n in range(4)]
    pair_rows = [as_row(pair) for pair in pairs]
    quad_low = to_row(pairs[1], flip_halves(twos[0]), pair_rows[0])
    quad_high = to_row(pairs[3], flip_halves(twos[2]), pair_rows[2])
    ends = as_row(to_column(quad_high, fours[0], quad_low))
    matrices = (fours[1], twos[3], ones[7], flip_23, flip_halves(ones[5]), flip_halves(ones[3]), ones[1])
    rows = (quad_high, pair_rows[3], vectors[7], pair_rows[1], vectors[5], vectors[3], vectors[1])
    for n, (matrix, vector) in enumerate(zip(matrices, rows)):
        chunk_ref[n] = matrix
        vector_ref[n : n + 1, :] = vector
    tail = doubled(ends, 1)
    low = lane_low((H, LANES))
    sums = half_sums(jnp.where(low, total[:H], 0.0) * tail)
    left = ends[:, :H] + sums[0:1]
    both = join_halves(total)
    pad = jnp.zeros((7, LANES), F32)
    left = jnp.concatenate([left, left], axis=1)
    send_map(jnp.concatenate([both[:H], left, pad], axis=0), flip(both[:H]), where_ref, out_ref)
    half_ref[...] = jnp.concatenate([flip(doubled(total[:H], 1)), tail, pad], axis=0)


def gradient_kernel(
    where_ref, own_ref, other_ref, coef_ref, chunk_ref, vector_ref, half_ref, cot_ref, ut_ref,
    xin_ref, bias_ref, states_ref, across_ref, keep_ref, give_ref, home_ref, full_ref,
):
    low = lane_low((CHUNKS, LANES))
    right = enter_device(where_ref, own_ref, other_ref, jnp.zeros((CHUNKS, LANES), F32), True)
    half = half_ref[...]
    middle = apply_row(right, half[:H], half[H : H + 1])
    last = jnp.where(low, middle, right)[0:1]
    vectors = vector_ref[...]
    three, five, six = (to_column(last, chunk_ref[n], vectors[n : n + 1]) for n in range(3))
    one = to_row(three, chunk_ref[3], vectors[3:4])
    four = to_row(five, chunk_ref[4], vectors[4:5])
    two = to_row(three, chunk_ref[5], vectors[5:6])
    zero = to_column(one, chunk_ref[6], vectors[6:7])
    passed = jnp.concatenate(
        [as_row(zero), one, two, as_row(three), four, as_row(five), as_row(six), last], axis=0
    )
    dz, dr, dn, ds = [None] * STEPS, [None] * STEPS, [None] * STEPS, [None] * STEPS
    for j in reversed(range(STEPS)):
        at = slice(j * CHUNKS, (j + 1) * CHUNKS)
        lam = cot_ref[at, :] + passed
        dz[j], dr[j], dn[j] = coef_ref[2, at, :] * lam, coef_ref[3, at, :] * lam, coef_ref[4, at, :] * lam
        ds[j] = coef_ref[5, at, :] * lam
        if j > 0:
            pulled = times_wide(jnp.concatenate([dz[j], dr[j], dn[j]], axis=1), ut_ref[...])
            passed = coef_ref[1, at, :] * lam + pulled
    dz, dr, dn, ds = (jnp.concatenate(part, axis=0) for part in (dz, dr, dn, ds))

    def stacked(value):
        return jnp.concatenate([value[:, :H], value[:, H:]], axis=0)

    sz, sr, sn, ss = (stacked(part) for part in (dz, dr, dn, ds))
    zero = jnp.zeros((2 * 64, H), F32)
    high, low_part = split(jnp.concatenate([sz, sr, ss, zero], axis=1))
    xin = xin_ref[...]
    grad_in = mm_tn(jnp.concatenate([high, low_part], axis=0), jnp.concatenate([xin, xin], axis=0))
    high, low_part = split(jnp.concatenate([sz, sr, sn, zero], axis=1))
    prev_high, prev_low = split(stacked(coef_ref[0]))
    grad_rec = mm_tn(
        jnp.concatenate([prev_high, prev_low, prev_high], axis=0),
        jnp.concatenate([high, high, low_part], axis=0),
    )
    full_ref[0:192, :] = grad_in[:192, :LANES]
    full_ref[192:384, :] = grad_in[:192, LANES:]
    full_ref[384:448, :] = grad_rec[:, :LANES]
    rest = grad_rec[:, LANES:]
    full_ref[448:480, :] = jnp.concatenate([rest[:32, :H], rest[32:, :H]], axis=1)
    sums = [jnp.sum(part, axis=0, keepdims=True) for part in (sz, sr, ss, sn)]
    scale = sums[0] / bias_ref[4:5, :H]
    tail = jnp.concatenate(
        [jnp.concatenate([scale, sums[1]], axis=1), jnp.concatenate([sums[2], sums[3]], axis=1)], axis=0
    )
    full_ref[480:512, :] = jnp.concatenate([tail, jnp.zeros((30, LANES), F32)], axis=0)
    core, x = where_ref[1], where_ref[3]
    for d in range(4):
        part = lax.bitwise_xor(x, d)
        rows = slice(d * 64, (d + 1) * 64)
        keep_ref[rows, :] = full_ref[pl.ds(pl.multiple_of((core * 4 + part) * 64, 64), 64), :]
        give_ref[rows, :] = full_ref[pl.ds(pl.multiple_of(((1 - core) * 4 + part) * 64, 64), 64), :]
    for d in range(4):
        part = lax.bitwise_xor(x, d)
        whole = jnp.where(part // 2 == core, states_ref[...], across_ref[...])
        block = jnp.where(lax.rem(part, 2) == 0, whole, swap_halves(whole))
        home_ref[d] = jnp.where(lane_low((32, LANES)), block[:32], swap_halves(block[32:]))


def home_kernel(where_ref, home_ref, two_ref, three_ref, one_ref, traj_ref):
    core, x = where_ref[1], where_ref[3]
    blocks = [home_ref[0]] + [ref[64:96, :] for ref in (one_ref, two_ref, three_ref)]
    for e in range(2):
        where = lax.bitwise_xor(x, 2 * core + e)
        block = blocks[0]
        for d in range(1, 4):
            block = jnp.where(where == d, blocks[d], block)
        block = jnp.concatenate([block, swap_halves(block)], axis=0)
        traj_ref[:, e, :] = jnp.transpose(block)[:H]


def unpack_kernel(
    where_ref, one_ref, three_ref, two_ref, both_ref, in_ref, rec_ref, scale_ref, bias_ref, full_ref
):
    x = where_ref[3]
    pieces = (both_ref, one_ref, two_ref, three_ref)
    for d in range(4):
        part = lax.bitwise_xor(x, d)
        for core in range(2):
            full_ref[pl.ds(pl.multiple_of((core * 4 + part) * 64, 64), 64), :] = pieces[d][core]
    in_ref[:, :LANES] = full_ref[0:192, :]
    in_ref[:, LANES:] = full_ref[192:384, :]
    rec_ref[:, :LANES] = full_ref[384:448, :]
    rec_ref[0:32, LANES:] = full_ref[448:480, :H]
    rec_ref[32:, LANES:] = full_ref[448:480, H:]
    one, two = full_ref[480:481, :], full_ref[481:482, :]
    scale_ref[...] = one[:, :H]
    bias_ref[...] = jnp.concatenate([one[:, H:], two[:, :H], two[:, H:]], axis=0)


def call(kernel, outs, kinds, *operands, scratch=()):
    spaces = {"s": SMEM, "v": VMEM, "h": pltpu.HBM}
    specs = [pl.BlockSpec(memory_space=spaces[kind]) for kind in kinds]
    operands = [
        pltpu.with_memory_space_constraint(operand, pltpu.HBM) if kind == "h" else operand
        for kind, operand in zip(kinds, operands)
    ]
    return pl.pallas_call(
        kernel,
        out_shape=[jax.ShapeDtypeStruct(*out) for out in outs],
        in_specs=specs,
        out_specs=[pl.BlockSpec(memory_space=VMEM)] * len(outs),
        scratch_shapes=list(scratch),
        compiler_params=pltpu.CompilerParams(vmem_limit_bytes=16 * 1024 * 1024),
    )(*operands)


def local(planes, width, ys, inputs, w_in, u_rec, timescale, other_bias, h_init, cotangent):
    place, part = lax.axis_index("seq"), lax.axis_index("batch")
    z, x, core = place // width, place % width, part % 2
    where = jnp.stack([x % 2, core, z * 2 + core, x]).astype(jnp.int32)

    def at(z, x, y, core):
        return (z * width + x) * (2 * ys) + y * 2 + core

    there = []
    for m in range(2):
        pairs = [
            (at(z, x, y, c), at(z, 2 * c + ((x % 2) ^ m), y, x // 2))
            for z in range(planes) for x in range(width) for y in range(ys) for c in range(2)
        ]
        there.append(pairs)
    step_x = {
        d: [(z * width + x, z * width + (x ^ d)) for z in range(planes) for x in range(width)]
        for d in range(1, width)
    }
    along_z = [[z * width + x for z in ORDER] for x in range(width)]
    step_y = {d: [(b, b ^ (2 * d)) for b in range(2 * ys)] for d in range(1, ys)}
    cores = [(b, b ^ 1) for b in range(2 * ys)]
    axes = ("seq", "batch")

    def exchange(value):
        own = lax.all_to_all(value, "seq", 0, 0, axis_index_groups=along_z, tiled=True)
        return own, lax.ppermute(own, "batch", cores)

    sems = pltpu.SemaphoreType.DMA((4,))
    one, two = call(
        pack_kernel, [((PART, LANES), F32)] * 2, "shhh", where, inputs, cotangent, h_init.T,
        scratch=[
            pltpu.VMEM(inputs.shape, BF16), pltpu.VMEM(cotangent.shape, F32), pltpu.VMEM((2, H), F32), sems
        ],
    )
    one = lax.ppermute(one, axes, there[0])
    two = lax.ppermute(two, axes, there[1])
    w3, ws, ut, ud, bias, w = call(
        weights_kernel,
        [
            ((384, 384), BF16), ((384, 512), BF16), ((384, 2 * LANES), BF16),
            ((3, H, LANES), F32), ((8, LANES), F32), ((192, 256), BF16),
        ],
        "hhhh", u_rec, timescale[None, :], other_bias, w_in.T,
        scratch=[pltpu.VMEM((H, 192), F32), pltpu.VMEM((1, H), F32), pltpu.VMEM((3, H), F32), sems],
    )
    maps_t, chunk_t = ((STEPS, ROWS, LANES), F32), ((CHUNKS, H, LANES), F32)
    rows_t, ends_t, send_t = ((8, LANES), F32), ((72, LANES), F32), ((planes, MAP, LANES), F32)
    x3, xin, cot, start, maps, chunk, vector, ends, send = call(
        first_kernel,
        [((3, 64, LANES), F32), ((128, 256), BF16), ((64, LANES), F32), ((8, LANES), F32), maps_t, chunk_t, rows_t, ends_t, send_t],
        "svvvvvvv", where, one, two, w, w3, ws, ud, bias,
        scratch=[pltpu.VMEM((64, LANES), F32)],
    )
    spread_s = pltpu.VMEM((H * CHUNKS, LANES), F32)
    for _ in range(NEWTON - 1):
        own, other = exchange(send)
        maps, chunk, vector, ends, send = call(
            next_kernel, [maps_t, chunk_t, rows_t, ends_t, send_t], "svvvvvvvvvvvv",
            where, own, other, start, x3, bias, w3, ws, ud, maps, chunk, vector, ends, scratch=[spread_s],
        )
    own, other = exchange(send)
    states, coef, chunk, vector, half, send = call(
        turn_kernel,
        [
            ((64, LANES), F32), ((6, 64, LANES), F32), chunk_t,
            ((8, LANES), F32), ((72, LANES), F32), send_t,
        ],
        "svvvvvvvvvvvvv", where, own, other, start, x3, bias, w3, ws, ud, maps, chunk, vector, ends, cot,
        scratch=[
            spread_s, pltpu.VMEM(*maps_t),
            pltpu.VMEM((H * CHUNKS, LANES), F32),
        ],
    )
    across = lax.ppermute(states, "batch", cores)
    own, other = exchange(send)
    keep, give, home = call(
        gradient_kernel, [((256, LANES), F32), ((256, LANES), F32), ((4, 32, LANES), F32)], "svvvvvvvvvvvv",
        where, own, other, coef, chunk, vector, half, cot, ut, xin, bias, states, across,
        scratch=[pltpu.VMEM((512, LANES), F32)],
    )

    def around(value_of, axis, steps, order):
        got = {d: lax.ppermute(value_of(d), axis, steps[d]) for d in order}
        return [got[d] for d in order]

    parts = (keep + lax.ppermute(give, "batch", cores)).reshape(width, -1, LANES)
    early = around(lambda d: jnp.concatenate([parts[d], home[d]], axis=0), "seq", step_x, (2, 3, 1))
    part = parts[0] + sum(piece[:64] for piece in early)
    part = part + sum(around(lambda d: part, "batch", step_y, (1, 3, 2)))
    wide = jnp.broadcast_to(part[None], (planes,) + part.shape)
    part = lax.all_to_all(wide, "seq", 0, 0, axis_index_groups=along_z, tiled=True).sum(0)
    other = lax.ppermute(part, "batch", cores)
    first = core == 0
    both = jnp.stack([jnp.where(first, part, other), jnp.where(first, other, part)])
    rest = around(lambda d: both, "seq", step_x, (1, 3, 2))
    (traj,) = call(home_kernel, [((H, 2, 64), F32)], "svvvv", where, home, *early)
    grad_in, grad_rec, grad_scale, grad_other = call(
        unpack_kernel,
        [((192, 256), F32), ((H, 192), F32), ((1, H), F32), ((3, H), F32)], "svvvv",
        where, *rest, both, scratch=[pltpu.VMEM((512, LANES), F32)],
    )
    return traj, grad_in.T, grad_rec, grad_scale[0], grad_other


def solution(mesh):
    width = 4
    planes = mesh.shape["seq"] // width
    ys = mesh.shape["batch"] // 2
    return jax.shard_map(
        functools.partial(local, planes, width, ys),
        mesh=mesh,
        in_specs=(P("batch", "seq", None), P(), P(), P(), P(), P(None, "batch"), P(None, "batch", "seq")),
        out_specs=(P(None, "batch", "seq"), P(), P(), P(), P()),
        check_vma=False,
    )
```
